32 devices in a mesh: groups: 2 (over y), lon: 4 (over z), lat: 2 (over x), rep: 2 (over core).
Axes of the slice: x: 2, y: 2, z: 4, core: 2. Of those that a mesh axis runs over, the one named last changes fastest.
Arguments:
- grid_state: bfloat16 [128, 256, 256], P(('groups', 'lat'), ('lon', 'rep')), parts along dimension 0, may hold values from -6 to 6
- mesh1_state: bfloat16 [64, 128, 256], P(('groups', 'lat'), ('lon', 'rep')), parts along dimension 0, may hold values from -6 to 6
- mesh2_state: bfloat16 [32, 64, 256], P(('groups', 'lat'), 'lon'), parts along dimension 0, may hold values from -6 to 6
- grid_edges: int32 [16, 32, 128], P(None, 'lat', ('lon', 'rep')), may hold values from 0 to 16383, as said below
- up_edges: int32 [8, 16, 64], P(None, 'lat', 'lon'), may hold values from 0 to 4095, as said below
- weights: bfloat16 [9, 256, 256], replicated, may hold values from -0.375 to 0.375
- cotangent: bfloat16 [64, 128, 256], P(('groups', 'lat'), ('lon', 'rep')), parts along dimension 0, may hold values from -6 to 6
Outputs:
- mesh_out: bfloat16 [64, 128, 256], P(('groups', 'lat'), ('lon', 'rep')), parts along dimension 0
- mesh1_grad: bfloat16 [64, 128, 256], P(('groups', 'lat'), ('lon', 'rep')), parts along dimension 0
- weight_grads: float32 [18, 256, 256], P('groups'), parts along dimension 0
The draws below stay inside these ranges and needn't reach their ends.
There are 2 independent parts, one for each index of `groups`. The reference program is written for one: setup_inputs(seed, part) draws one part's arguments, and reference() takes and returns one part's arrays. A program takes and returns all parts, laid end to end along the dimension named above; an argument that names none is the same for every part. Nothing has to cross between parts.
Inputs may be any that keep to these rules, and one draw needn't show every extreme that they name: `grid_edges`: Level-one node (i, j) draws its senders from grid rows 2i - 2 to 2i + 3 (clipped to the grid) and columns 2j - 2 to 2j + 3 (modulo 256); every node has one edge at a corner of that window. `up_edges`: Level-two node (a, b) draws its senders from level-one rows 2a - 1 to 2a + 2 (clipped) and columns 2b - 1 to 2b + 2 (modulo 128); every node has one edge at a corner of that window.
All inputs are finite; a program needn't handle non-finite values.
Results may differ from the reference program's by a relative error of at most 0.0061.
Values may be sent and summed in bfloat16 or wider, within the bound.
No kernel may reach another device: no remote copies, remote signals or barrier semaphores. Data moves between devices by JAX's collectives and lax.ppermute only.
A program may use at most 64 MiB of HBM per device.

```python
import jax
import jax.numpy as jnp
from jax import lax

D = 256
K_G = 16
K_U = 8
GLAT = 64
GLON = 256
M1LAT = 32
M1LON = 128
M2LAT = 16
M2LON = 64


def window_edges(key, edge_count, row_count, col_count, reach_cells, row_limit, col_limit):
    key_list = jax.random.split(key, 5)
    dims = (edge_count, row_count, col_count)
    off_row = jax.random.randint(key_list[0], dims, -reach_cells, 2 + reach_cells)
    off_col = jax.random.randint(key_list[1], dims, -reach_cells, 2 + reach_cells)
    corner_slot = jax.random.randint(key_list[2], (1, row_count, col_count), 0, edge_count)
    corner_slot = corner_slot.at[0, 0, 0].set(1).at[0, row_count - 1, col_count - 1].set(1)
    row_side = jax.random.randint(key_list[3], (1, row_count, col_count), 0, 2)
    col_side = jax.random.randint(key_list[4], (1, row_count, col_count), 0, 2)
    slots = jnp.arange(edge_count, dtype=jnp.int32).reshape(edge_count, 1, 1)
    is_corner = slots == corner_slot
    off_row = jnp.where(is_corner, -reach_cells + row_side * (1 + 2 * reach_cells), off_row)
    off_col = jnp.where(is_corner, -reach_cells + col_side * (1 + 2 * reach_cells), off_col)
    base_row = 2 * jnp.arange(row_count, dtype=jnp.int32).reshape(1, row_count, 1)
    base_col = 2 * jnp.arange(col_count, dtype=jnp.int32).reshape(1, 1, col_count)
    rows_out = jnp.clip(base_row + off_row, 0, row_limit - 1)
    cols_out = (base_col + off_col) % col_limit
    flat = (rows_out * col_limit + cols_out).astype(jnp.int32)
    flat = flat.at[0, 0, 0].set(0)
    flat = flat.at[0, row_count - 1, col_count - 1].set(row_limit * col_limit - 1)
    return flat


def draw_grid_edges(key, part):
    key = jax.random.fold_in(key, 11)
    return window_edges(key, K_G, M1LAT, M1LON, 2, GLAT, GLON)


def draw_up_edges(key, part):
    key = jax.random.fold_in(key, 12)
    return window_edges(key, K_U, M2LAT, M2LON, 1, M1LAT, M1LON)


def block_levels(own_key, extent, cuts, least, top_value):
    factor_of = 1.0
    for position, parts in cuts:
        draws = jax.random.uniform(jax.random.fold_in(jax.random.fold_in(own_key, 6), position), (parts,), jnp.float32, least / len(cuts), top_value / len(cuts))
        factor_of = factor_of * jnp.repeat(jnp.exp(draws), extent[position] // parts).reshape((-1,) + (1,) * (len(extent) - 1 - position))
    return factor_of


def scatter_about(own_key, extent, scale, limit, pieces=(), kind=jnp.bfloat16):
    gain = block_levels(own_key, extent, pieces, -0.22, 0.18) if pieces else 1.0
    array = jax.random.normal(own_key, extent, jnp.float32) * scale * gain
    return jnp.minimum(jnp.maximum(array, -limit), limit).astype(kind)


def setup_inputs(seed: int = 0, part: int = 0) -> dict:
    seeds = jax.random.split(jax.random.key(seed), 8)
    part_splits = jax.random.split(jax.random.fold_in(seeds[7], part), 8)
    return {
        "grid_state": scatter_about(part_splits[0], (GLAT, GLON, D), 1.0, 6.0, ((0, 2), (1, 8))),
        "mesh1_state": scatter_about(part_splits[1], (M1LAT, M1LON, D), 1.0, 6.0, ((0, 2), (1, 8))),
        "mesh2_state": scatter_about(part_splits[2], (M2LAT, M2LON, D), 1.0, 6.0, ((0, 2), (1, 4))),
        "grid_edges": draw_grid_edges(jax.random.fold_in(seeds[7], 71), part),
        "up_edges": draw_up_edges(jax.random.fold_in(seeds[7], 71), part),
        "weights": scatter_about(seeds[5], (9, D, D), D ** -0.5, 0.375),
        "cotangent": scatter_about(part_splits[6], (M1LAT, M1LON, D), 1.0, 6.0, ((0, 2), (1, 8))),
    }


def matmul(left, right):
    return jnp.dot(left, right, preferred_element_type=jnp.float32)


def matmul_high(left, right):
    return jnp.dot(left, right, precision=lax.Precision.HIGHEST, preferred_element_type=jnp.float32)


def silu_slope(value):
    sigmoid = jax.nn.sigmoid(value)
    return sigmoid * (1.0 + value * (1.0 - sigmoid))


def reference(grid_state, mesh1_state, mesh2_state, grid_edges, up_edges, weights, cotangent):
    fine_count = M1LAT * M1LON
    coarse_count = M2LAT * M2LON
    grid_table = grid_state.reshape(GLAT * GLON, D)
    fine_in = mesh1_state.reshape(fine_count, D)
    coarse_in = mesh2_state.reshape(coarse_count, D)
    cotan_rows = cotangent.reshape(fine_count, D)
    enc_sources = grid_edges.reshape(K_G, fine_count)
    up_sources = up_edges.reshape(K_U, coarse_count)
    weights_wide = weights.astype(jnp.float32)

    enc_recv = matmul(fine_in, weights[1])

    def enc_forward(running, sources):
        pre_act = matmul(jnp.take(grid_table, sources, axis=0), weights[0]) + enc_recv
        return running + jax.nn.silu(pre_act), None

    enc_total, _ = lax.scan(enc_forward, jnp.zeros((fine_count, D), jnp.float32), enc_sources)
    enc_pool = (enc_total / K_G).astype(jnp.bfloat16)
    fine = (fine_in.astype(jnp.float32) + matmul(enc_pool, weights[2])).astype(jnp.bfloat16)

    up_recv = matmul(coarse_in, weights[4])

    def up_forward(running, sources):
        pre_act = matmul(jnp.take(fine, sources, axis=0), weights[3]) + up_recv
        return running + jax.nn.silu(pre_act), None

    up_total, _ = lax.scan(up_forward, jnp.zeros((coarse_count, D), jnp.float32), up_sources)
    up_pool = (up_total / K_U).astype(jnp.bfloat16)
    coarse = (coarse_in.astype(jnp.float32) + matmul(up_pool, weights[5])).astype(jnp.bfloat16)
    coarse_proj = matmul(coarse, weights[6]).reshape(M2LAT, M2LON, D)
    parent_proj = jnp.repeat(jnp.repeat(coarse_proj, 2, axis=0), 2, axis=1).reshape(fine_count, D)
    down_pre = parent_proj + matmul(fine, weights[7])
    down_act = jax.nn.silu(down_pre).astype(jnp.bfloat16)
    mesh_out = (fine.astype(jnp.float32) + matmul(down_act, weights[8])).astype(jnp.bfloat16)

    grad8 = matmul(down_act.T, cotan_rows)
    down_delta = (matmul(cotan_rows, weights[8].T) * silu_slope(down_pre)).astype(jnp.bfloat16)
    child_sum = down_delta.astype(jnp.float32).reshape(M2LAT, 2, M2LON, 2, D).sum(axis=(1, 3)).reshape(coarse_count, D)
    grad6 = matmul_high(coarse.astype(jnp.float32).T, child_sum)
    grad7 = matmul(fine.T, down_delta)
    coarse_delta = matmul_high(child_sum, weights_wide[6].T).astype(jnp.bfloat16)
    grad5 = matmul(up_pool.T, coarse_delta)
    pool2_delta = matmul(coarse_delta, weights[5].T) / K_U

    def up_backward(carried, sources):
        grad_send, node_total, fine_back = carried
        senders = jnp.take(fine, sources, axis=0)
        pre_act = matmul(senders, weights[3]) + up_recv
        delta = (pool2_delta * silu_slope(pre_act)).astype(jnp.bfloat16)
        grad_send = grad_send + matmul(senders.T, delta)
        node_total = node_total + delta.astype(jnp.float32)
        fine_back = fine_back + jax.ops.segment_sum(matmul(delta, weights[3].T), sources, num_segments=fine_count)
        return (grad_send, node_total, fine_back), None

    start_up = (jnp.zeros((D, D), jnp.float32), jnp.zeros((coarse_count, D), jnp.float32), jnp.zeros((fine_count, D), jnp.float32))
    (grad3, up_nodes, fine_back), _ = lax.scan(up_backward, start_up, up_sources)
    grad4 = matmul_high(coarse_in.astype(jnp.float32).T, up_nodes)
    fine_delta = cotan_rows.astype(jnp.float32) + matmul(down_delta, weights[7].T) + fine_back
    fine_delta_b = fine_delta.astype(jnp.bfloat16)
    grad2 = matmul(enc_pool.T, fine_delta_b)
    pool_delta = matmul(fine_delta_b, weights[2].T) / K_G

    def enc_backward(carried, sources):
        grad_send, node_total = carried
        senders = jnp.take(grid_table, sources, axis=0)
        pre_act = matmul(senders, weights[0]) + enc_recv
        delta = (pool_delta * silu_slope(pre_act)).astype(jnp.bfloat16)
        return (grad_send + matmul(senders.T, delta), node_total + delta.astype(jnp.float32)), None

    start_enc = (jnp.zeros((D, D), jnp.float32), jnp.zeros((fine_count, D), jnp.float32))
    (grad0, node_delta), _ = lax.scan(enc_backward, start_enc, enc_sources)
    grad1 = matmul_high(fine_in.astype(jnp.float32).T, node_delta)
    mesh1_grad = (fine_delta + matmul_high(node_delta, weights_wide[1].T)).astype(jnp.bfloat16)
    scale_factor = float(fine_count) ** -0.5
    weight_grads = jnp.stack([grad0, grad1, grad2, grad3, grad4, grad5, grad6, grad7, grad8]) * scale_factor
    return (mesh_out.reshape(M1LAT, M1LON, D), mesh1_grad.reshape(M1LAT, M1LON, D), weight_grads)
```

```python
import functools

import jax
import jax.numpy as jnp
from jax import lax
from jax.sharding import PartitionSpec as P


def with_halo(cells, sides, width):
    for axis, dim in sides:
        count = lax.axis_size(axis)
        head = lax.slice_in_dim(cells, 0, width, axis=dim)
        tail = lax.slice_in_dim(cells, cells.shape[dim] - width, cells.shape[dim], axis=dim)
        cells = jnp.concatenate(
            [
                lax.ppermute(tail, axis, [(i, (i + 1) % count) for i in range(count)]),
                cells,
                lax.ppermute(head, axis, [((i + 1) % count, i) for i in range(count)]),
            ],
            axis=dim,
        )
    return cells


def matmul(left, right):
    return jnp.dot(left, right, preferred_element_type=jnp.float32)


def matmul_high(left, right):
    return jnp.dot(left, right, precision=lax.Precision.HIGHEST, preferred_element_type=jnp.float32)


def silu_slope(value):
    sigmoid = jax.nn.sigmoid(value)
    return sigmoid * (1.0 + value * (1.0 - sigmoid))


def local_index(edges, total_cols, row_start, col_start, reach_cells, ext_cols):
    global_row = edges // total_cols
    global_col = edges % total_cols
    local_row = global_row - row_start + reach_cells
    local_col = (global_col - col_start + reach_cells) % total_cols
    return (local_row * ext_cols + local_col).reshape(-1)


def fold_rims(ext_grad, widened, reach_cells):
    rows_in = ext_grad.shape[0] - 2 * reach_cells
    cols_in = ext_grad.shape[1] - 2 * reach_cells
    inner = ext_grad[reach_cells : reach_cells + rows_in, reach_cells : reach_cells + cols_in]
    inner = inner.at[:reach_cells, :].add(
        widened[:reach_cells, 2 * reach_cells : 2 * reach_cells + cols_in]
    )
    inner = inner.at[rows_in - reach_cells :, :].add(
        widened[rows_in + 3 * reach_cells :, 2 * reach_cells : 2 * reach_cells + cols_in]
    )
    inner = inner.at[:, :reach_cells].add(
        widened[2 * reach_cells : 2 * reach_cells + rows_in, :reach_cells]
    )
    inner = inner.at[:, cols_in - reach_cells :].add(
        widened[2 * reach_cells : 2 * reach_cells + rows_in, cols_in + 3 * reach_cells :]
    )
    inner = inner.at[:reach_cells, :reach_cells].add(widened[:reach_cells, :reach_cells])
    inner = inner.at[:reach_cells, cols_in - reach_cells :].add(
        widened[:reach_cells, cols_in + 3 * reach_cells :]
    )
    inner = inner.at[rows_in - reach_cells :, :reach_cells].add(
        widened[rows_in + 3 * reach_cells :, :reach_cells]
    )
    inner = inner.at[rows_in - reach_cells :, cols_in - reach_cells :].add(
        widened[rows_in + 3 * reach_cells :, cols_in + 3 * reach_cells :]
    )
    return inner


def coarse_pass(
    fine_band,
    cotan_band,
    mesh2_part,
    up_part,
    row_start,
    col_start,
    m1lon_total,
    weights,
    spread,
    fold_back,
):
    features = fine_band.shape[2]
    rows_in = fine_band.shape[0]
    cols_in = fine_band.shape[1]
    up_count = up_part.shape[0]
    fine_ext = spread(fine_band)
    up_index = local_index(up_part, m1lon_total, row_start, col_start, 1, cols_in + 2)
    senders = jnp.take(fine_ext.reshape(-1, features), up_index, axis=0)
    coarse_in = mesh2_part.reshape(-1, features)
    up_pre = (
        matmul(senders, weights[3]).reshape(up_count, -1, features)
        + matmul(coarse_in, weights[4])[None]
    )
    up_pool = (jnp.sum(jax.nn.silu(up_pre), axis=0) / up_count).astype(jnp.bfloat16)
    coarse = (coarse_in.astype(jnp.float32) + matmul(up_pool, weights[5])).astype(jnp.bfloat16)
    coarse_proj = matmul(coarse, weights[6]).reshape(rows_in // 2, cols_in // 2, features)
    parent_proj = jnp.repeat(jnp.repeat(coarse_proj, 2, axis=0), 2, axis=1).reshape(-1, features)
    fine_flat = fine_band.reshape(-1, features)
    cotan_flat = cotan_band.reshape(-1, features)
    down_pre = parent_proj + matmul(fine_flat, weights[7])
    down_act = jax.nn.silu(down_pre).astype(jnp.bfloat16)
    out_band = (fine_flat.astype(jnp.float32) + matmul(down_act, weights[8])).astype(jnp.bfloat16)
    grad8 = matmul(down_act.T, cotan_flat)
    down_delta = (matmul(cotan_flat, weights[8].T) * silu_slope(down_pre)).astype(jnp.bfloat16)
    child_sum = (
        down_delta.astype(jnp.float32)
        .reshape(rows_in // 2, 2, cols_in // 2, 2, features)
        .sum(axis=(1, 3))
        .reshape(-1, features)
    )
    grad6 = matmul_high(coarse.astype(jnp.float32).T, child_sum)
    grad7 = matmul(fine_flat.T, down_delta)
    coarse_delta = matmul_high(child_sum, weights[6].astype(jnp.float32).T).astype(jnp.bfloat16)
    grad5 = matmul(up_pool.T, coarse_delta)
    pool2_delta = matmul(coarse_delta, weights[5].T) / up_count
    up_delta = (pool2_delta[None] * silu_slope(up_pre)).astype(jnp.bfloat16)
    up_delta_flat = up_delta.reshape(-1, features)
    grad3 = matmul(senders.T, up_delta_flat)
    grad4 = matmul_high(
        coarse_in.astype(jnp.float32).T, jnp.sum(up_delta.astype(jnp.float32), axis=0)
    )
    edge_back = matmul(up_delta_flat, weights[3].T)
    ext_grad = (
        jnp.zeros(((rows_in + 2) * (cols_in + 2), features), jnp.float32)
        .at[up_index]
        .add(edge_back)
    )
    rim_total = fold_back(ext_grad.reshape(rows_in + 2, cols_in + 2, features))
    fine_delta = (
        cotan_flat.astype(jnp.float32)
        + matmul(down_delta, weights[7].T)
        + rim_total.reshape(-1, features)
    )
    return (out_band, fine_delta, (grad3, grad4, grad5, grad6, grad7, grad8))


def swap_over(values, axes, partner, sizes):
    total = 1
    for size in sizes:
        total *= size
    return lax.ppermute(values, axes, [(i, partner(i)) for i in range(total)])


def sum_over_slice(stacked, mesh):
    lat_size, lon_size = mesh.shape["lat"], mesh.shape["lon"]
    rep = lax.axis_index("rep")
    lat, lon = lax.axis_index("lat"), lax.axis_index("lon")
    place = (lat % 2) * 2 + lon % 2
    low = jnp.bfloat16

    def between(values, lon_bit, lat_bit):
        return swap_over(
            values, ("lon", "lat"),
            lambda i: ((i // lat_size) ^ lon_bit) * lat_size + ((i % lat_size) ^ lat_bit),
            (lon_size, lat_size),
        )

    def siblings(values):
        return swap_over(values, "rep", lambda i: i ^ 1, (2,))

    count, rows, cols = stacked.shape
    halves = stacked.reshape(count, 2, rows // 2, cols)
    sent = lax.dynamic_index_in_dim(halves, 1 - rep, 1, keepdims=False).astype(low)
    kept = lax.dynamic_index_in_dim(halves, rep, 1, keepdims=False)
    half = kept + siblings(sent).astype(jnp.float32)
    quarters = half.reshape(count, 4, rows // 8, cols)
    total = lax.dynamic_index_in_dim(quarters, place, 1, keepdims=False)
    for step in (1, 2, 3):
        piece = lax.dynamic_index_in_dim(quarters, place ^ step, 1, keepdims=False).astype(low)
        total = total + between(piece, step & 1, step >> 1).astype(jnp.float32)
    bit = 2
    while bit < lon_size:
        rounded = total.astype(low)
        total = rounded.astype(jnp.float32) + between(rounded, bit, 0).astype(jnp.float32)
        bit *= 2
    bit = 2
    while bit < lat_size:
        rounded = total.astype(low)
        total = rounded.astype(jnp.float32) + between(rounded, 0, bit).astype(jnp.float32)
        bit *= 2
    own = total.astype(low)
    pieces = [own] + [between(own, step & 1, step >> 1) for step in (1, 2, 3)]
    theirs = [siblings(piece) for piece in pieces]
    mine_all = jnp.stack(pieces, 0)
    theirs_all = jnp.stack(theirs, 0)
    order = jnp.arange(4) ^ place
    mine_half = jnp.take(mine_all, order, axis=0)
    their_half = jnp.take(theirs_all, order, axis=0)
    first = jnp.where(rep == 0, mine_half, their_half)
    second = jnp.where(rep == 0, their_half, mine_half)
    both = jnp.stack([first, second], 0)
    return jnp.moveaxis(both, 2, 0).reshape(count, rows, cols).astype(jnp.float32)


def body(mesh, grid_state, mesh1_state, mesh2_state, grid_edges, up_edges, weights, cotangent):
    features = weights.shape[1]
    lat_pos = lax.axis_index("lat")
    col_pos = lax.axis_index(("lon", "rep"))
    rep_pos = lax.axis_index("rep")
    grid_rows = grid_state.shape[0]
    grid_cols = grid_state.shape[1]
    fine_rows = mesh1_state.shape[0]
    fine_cols = mesh1_state.shape[1]
    glon_total = grid_cols * lax.axis_size(("lon", "rep"))
    m1lon_total = fine_cols * lax.axis_size(("lon", "rep"))
    node_total = fine_rows * lax.axis_size("lat") * m1lon_total
    edge_count = grid_edges.shape[0]
    grid_ext = with_halo(grid_state, (("lat", 0), (("lon", "rep"), 1)), 2)
    enc_index = local_index(
        grid_edges, glon_total, lat_pos * grid_rows, col_pos * grid_cols, 2, grid_cols + 4
    )
    enc_senders = jnp.take(grid_ext.reshape(-1, features), enc_index, axis=0)
    fine_in = mesh1_state.reshape(-1, features)
    enc_recv = matmul(fine_in, weights[1])
    enc_pre = matmul(enc_senders, weights[0]).reshape(edge_count, -1, features) + enc_recv[None]
    enc_pool = (jnp.sum(jax.nn.silu(enc_pre), axis=0) / edge_count).astype(jnp.bfloat16)
    fine = (fine_in.astype(jnp.float32) + matmul(enc_pool, weights[2])).astype(jnp.bfloat16)
    fine = fine.reshape(fine_rows, fine_cols, features)
    fine_band, cotan_band = (
        lax.all_gather(fine, "rep", axis=1, tiled=True),
        lax.all_gather(cotangent, "rep", axis=1, tiled=True),
    )
    band_cols = fine_band.shape[1]
    lon_pos = lax.axis_index("lon")

    def spread_band(values):
        return with_halo(values, (("lat", 0), ("lon", 1)), 1)

    def fold_band(ext_grad):
        return fold_rims(
            ext_grad,
            with_halo(ext_grad.astype(jnp.bfloat16), (("lat", 0), ("lon", 1)), 1).astype(
                ext_grad.dtype
            ),
            1,
        )

    out_band, delta_band, coarse_grads = coarse_pass(
        fine_band,
        cotan_band,
        mesh2_state,
        up_edges,
        lat_pos * fine_rows,
        lon_pos * band_cols,
        m1lon_total,
        weights,
        spread_band,
        fold_band,
    )
    keep_first = (rep_pos == 0).astype(jnp.float32)
    coarse_grads = tuple((grad_part * keep_first for grad_part in coarse_grads))
    col_start = rep_pos * fine_cols
    mesh_out = lax.dynamic_slice_in_dim(
        out_band.reshape(fine_rows, band_cols, features), col_start, fine_cols, 1
    )
    fine_delta = lax.dynamic_slice_in_dim(
        delta_band.reshape(fine_rows, band_cols, features), col_start, fine_cols, 1
    )
    fine_delta = fine_delta.reshape(-1, features)
    fine_delta_b = fine_delta.astype(jnp.bfloat16)
    grad2 = matmul(enc_pool.T, fine_delta_b)
    pool_delta = matmul(fine_delta_b, weights[2].T) / edge_count
    enc_delta = (pool_delta[None] * silu_slope(enc_pre)).astype(jnp.bfloat16)
    grad0 = matmul(enc_senders.T, enc_delta.reshape(-1, features))
    node_delta = jnp.sum(enc_delta.astype(jnp.float32), axis=0)
    grad1 = matmul_high(fine_in.astype(jnp.float32).T, node_delta)
    mesh1_grad = (fine_delta + matmul_high(node_delta, weights[1].astype(jnp.float32).T)).astype(
        jnp.bfloat16
    )
    stacked = jnp.stack([grad0, grad1, grad2] + list(coarse_grads))
    summed = sum_over_slice(stacked, mesh)
    weight_grads = summed * float(node_total) ** (-0.5)
    return (mesh_out, mesh1_grad.reshape(fine_rows, fine_cols, features), weight_grads)


def solution(mesh):
    in_specs = (
        P(("groups", "lat"), ("lon", "rep"), None),
        P(("groups", "lat"), ("lon", "rep"), None),
        P(("groups", "lat"), "lon", None),
        P(None, "lat", ("lon", "rep")),
        P(None, "lat", "lon"),
        P(),
        P(("groups", "lat"), ("lon", "rep"), None),
    )
    out_specs = (
        P(("groups", "lat"), ("lon", "rep"), None),
        P(("groups", "lat"), ("lon", "rep"), None),
        P("groups", None, None),
    )
    return jax.shard_map(functools.partial(body, mesh), mesh=mesh, in_specs=in_specs, out_specs=out_specs, check_vma=False)
```

```python
import functools

import jax
import jax.numpy as jnp
from jax import lax
from jax.experimental import pallas as pl
from jax.experimental.pallas import tpu as pltpu
from jax.sharding import PartitionSpec as P

LOW = jnp.bfloat16
WIDE = jnp.float32
VMEM_BYTES = 48 * 1024 * 1024

SIDE_ROWS = 496
BAND_ROWS = 416
CORNER_ROWS = 160


def permute(values, axes, partner, sizes):
    total = 1
    for size in sizes:
        total *= size
    pairs = [(i, partner(i)) for i in range(total)]
    return lax.ppermute(values, axes, [(i, j) for i, j in pairs if j is not None])


def mm(left, right):
    return jnp.dot(left, right, preferred_element_type=WIDE)


def mm_nt(left, right):
    return lax.dot_general(left, right, (((1,), (1,)), ((), ())), preferred_element_type=WIDE)


def mm_tn(left, right):
    return lax.dot_general(left, right, (((0,), (0,)), ((), ())), preferred_element_type=WIDE)


def two_parts(value):
    high = value.astype(LOW)
    return high, (value - high.astype(WIDE)).astype(LOW)


def sigmoid_of(value):
    return 0.5 * jnp.tanh(0.5 * value) + 0.5


def iota(shape, dim):
    return lax.broadcasted_iota(jnp.int32, shape, dim)


def edge_codes(grid_edges, up_half, glon, m1lon, lat, col):
    keep, rows, cols = grid_edges.shape
    row = lax.broadcasted_iota(jnp.int32, grid_edges.shape, 1)
    j = lax.broadcasted_iota(jnp.int32, grid_edges.shape, 2)
    down = grid_edges // glon - (2 * (lat * rows + row) - 2)
    across = jnp.mod(grid_edges % glon - (2 * (col * cols + j) - 2), glon)
    place = 2 * (j % 8) + 6 + across
    own = down * 16 + place + jnp.where(place >= 16, 112, 0)
    sent = down * 16 + across + 6 + jnp.where(j >= 8, 2 * (j - 16), 128 + 2 * j)
    both = jnp.stack([own, sent], 0).astype(WIDE)
    both = jnp.transpose(both, (0, 2, 1, 3)).reshape(2 * rows, keep * cols)
    up_rows, up_cols = up_half.shape[1:]
    a = lax.broadcasted_iota(jnp.int32, up_half.shape, 1)
    b = lax.broadcasted_iota(jnp.int32, up_half.shape, 2)
    down = up_half // m1lon - (2 * (lat * up_rows + a) - 1)
    across = jnp.mod(up_half % m1lon - (2 * (col * up_cols + b) - 1), m1lon)

    def code(base):
        at = 2 * base - 1 + across
        at = jnp.where(at < 0, at + 20, jnp.where(at >= 16, at + 4, at))
        return down * 32 + at

    up = jnp.concatenate([code(b), code(jnp.where(b >= 4, b - 8, b + 8))], 2).astype(WIDE)
    up = jnp.transpose(up, (1, 0, 2)).reshape(up_rows, -1)
    up = jnp.pad(up, ((0, 16 - up_rows), (0, both.shape[1] - up.shape[1])))
    return jnp.concatenate([both, up], 0).astype(LOW)


def pack_kernel(dirs, grid, m1, cot, m2, codes, *outs):
    rep = lax.axis_index("rep")
    lat = lax.axis_index("lat")
    sides = outs[:2]
    bands = outs[2:]
    half = pl.multiple_of(rep * 8, 8)

    def column(right):
        g = grid[:, 16:32, :] if right else grid[:, 0:16, :]
        g = g.astype(WIDE)[:, 8:16] if right else g.astype(WIDE)[:, 0:8]
        s = slice(8, 16) if right else slice(0, 8)
        mm1 = m1[...].astype(WIDE)[:, s]
        cc = cot[...].astype(WIDE)[:, s]
        if right:
            pair = jnp.concatenate([mm1[:, 4:8], cc[:, 4:8]], axis=1)
        else:
            pair = jnp.concatenate([mm1[:, 0:4], cc[:, 0:4]], axis=1)
        return g, pair

    m2w = m2[...].astype(WIDE)
    m2_half = jnp.where(rep == 0, m2w[:, 0:8], m2w[:, 8:16])

    def fill(targets, right):
        side, corners = targets
        g, pair = column(right)
        side[0:256, :] = g.reshape(256, 256).astype(LOW)
        side[256:384, :] = pair.reshape(128, 256).astype(LOW)
        side[384:448, :] = m2_half.reshape(64, 256).astype(LOW)
        side[448:496, :] = codes[...]
        for sends_bottom, corner in corners:
            if sends_bottom is None:
                low = lat == 0
                gg = jnp.where(low, g[24:32], g[0:8])
                pp = jnp.where(low, pair[12:16], pair[0:4])
                mt = jnp.where(low, m2_half[7], m2_half[0])
            elif sends_bottom:
                gg, pp, mt = g[24:32], pair[12:16], m2_half[7]
            else:
                gg, pp, mt = g[0:8], pair[0:4], m2_half[0]
            corner[0:64, :] = gg.reshape(64, 256).astype(LOW)
            corner[64:96, :] = pp.reshape(32, 256).astype(LOW)
            corner[96:112, :] = jnp.concatenate([mt, mt], 0).astype(LOW)
            corner[112:160, :] = codes[...]

    sib = (sides[0], [(d, bands[3 * i + 1]) for i, d in enumerate(dirs)])
    out = (sides[1], [(d, bands[3 * i + 2]) for i, d in enumerate(dirs)])

    @pl.when(rep == 0)
    def _():
        fill(sib, True)
        fill(out, False)

    @pl.when(rep == 1)
    def _():
        fill(sib, False)
        fill(out, True)

    for i, sends_bottom in enumerate(dirs):
        band = bands[3 * i]
        if sends_bottom is None:
            first = jnp.where(lat == 0, 1, 0)
        else:
            first = 1 if sends_bottom else 0
        band[0:256, :] = grid[pl.ds(first * 24, 8)].reshape(256, 256)
        band[256:320, :] = m1[pl.ds(first * 12, 4)].reshape(64, 256)
        band[320:352, :] = cot[pl.ds(first * 14, 2)].reshape(32, 256)
        mt = jnp.where(first == 1, m2_half[7], m2_half[0])
        band[352:368, :] = jnp.concatenate([mt, mt], 0).astype(LOW)
        band[368:416, :] = codes[...]


def main_kernel(
    dirs, n_lat, own, sides, bands, weights, outs, scratch
):
    grid, m1, cot, m2, codes = own
    mesh_out, mesh1_grad, keep, send = outs
    gx, m1x, recv, ko, k2, uv, sx, slope, ssum, pool, fx, cx, m2x, ohu, su, uslope, dd, acc_s, fd_s, m0s = scratch
    rep = lax.axis_index("rep")
    lat = lax.axis_index("lat")
    frame = m1x.shape[0]
    a_frame = m2x.shape[0]
    if n_lat == 2:
        g_own, f_own, c_own, a_own = 4 + 4 * lat, 1 + 2 * lat, 2 * lat, lat
        f_first = 1 - lat
        f_count = frame - 1
    else:
        g_own, f_own, c_own, a_own = 8, 3, 2, 1
        f_first = 0
        f_count = frame

    def left_right(sib, out):
        return jnp.where(rep == 1, sib, out), jnp.where(rep == 1, out, sib)

    zero_rows = jnp.zeros((4, 16, 256), LOW)
    for blk in range(3):
        gx[blk, 0:4] = zero_rows
        gx[blk, gx.shape[1] - 6 : gx.shape[1] - 2] = zero_rows
        gx[blk, gx.shape[1] - 4 :] = zero_rows

    def put_grid(at, mid, sib, out):
        n = mid.shape[0]
        left, right = left_right(sib.astype(WIDE), out.astype(WIDE))
        left = left.reshape(n, 8, 256)
        right = right.reshape(n, 8, 256)
        wide = mid.astype(WIDE)
        gx[0, pl.ds(at, n)] = jnp.concatenate([left, wide[:, 0:8]], 1).astype(LOW)
        gx[1, pl.ds(at, n)] = wide[:, 8:24].astype(LOW)
        gx[2, pl.ds(at, n)] = jnp.concatenate([wide[:, 24:32], right], 1).astype(LOW)

    def own_grid(step, carry):
        r = step * 8
        r8 = pl.multiple_of(step * 64, 64)
        put_grid(g_own + r, grid[pl.ds(r, 8)], sides[0][pl.ds(r8, 64), :], sides[1][pl.ds(r8, 64), :])
        return carry

    lax.fori_loop(0, 4, own_grid, 0)

    def put_fine(sib, out, n):
        left, right = left_right(sib.astype(WIDE), out.astype(WIDE))
        left = left.reshape(n, 8, 256)
        right = right.reshape(n, 8, 256)
        states = jnp.concatenate([left[:, 0:4], right[:, 0:4]], 1)
        cots = jnp.concatenate([left[:, 4:8], right[:, 4:8]], 1)
        return states, cots

    m1x[...] = jnp.zeros_like(m1x)
    cx[...] = jnp.zeros_like(cx)
    states, cots = put_fine(sides[0][256:384, :], sides[1][256:384, :], 16)
    m1x[pl.ds(f_own, 16), 0:16] = m1[...].astype(WIDE)
    m1x[pl.ds(f_own, 16), 16:24] = states
    cx[pl.ds(c_own, 16), 0:16] = cot[...]
    cx[pl.ds(c_own, 16), 16:32] = jnp.concatenate([cots, jnp.zeros_like(cots)], 1).astype(LOW)

    def put_m2(at, mid, sib, out, n):
        left, right = left_right(sib.astype(WIDE), out.astype(WIDE))
        slot = iota((n, 8, 256), 1)
        left = left.reshape(n, 8, 256)
        right = right.reshape(n, 8, 256)
        ghost = jnp.where(slot == 7, left, jnp.where(slot == 0, right, 0.0))
        m2x[pl.ds(at, n)] = jnp.concatenate([mid.reshape(n, 8, 256), ghost], 1)

    m2w = m2[...].astype(WIDE)
    m2_half = jnp.where(rep == 0, m2w[:, 0:8], m2w[:, 8:16])
    put_m2(a_own, m2_half, sides[0][384:448, :], sides[1][384:448, :], 8)

    lane = iota((16, 256), 1) % 16

    def codes_of(mid, sib, out):
        left, right = left_right(sib.astype(WIDE), out.astype(WIDE))
        mid = mid.astype(WIDE)
        halo = jnp.where(lane >= 8, left[16:32], right[16:32])
        up = jnp.where(lane < 8, mid[32:48], jnp.where(lane < 12, right[32:48], left[32:48]))
        return mid[0:16], halo, up[:, 0:128]

    def put_codes(f_at, a_at, own_rows, halo_rows, up_rows):
        for r in range(own_rows.shape[0]):
            ko[f_at + r] = jnp.broadcast_to(own_rows[r : r + 1], (8, 256))
            k2[f_at + r] = jnp.broadcast_to(halo_rows[r : r + 1], (8, 256))
        for r in range(up_rows.shape[0]):
            uv[a_at + r] = jnp.broadcast_to(up_rows[r : r + 1], (8, 128))

    own_k, halo_k, up_k = codes_of(codes[...], sides[0][448:496, :], sides[1][448:496, :])
    put_codes(f_own, a_own, own_k, halo_k, up_k[0:8])

    for i, sends_bottom in enumerate(dirs):
        band, corner_sib, corner_out = bands[3 * i : 3 * i + 3]
        if sends_bottom is None:
            top = lat
        else:
            top = 1 if sends_bottom else 0
        below = 1 - top
        put_grid(
            below * (g_own + 32), band[0:256, :].reshape(8, 32, 256), corner_sib[0:64, :], corner_out[0:64, :]
        )
        states, cots = put_fine(corner_sib[64:96, :], corner_out[64:96, :], 4)
        is_top = top == 1
        f_at = below * (f_own + 16)
        c_at = below * (c_own + 16)
        a_at = below * (a_own + 8)
        mids = band[256:320, :].astype(WIDE).reshape(4, 16, 256)
        m1x[pl.ds(f_at, 3), 0:16] = jnp.where(is_top, mids[1:4], mids[0:3])
        m1x[pl.ds(f_at, 3), 16:24] = jnp.where(is_top, states[1:4], states[0:3])
        cx[pl.ds(c_at, 2), 0:16] = band[320:352, :].reshape(2, 16, 256)
        cots = jnp.where(is_top, cots[2:4], cots[0:2])
        cx[pl.ds(c_at, 2), 16:32] = jnp.concatenate([cots, jnp.zeros_like(cots)], 1).astype(LOW)
        put_m2(
            a_at, band[352:368, :].astype(WIDE)[0:8], corner_sib[96:112, :].astype(WIDE)[0:8],
            corner_out[96:112, :].astype(WIDE)[0:8], 1,
        )
        own_k, halo_k, up_k = codes_of(band[368:416, :], corner_sib[112:160, :], corner_out[112:160, :])
        put_codes(
            f_at, a_at,
            jnp.where(is_top, own_k[13:16], own_k[0:3]),
            jnp.where(is_top, halo_k[13:16], halo_k[0:3]),
            jnp.where(is_top, up_k[7:8], up_k[0:1]),
        )

    edge = iota((128, 256), 0)
    lanes = iota((128, 256), 1)
    slot = edge % 8
    base = (edge // 8) * 16
    m0s[0] = jnp.where(lanes == base + slot, 1.0, 0.0)
    m0s[1] = jnp.where(lanes == base + 8 + slot, 1.0, 0.0)
    m0s[2] = jnp.where(lanes == base + jnp.where(slot < 4, 12 + slot, slot - 4), 1.0, 0.0)
    ones = jnp.ones((256, 256), LOW)
    places = lanes.astype(WIDE)
    recv[...] = mm(m1x[...].reshape(frame * 24, 256).astype(LOW), weights[1]).reshape(frame, 24, 256)
    pool[...] = jnp.zeros_like(pool)

    def encode(f, carry):
        for tile, (first, second) in enumerate(((0, 1), (1, 2), (0, 2))):
            vec = ko[f] if tile < 2 else k2[f]
            picked = (m0s[tile].reshape(16, 8, 256) * vec[None]).reshape(128, 256).astype(LOW)
            chosen = jnp.where(mm(picked, ones) == places, 1.0, 0.0).astype(LOW)
            window = jnp.concatenate(
                [gx[first, pl.ds(2 * f, 8)].reshape(128, 256), gx[second, pl.ds(2 * f, 8)].reshape(128, 256)], 0
            )
            senders = mm(chosen, window).astype(LOW)
            pre = mm(senders, weights[0]).reshape(16, 8, 256) + recv[f, tile * 8 : tile * 8 + 8][None]
            sig = sigmoid_of(pre)
            act = pre * sig
            pool[f, tile * 8 : tile * 8 + 8] = jnp.sum(act, axis=0) * (1.0 / 16)
            if tile < 2:
                rise = sig + act * (1.0 - sig)
                sx[f, tile] = senders
                slope[f, tile] = rise.reshape(128, 256).astype(LOW)
                ssum[f, tile * 8 : tile * 8 + 8] = jnp.sum(rise, axis=0)
        return carry

    lax.fori_loop(f_first, f_first + f_count, encode, 0)
    fine = m1x[...].reshape(frame * 24, 256) + mm(pool[...].reshape(frame * 24, 256).astype(LOW), weights[2])
    fine = fine.reshape(frame, 24, 256)
    fx[:, 0:16] = fine[:, 0:16].astype(LOW)
    fx[:, 16:32] = jnp.concatenate([fine[:, 16:24], jnp.zeros((frame, 8, 256), WIDE)], 1).astype(LOW)

    edge = iota((128, 128), 0)
    lanes = iota((128, 128), 1)
    up_mask = jnp.where(lanes == edge, 1.0, 0.0)
    up_places = lanes.astype(WIDE)
    up_ones = jnp.ones((128, 128), LOW)
    m2_flat = m2x[...].reshape(a_frame * 16, 256)
    m2_low = m2_flat.astype(LOW)
    up_recv = mm(m2_low, weights[4]).reshape(a_frame, 16, 256)
    pools = []
    for aa in range(a_frame):
        vec = uv[aa]
        picked = (up_mask.reshape(16, 8, 128) * vec[None]).reshape(128, 128).astype(LOW)
        chosen = jnp.where(mm(picked, up_ones) == up_places, 1.0, 0.0).astype(LOW)
        ohu[aa] = chosen
        senders = mm(chosen, fx[2 * aa : 2 * aa + 4].reshape(128, 256)).astype(LOW)
        su[aa] = senders
        pre = mm(senders, weights[3]).reshape(8, 16, 256) + up_recv[aa][None]
        sig = sigmoid_of(pre)
        act = pre * sig
        pools.append(jnp.sum(act, axis=0) * (1.0 / 8))
        uslope[aa] = (sig + act * (1.0 - sig)).reshape(128, 256)
    up_pool = jnp.concatenate(pools, 0).astype(LOW)
    coarse = (m2_flat + mm(up_pool, weights[5])).astype(LOW)

    c_frame = 2 * a_frame
    nodes = a_frame * 16

    def parent_slot(q):
        return jnp.where(q < 16, q // 2, jnp.where((q == 18) | (q == 19), 15, jnp.where((q == 20) | (q == 21), 8, -1)))

    r_i = iota((c_frame * 32, nodes), 0)
    r_j = iota((c_frame * 32, nodes), 1)
    spread = (r_i // 64 == r_j // 16) & (parent_slot(r_i % 32) == r_j % 16)
    spread = jnp.where(spread, 1.0, 0.0).astype(LOW)
    t_i = iota((nodes, c_frame * 32), 1)
    t_j = iota((nodes, c_frame * 32), 0)
    gather = (t_i // 64 == t_j // 16) & (parent_slot(t_i % 32) == t_j % 16)
    gather = jnp.where(gather, 1.0, 0.0).astype(LOW)
    parents = mm(spread, coarse).astype(LOW)
    fine_mid = fx[1 : 1 + c_frame].reshape(c_frame * 32, 256)
    down_pre = mm(parents, weights[6]) + mm(fine_mid, weights[7])
    sig = sigmoid_of(down_pre)
    act = down_pre * sig
    cot_w = mm_nt(cx[...].reshape(c_frame * 32, 256), weights[8])
    dd[0] = (cot_w * (sig + act * (1.0 - sig))).astype(LOW).reshape(c_frame, 32, 256)
    dd[1] = act.astype(LOW).reshape(c_frame, 32, 256)

    def put_grad(index, value):
        acc_s[...] = value
        keep[index] = acc_s[pl.ds(pl.multiple_of(rep * 128, 128), 128), :]
        send[index] = acc_s[pl.ds(pl.multiple_of((1 - rep) * 128, 128), 128), :].astype(LOW)

    act_own = dd[1, pl.ds(c_own, 16), 0:16].reshape(256, 256)
    delta_own = dd[0, pl.ds(c_own, 16), 0:16].reshape(256, 256)
    fine_own = fx[pl.ds(f_own, 16), 0:16].reshape(256, 256)
    cot_own = cot[...].reshape(256, 256)
    out = fine_own.astype(WIDE) + mm(act_own, weights[8])
    mesh_out[...] = out.astype(LOW).reshape(16, 16, 256)
    put_grad(8, mm_tn(act_own, cot_own))
    put_grad(7, mm_tn(fine_own, delta_own))

    child_sum = mm(gather, dd[0].reshape(c_frame * 32, 256))
    n_i = iota((nodes, 256), 0)
    aa_i, bb_i = n_i // 16, n_i % 16
    is_own = (aa_i >= a_own) & (aa_i < a_own + 8) & (bb_i < 8)
    is_real = (bb_i <= 8) | (bb_i == 15)
    if n_lat != 2:
        above = lat * 8 - 1 + aa_i
        is_real = is_real & (above >= 0) & (above < n_lat * 8)
    sum_high, sum_low = two_parts(child_sum)
    coarse_delta = (mm_nt(sum_high, weights[6]) + mm_nt(sum_low, weights[6])).astype(LOW)
    own_high, own_low = two_parts(jnp.where(is_own, child_sum, 0.0))
    put_grad(6, mm_tn(coarse, own_high) + mm_tn(coarse, own_low))
    own_delta = jnp.where(is_own, coarse_delta.astype(WIDE), 0.0).astype(LOW)
    put_grad(5, mm_tn(up_pool, own_delta))
    pool2 = jnp.where(is_real, mm_nt(coarse_delta, weights[5]) * (1.0 / 8), 0.0)
    own_f = jnp.where(is_own, 1.0, 0.0)
    recv[...] = jnp.zeros_like(recv)
    acc_s[...] = jnp.zeros_like(acc_s)
    node_sums = []
    for aa in range(a_frame):
        d = pool2[aa * 16 : aa * 16 + 16][None] * uslope[aa].reshape(8, 16, 256)
        mine = own_f[aa * 16 : aa * 16 + 16][None]
        up_delta = d.astype(LOW)
        wide = up_delta.astype(WIDE)
        owned = wide * mine
        node_sums.append(jnp.sum(owned, axis=0))
        back = mm_tn(ohu[aa], up_delta.reshape(128, 256)).reshape(4, 32, 256)
        recv[2 * aa : 2 * aa + 4] += back[:, 0:24]
        acc_s[...] += mm_tn(su[aa], owned.reshape(128, 256).astype(LOW))
    put_grad(3, acc_s[...])
    ns_high, ns_low = two_parts(jnp.concatenate(node_sums, 0))
    put_grad(4, mm_tn(m2_low, ns_high) + mm_tn(m2_low, ns_low))
    back_high, back_low = two_parts(recv[pl.ds(f_own, 16), 0:16].reshape(256, 256))
    fine_delta = (
        cot_own.astype(WIDE)
        + mm_nt(delta_own, weights[7])
        + mm_nt(back_high, weights[3])
        + mm_nt(back_low, weights[3])
    )
    fd_s[...] = fine_delta
    fine_delta_b = fine_delta.astype(LOW)

    pool_own = pool[pl.ds(f_own, 16), 0:16].reshape(256, 256).astype(LOW)
    put_grad(2, mm_tn(pool_own, fine_delta_b))
    pool_delta = mm_nt(fine_delta_b, weights[2]) * (1.0 / 16)
    node_delta = pool_delta * ssum[pl.ds(f_own, 16)].reshape(256, 256)
    nd_high, nd_low = two_parts(node_delta)
    m1_own = m1[...].reshape(256, 256)
    put_grad(1, mm_tn(m1_own, nd_high) + mm_tn(m1_own, nd_low))
    grad_in = fd_s[...] + (mm_nt(nd_high, weights[1]) + mm_nt(nd_low, weights[1]))
    mesh1_grad[...] = grad_in.astype(LOW).reshape(16, 16, 256)
    m1x[0:16, 0:16] = pool_delta.reshape(16, 16, 256)
    acc_s[...] = jnp.zeros_like(acc_s)

    def encode_back(r, carry):
        deltas = []
        for tile in range(2):
            d = m1x[r, tile * 8 : tile * 8 + 8][None] * slope[f_own + r, tile].astype(WIDE).reshape(16, 8, 256)
            deltas.append(d.reshape(128, 256).astype(LOW))
        acc_s[...] += mm_tn(sx[f_own + r].reshape(256, 256), jnp.concatenate(deltas, 0))
        return carry

    lax.fori_loop(0, 16, encode_back, 0)
    put_grad(0, acc_s[...])


def flat_main(dirs, n_lat, *refs):
    n_bands = 3 * len(dirs)
    own, refs = refs[:5], refs[5:]
    sides, refs = refs[:2], refs[2:]
    bands, refs = refs[:n_bands], refs[n_bands:]
    weights, refs = refs[0], refs[1:]
    outs, scratch = refs[:4], refs[4:]
    main_kernel(dirs, n_lat, own, sides, bands, weights, outs, scratch)


def sum_over_slice(kept, sent, mesh):
    lat_size, lon_size = mesh.shape["lat"], mesh.shape["lon"]
    rep = lax.axis_index("rep")
    lat, lon = lax.axis_index("lat"), lax.axis_index("lon")
    place = (lat % 2) * 2 + lon % 2

    def between(values, lon_bit, lat_bit):
        return permute(
            values,
            ("lon", "lat"),
            lambda i: ((i // lat_size) ^ lon_bit) * lat_size + ((i % lat_size) ^ lat_bit),
            (lon_size, lat_size),
        )

    def siblings(values):
        return permute(values, "rep", lambda i: i ^ 1, (2,))

    count, rows, cols = kept.shape
    half = kept + siblings(sent).astype(WIDE)
    quarters = half.reshape(count, 4, rows // 4, cols)
    total = lax.dynamic_index_in_dim(quarters, place, 1, keepdims=False)
    for step in (1, 2, 3):
        piece = lax.dynamic_index_in_dim(quarters, place ^ step, 1, keepdims=False).astype(LOW)
        total = total + between(piece, step & 1, step >> 1).astype(WIDE)
    bit = 2
    while bit < lon_size:
        rounded = total.astype(LOW)
        total = rounded.astype(WIDE) + between(rounded, bit, 0).astype(WIDE)
        bit *= 2
    bit = 2
    while bit < lat_size:
        rounded = total.astype(LOW)
        total = rounded.astype(WIDE) + between(rounded, 0, bit).astype(WIDE)
        bit *= 2
    own = total.astype(LOW)
    pieces = [own] + [between(own, step & 1, step >> 1) for step in (1, 2, 3)]
    theirs = [siblings(piece) for piece in pieces]
    mine_all = jnp.stack(pieces, 0)
    theirs_all = jnp.stack(theirs, 0)
    order = jnp.arange(4) ^ place
    mine_half = jnp.take(mine_all, order, axis=0)
    their_half = jnp.take(theirs_all, order, axis=0)
    first = jnp.where(rep == 0, mine_half, their_half)
    second = jnp.where(rep == 0, their_half, mine_half)
    both = jnp.stack([first, second], 0)
    return jnp.moveaxis(both, 2, 0).reshape(count, 2 * rows, cols).astype(WIDE)


def body(mesh, grid_state, mesh1_state, mesh2_state, grid_edges, up_edges, weights, cotangent):
    n_lat, n_lon = mesh.shape["lat"], mesh.shape["lon"]
    lat = lax.axis_index("lat")
    col = lax.axis_index(("lon", "rep"))
    rep = lax.axis_index("rep")
    glon = grid_state.shape[1] * 2 * n_lon
    m1lon = mesh1_state.shape[1] * 2 * n_lon
    half_cols = up_edges.shape[2] // 2
    up_half = lax.dynamic_slice_in_dim(up_edges, rep * half_cols, half_cols, 2)
    codes = edge_codes(grid_edges, up_half, glon, m1lon, lat, col)
    dirs = (None,) if n_lat == 2 else (True, False)
    vmem = pl.BlockSpec(memory_space=pltpu.VMEM)
    params = pltpu.CompilerParams(vmem_limit_bytes=VMEM_BYTES)
    own = (grid_state, mesh1_state, cotangent, mesh2_state, codes)
    shapes = [SIDE_ROWS] * 2 + [BAND_ROWS, CORNER_ROWS, CORNER_ROWS] * len(dirs)
    buffers = pl.pallas_call(
        functools.partial(pack_kernel, dirs),
        out_shape=[jax.ShapeDtypeStruct((n, 256), LOW) for n in shapes],
        in_specs=[vmem] * 5,
        out_specs=[vmem] * len(shapes),
        compiler_params=params,
        name="pack_halos",
    )(*own)

    def beyond(lon, core):
        return ((lon + (1 if core else -1)) % n_lon, 1 - core)

    def send_to(values, other_lat, column):
        def partner(i):
            lon, rest = divmod(i, n_lat * 2)
            row, core = divmod(rest, 2)
            row = other_lat(row)
            if row is None:
                return None
            if column == "sibling":
                core = 1 - core
            elif column == "beyond":
                lon, core = beyond(lon, core)
            return (lon * n_lat + row) * 2 + core

        return permute(values, ("lon", "lat", "rep"), partner, (n_lon, n_lat, 2))

    def shift(sends_bottom):
        if sends_bottom is None:
            return lambda row: row ^ 1
        if sends_bottom:
            return lambda row: row + 1 if row + 1 < n_lat else None
        return lambda row: row - 1 if row else None

    got_sides = [send_to(buffers[0], lambda row: row, "sibling"), send_to(buffers[1], lambda row: row, "beyond")]
    got_bands = []
    for i, sends_bottom in enumerate(dirs):
        for k, column in enumerate(("same", "sibling", "beyond")):
            got_bands.append(send_to(buffers[2 + 3 * i + k], shift(sends_bottom), column))

    frame = 20 if n_lat == 2 else 22
    a_frame = 9 if n_lat == 2 else 10
    c_frame = 2 * a_frame
    g_frame = 2 * frame + 6
    scratch = [
        pltpu.VMEM((3, g_frame, 16, 256), LOW),
        pltpu.VMEM((frame, 24, 256), WIDE),
        pltpu.VMEM((frame, 24, 256), WIDE),
        pltpu.VMEM((frame, 8, 256), WIDE),
        pltpu.VMEM((frame, 8, 256), WIDE),
        pltpu.VMEM((a_frame, 8, 128), WIDE),
        pltpu.VMEM((frame, 2, 128, 256), LOW),
        pltpu.VMEM((frame, 2, 128, 256), LOW),
        pltpu.VMEM((frame, 16, 256), WIDE),
        pltpu.VMEM((frame, 24, 256), WIDE),
        pltpu.VMEM((frame, 32, 256), LOW),
        pltpu.VMEM((c_frame, 32, 256), LOW),
        pltpu.VMEM((a_frame, 16, 256), WIDE),
        pltpu.VMEM((a_frame, 128, 128), LOW),
        pltpu.VMEM((a_frame, 128, 256), LOW),
        pltpu.VMEM((a_frame, 128, 256), WIDE),
        pltpu.VMEM((2, c_frame, 32, 256), LOW),
        pltpu.VMEM((256, 256), WIDE),
        pltpu.VMEM((256, 256), WIDE),
        pltpu.VMEM((3, 128, 256), WIDE),
    ]
    n_in = 5 + 2 + len(got_bands) + 1
    mesh_out, mesh1_grad, kept, sent = pl.pallas_call(
        functools.partial(flat_main, dirs, n_lat),
        out_shape=[
            jax.ShapeDtypeStruct(mesh1_state.shape, LOW),
            jax.ShapeDtypeStruct(mesh1_state.shape, LOW),
            jax.ShapeDtypeStruct((9, 128, 256), WIDE),
            jax.ShapeDtypeStruct((9, 128, 256), LOW),
        ],
        in_specs=[vmem] * n_in,
        out_specs=[vmem] * 4,
        scratch_shapes=scratch,
        compiler_params=params,
        name="sweep",
    )(*own, *got_sides, *got_bands, weights)
    node_total = mesh1_state.shape[0] * mesh1_state.shape[1] * n_lat * n_lon * 2
    weight_grads = sum_over_slice(kept, sent, mesh) * float(node_total) ** (-0.5)
    return (mesh_out, mesh1_grad, weight_grads)


def solution(mesh):
    in_specs = (
        P(("groups", "lat"), ("lon", "rep"), None),
        P(("groups", "lat"), ("lon", "rep"), None),
        P(("groups", "lat"), "lon", None),
        P(None, "lat", ("lon", "rep")),
        P(None, "lat", "lon"),
        P(),
        P(("groups", "lat"), ("lon", "rep"), None),
    )
    out_specs = (
        P(("groups", "lat"), ("lon", "rep"), None),
        P(("groups", "lat"), ("lon", "rep"), None),
        P("groups", None, None),
    )
    return jax.shard_map(
        functools.partial(body, mesh), mesh=mesh, in_specs=in_specs, out_specs=out_specs, check_vma=False
    )
```

```python
import functools

import jax
import jax.numpy as jnp
from jax import lax
from jax.experimental import pallas as pl
from jax.experimental.pallas import tpu as pltpu
from jax.sharding import PartitionSpec as P

LOW = jnp.bfloat16
WIDE = jnp.float32
VMEM_BYTES = 36 * 1024 * 1024
HALO_ROWS = 2

SIDE_ROWS = 416
BAND_ROWS = 352
CORNER_ROWS = 112


def permute(values, axes, partner, sizes):
    total = 1
    for size in sizes:
        total *= size
    pairs = [(i, partner(i)) for i in range(total)]
    return lax.ppermute(values, axes, [(i, j) for i, j in pairs if j is not None])


def mm(left, right):
    return jnp.dot(left, right, preferred_element_type=WIDE)


def mm_nt(left, right):
    return lax.dot_general(left, right, (((1,), (1,)), ((), ())), preferred_element_type=WIDE)


def mm_tn(left, right):
    return lax.dot_general(left, right, (((0,), (0,)), ((), ())), preferred_element_type=WIDE)


def two_parts(value):
    high = value.astype(LOW)
    return high, (value - high.astype(WIDE)).astype(LOW)


def sigmoid_of(value):
    return 0.5 * jnp.tanh(0.5 * value) + 0.5


def iota(shape, dim):
    return lax.broadcasted_iota(jnp.int32, shape, dim)


def split(value, size):
    if size & (size - 1) == 0:
        return value >> (size.bit_length() - 1), value & (size - 1)
    return value // size, value % size


def wrapped(value, size):
    if size & (size - 1) == 0:
        return value & (size - 1)
    return jnp.mod(value, size)


def edge_codes(edges, glon, lat, col, rows, cols):
    row = iota(edges.shape, 0)
    lane = iota(edges.shape, 1)
    j = lane % 16
    at_row, at_col = split(edges, glon)
    down = at_row - (2 * (lat * rows + row) - 2)
    across = wrapped(at_col - (2 * (col * cols + j) - 2), glon)
    place = 2 * (j % 8) + 6 + across
    own = down * 16 + place + jnp.where(place >= 16, 112, 0)
    base = down * 16 + across + 6
    turned = jnp.where(j < 4, pltpu.roll(base, 256 - 12, 1), pltpu.roll(base, 4, 1))
    sent = turned + 2 * (j - 4) + jnp.where(j < 4, 0, 128)
    return own.astype(WIDE), sent.astype(WIDE)


def up_codes(edges, m1lon, lat, col, rep, rows, cols):
    row = iota(edges.shape, 0)
    l16 = iota(edges.shape, 1) % 16
    low = jnp.where(l16 < 8, edges, pltpu.roll(edges, 8, 1))
    high = jnp.where(l16 < 8, pltpu.roll(edges, 128 - 8, 1), edges)
    edges = jnp.where(rep == 0, low, high)
    b = l16 % 8
    at_row, at_col = split(edges, m1lon)
    down = at_row - (2 * (lat * rows + row) - 1)
    across = wrapped(at_col - (2 * (col * cols + b) - 1), m1lon)
    base = jnp.where(l16 < 8, b, jnp.where(b >= 4, b - 8, b + 8))
    at = 2 * base - 1 + across
    at = jnp.where(at < 0, at + 20, jnp.where(at >= 16, at + 4, at))
    return (down * 32 + at).astype(WIDE)


def pack_kernel(dirs, glon, m1lon, grid, m1, cot, m2, edges, ups, codes, *outs):
    rep = lax.axis_index("rep")
    lat = lax.axis_index("lat")
    col = lax.axis_index("lon") * 2 + rep
    sides = outs[:2]
    bands = outs[2:]
    flat = jnp.concatenate([edges[k] for k in range(16)], axis=1)
    own_k, sent_k = edge_codes(flat, glon, lat, col, 16, 16)
    flat = jnp.concatenate([ups[k] for k in range(8)], axis=1)
    up_k = up_codes(flat, m1lon, lat, col, rep, 8, 8)
    up_k = jnp.concatenate([up_k, jnp.zeros_like(up_k)], 1)
    codes[0:16, :] = own_k.astype(LOW)
    codes[16:32, :] = sent_k.astype(LOW)
    codes[32:48, :] = jnp.concatenate([up_k, jnp.zeros_like(up_k)], 0).astype(LOW)
    m2w = m2[...].astype(WIDE)
    m2_half = jnp.where(rep == 0, m2w[:, 0:8], m2w[:, 8:16])
    row8 = iota((8, 256), 0)

    def few(k_rows, last, ghost):
        up = jnp.where(last, up_k[7:8], up_k[0:1])
        rest = jnp.where(row8 == 3, jnp.broadcast_to(up, (8, 256)), 0.0)
        if ghost is not None:
            rest = jnp.where(row8 == 4, jnp.broadcast_to(ghost, (8, 256)), rest)
        return jnp.where(last, jnp.where(row8 >= 5, k_rows[8:16], rest), jnp.where(row8 < 3, k_rows[0:8], rest))

    def last_rows(sends_bottom):
        if sends_bottom is None:
            return lat == 0
        return jnp.bool_(sends_bottom)

    def fill(targets, right):
        side, corners = targets
        g = grid[:, 16:32, :] if right else grid[:, 0:16, :]
        g = g.astype(WIDE)[:, 8:16] if right else g.astype(WIDE)[:, 0:8]
        part = slice(12, 16) if right else slice(0, 4)
        pair = jnp.concatenate([m1[...].astype(WIDE)[:, part], cot[...].astype(WIDE)[:, part]], axis=1)
        edge = 7 if right else 0
        ghosts = jnp.zeros((8, 256), WIDE)
        for a in range(8):
            ghosts = jnp.where(row8 == a, jnp.broadcast_to(m2_half[a, edge : edge + 1], (8, 256)), ghosts)
        side[0:256, :] = g.reshape(256, 256).astype(LOW)
        side[256:384, :] = pair.reshape(128, 256).astype(LOW)
        side[384:400, :] = sent_k.astype(LOW)
        side[400:416, :] = jnp.concatenate([up_k, ghosts], 0).astype(LOW)
        for sends_bottom, corner in corners:
            last = last_rows(sends_bottom)
            corner[0:64, :] = jnp.where(last, g[24:32], g[0:8]).reshape(64, 256).astype(LOW)
            corner[64:96, :] = jnp.where(last, pair[12:16], pair[0:4]).reshape(32, 256).astype(LOW)
            block = few(sent_k, last, jnp.where(last, ghosts[7:8], ghosts[0:1]))
            corner[96:112, :] = jnp.concatenate([block, block], 0).astype(LOW)

    sib = (sides[0], [(d, bands[3 * i + 1]) for i, d in enumerate(dirs)])
    out = (sides[1], [(d, bands[3 * i + 2]) for i, d in enumerate(dirs)])

    @pl.when(rep == 0)
    def _():
        fill(sib, True)
        fill(out, False)

    @pl.when(rep == 1)
    def _():
        fill(sib, False)
        fill(out, True)

    for i, sends_bottom in enumerate(dirs):
        band = bands[3 * i]
        last = last_rows(sends_bottom)
        first = jnp.where(last, 1, 0)
        band[0:256, :] = grid[pl.ds(first * 24, 8)].reshape(256, 256)
        band[256:304, :] = m1[pl.ds(first * 13, 3)].reshape(48, 256)
        band[304:336, :] = cot[pl.ds(first * 14, 2)].reshape(32, 256)
        mt = jnp.where(last, m2_half[7], m2_half[0])
        band[336:352, :] = jnp.concatenate([few(own_k, last, None), mt], 0).astype(LOW)


def set_masks(masks):
    edge = iota((128, 256), 0)
    lanes = iota((128, 256), 1)
    slot = edge % 8
    base = (edge // 8) * 16
    masks[0] = jnp.where(lanes == base + slot, 1.0, 0.0).astype(LOW)
    masks[1] = jnp.where(lanes == base + 8 + slot, 1.0, 0.0).astype(LOW)
    masks[2] = jnp.where(lanes == base + jnp.where(slot < 7, slot, 15), 1.0, 0.0).astype(LOW)


def encode_tiles(tiles, weight):
    count = len(tiles)
    ones = jnp.ones((256, 256), LOW)
    places = iota((128, 256), 1).astype(WIDE)
    picked = [(mask.reshape(8, 16, 256) * codes[None]).reshape(128, 256) for mask, codes, _, _ in tiles]
    found = mm(jnp.concatenate(picked, 0), ones)
    senders = []
    for i, (_, _, window, _) in enumerate(tiles):
        chosen = jnp.where(found[i * 128 : i * 128 + 128] == places, 1.0, 0.0).astype(LOW)
        senders.append(mm(chosen, jnp.concatenate(window, 0)).astype(LOW))
    pre_all = mm(jnp.concatenate(senders, 0), weight)
    results = []
    for i in range(count):
        pre = pre_all[i * 128 : i * 128 + 128].reshape(16, 8, 256) + tiles[i][3][None]
        sig = sigmoid_of(pre)
        act = pre * sig
        rise = sig + act * (1.0 - sig)
        results.append(
            (senders[i], jnp.sum(act, axis=0) * (1.0 / 16), rise.reshape(128, 256).astype(LOW), jnp.sum(rise, axis=0))
        )
    return results


BLOCKS = ((0, 1), (1, 2), (0, 2))


def inner_kernel(grid, m1, codes, weights, sx, slope, pool, ssum, gx, masks, ko, recv):
    set_masks(masks)

    def place_grid(step, carry):
        r = step * 8
        wide = grid[pl.ds(r, 8)].astype(WIDE)
        edge = jnp.zeros((8, 8, 256), WIDE)
        gx[0, pl.ds(r, 8)] = jnp.concatenate([edge, wide[:, 0:8]], 1).astype(LOW)
        gx[1, pl.ds(r, 8)] = wide[:, 8:24].astype(LOW)
        gx[2, pl.ds(r, 8)] = jnp.concatenate([wide[:, 24:32], edge], 1).astype(LOW)
        return carry

    lax.fori_loop(0, 4, place_grid, 0)
    gx[:, 32:34] = jnp.zeros((3, 2, 16, 256), LOW)
    own = codes[0:16, :].astype(WIDE)
    for r in range(16):
        ko[r] = jnp.broadcast_to(own[r : r + 1], (16, 256)).astype(LOW)
    recv[...] = mm(m1[...].reshape(256, 256), weights[1]).reshape(16, 16, 256)

    def rows(step, carry):
        tiles = []
        for k in range(2):
            r = 1 + 2 * step + k
            for tile in range(2):
                window = [gx[blk, pl.ds(2 * r - 2, 8)].reshape(128, 256) for blk in BLOCKS[tile]]
                tiles.append((masks[tile], ko[r], window, recv[r, tile * 8 : tile * 8 + 8]))
        done = encode_tiles(tiles, weights[0])
        for k in range(2):
            r = 1 + 2 * step + k
            for tile in range(2):
                senders, mean, rise, total = done[2 * k + tile]
                sx[r, tile] = senders
                slope[r, tile] = rise
                pool[r, tile * 8 : tile * 8 + 8] = mean
                ssum[r, tile * 8 : tile * 8 + 8] = total
        return carry

    lax.fori_loop(0, 7, rows, 0)


def main_kernel(
    dirs, n_lat, own, sides, bands, weights, outs, scratch
):
    grid, m1, cot, m2, codes, sx_in, slope_in, pool_in, ssum_in = own
    mesh_out, mesh1_grad, keep, send = outs
    gx, m1x, recv, ko, k2, uv, sx, slope, ssum, pool, fx, cx, m2x, ohu, su, uslope, dd, acc_s, fd_s, masks = scratch
    rep = lax.axis_index("rep")
    lat = lax.axis_index("lat")
    frame = m1x.shape[0]
    a_frame = m2x.shape[0]
    if n_lat == 2:
        g_own, f_own, c_own, a_own = 4 + 4 * lat, 1 + 2 * lat, 2 * lat, lat
        odd_rows = 5
        odd_row = lambda i: jnp.where(lat == 0, jnp.where(i == 0, 1, 15 + i), jnp.where(i < 4, i, 18))
    else:
        g_own, f_own, c_own, a_own = 8, 3, 2, 1
        odd_rows = 8
        odd_row = lambda i: jnp.where(i < 4, i, 14 + i)

    def left_right(sib, out):
        return jnp.where(rep == 1, sib, out), jnp.where(rep == 1, out, sib)

    zero_rows = jnp.zeros((4, 16, 256), LOW)
    for blk in range(3):
        gx[blk, 0:4] = zero_rows
        gx[blk, gx.shape[1] - 6 : gx.shape[1] - 2] = zero_rows
        gx[blk, gx.shape[1] - 4 :] = zero_rows

    def put_grid(at, mid, sib, out):
        n = mid.shape[0]
        left, right = left_right(sib.astype(WIDE), out.astype(WIDE))
        left = left.reshape(n, 8, 256)
        right = right.reshape(n, 8, 256)
        wide = mid.astype(WIDE)
        gx[0, pl.ds(at, n)] = jnp.concatenate([left, wide[:, 0:8]], 1).astype(LOW)
        gx[1, pl.ds(at, n)] = wide[:, 8:24].astype(LOW)
        gx[2, pl.ds(at, n)] = jnp.concatenate([wide[:, 24:32], right], 1).astype(LOW)

    def own_grid(step, carry):
        r = step * 8
        r8 = pl.multiple_of(step * 64, 64)
        put_grid(g_own + r, grid[pl.ds(r, 8)], sides[0][pl.ds(r8, 64), :], sides[1][pl.ds(r8, 64), :])
        return carry

    lax.fori_loop(0, 4, own_grid, 0)

    def put_fine(sib, out, n, mid):
        left, right = left_right(sib.astype(WIDE), out.astype(WIDE))
        left = left.reshape(n, 8, 256)
        right = right.reshape(n, 8, 256)
        slot = iota((n, 8, 256), 1)
        states = jnp.concatenate([left[:, 0:4], right[:, 0:4]], 1)
        states = jnp.where(slot == 0, mid[:, 0:8], jnp.where(slot == 7, mid[:, 8:16], states))
        cots = jnp.concatenate([left[:, 4:8], right[:, 4:8]], 1)
        return states, cots

    m1x[...] = jnp.zeros_like(m1x)
    cx[...] = jnp.zeros_like(cx)
    m1_wide = m1[...].astype(WIDE)
    states, cots = put_fine(sides[0][256:384, :], sides[1][256:384, :], 16, m1_wide)
    m1x[pl.ds(f_own, 16), 0:16] = m1_wide
    m1x[pl.ds(f_own, 16), 16:24] = states
    cx[pl.ds(c_own, 16), 0:16] = cot[...]
    cx[pl.ds(c_own, 16), 16:32] = jnp.concatenate([cots, jnp.zeros_like(cots)], 1).astype(LOW)

    def put_m2(at, mid, sib, out, n):
        left, right = left_right(sib, out)
        slot = iota((8, 256), 0)
        for a in range(n):
            l_a = jnp.broadcast_to(left[a : a + 1], (8, 256))
            r_a = jnp.broadcast_to(right[a : a + 1], (8, 256))
            ghost = jnp.where(slot == 7, l_a, jnp.where(slot == 0, r_a, 0.0))
            m2x[at + a] = jnp.concatenate([mid[a], ghost], 0)

    m2w = m2[...].astype(WIDE)
    m2_half = jnp.where(rep == 0, m2w[:, 0:8], m2w[:, 8:16])
    side_few = [side[384:416, :].astype(WIDE) for side in sides]
    put_m2(a_own, m2_half, side_few[0][24:32], side_few[1][24:32], 8)

    def codes_of(mid, sib, out):
        left, right = left_right(sib, out)
        l16 = iota(mid.shape, 1) % 16
        return jnp.where((l16 == 0) | (l16 == 15), mid, jnp.where(l16 < 4, left, right))

    def ups_of(mid, sib, out):
        left, right = left_right(sib, out)
        l16 = iota(mid.shape, 1) % 16
        return jnp.where(l16 < 8, mid, jnp.where(l16 < 12, right, left))[:, 0:128]

    def put_codes(f_at, a_at, own_rows, halo_rows, up_rows):
        for r in range(own_rows.shape[0]):
            ko[f_at + r] = jnp.broadcast_to(own_rows[r : r + 1], (16, 256)).astype(LOW)
            k2[f_at + r] = jnp.broadcast_to(halo_rows[r : r + 1], (16, 256)).astype(LOW)
        for r in range(up_rows.shape[0]):
            uv[a_at + r] = jnp.broadcast_to(up_rows[r : r + 1], (8, 128))

    own_codes = codes[...].astype(WIDE)
    put_codes(
        f_own, a_own, own_codes[0:16],
        codes_of(own_codes[0:16], side_few[0][0:16], side_few[1][0:16]),
        ups_of(own_codes[32:40], side_few[0][16:24], side_few[1][16:24]),
    )
    for i, sends_bottom in enumerate(dirs):
        band, corner_sib, corner_out = bands[3 * i : 3 * i + 3]
        if sends_bottom is None:
            top = lat
        else:
            top = 1 if sends_bottom else 0
        below = 1 - top
        put_grid(
            below * (g_own + 32), band[0:256, :].reshape(8, 32, 256), corner_sib[0:64, :], corner_out[0:64, :]
        )
        is_top = top == 1
        mids = band[256:304, :].astype(WIDE).reshape(3, 16, 256)
        mids4 = jnp.where(is_top, jnp.concatenate([mids[0:1], mids], 0), jnp.concatenate([mids, mids[2:3]], 0))
        states, cots = put_fine(corner_sib[64:96, :], corner_out[64:96, :], 4, mids4)
        f_at = below * (f_own + 16)
        c_at = below * (c_own + 16)
        a_at = below * (a_own + 8)
        m1x[pl.ds(f_at, 3), 0:16] = mids
        m1x[pl.ds(f_at, 3), 16:24] = jnp.where(is_top, states[1:4], states[0:3])
        cx[pl.ds(c_at, 2), 0:16] = band[304:336, :].reshape(2, 16, 256)
        cots = jnp.where(is_top, cots[2:4], cots[0:2])
        cx[pl.ds(c_at, 2), 16:32] = jnp.concatenate([cots, jnp.zeros_like(cots)], 1).astype(LOW)
        band_few = band[336:352, :].astype(WIDE)
        sib_few = corner_sib[96:112, :].astype(WIDE)[0:8]
        out_few = corner_out[96:112, :].astype(WIDE)[0:8]
        put_m2(a_at, band_few[8:16].reshape(1, 8, 256), sib_few[4:5], out_few[4:5], 1)
        own_k = band_few[0:8]
        halo_k = codes_of(own_k, sib_few, out_few)
        up_k = ups_of(own_k, sib_few, out_few)
        put_codes(
            f_at, a_at,
            jnp.where(is_top, own_k[5:8], own_k[0:3]),
            jnp.where(is_top, halo_k[5:8], halo_k[0:3]),
            up_k[3:4],
        )

    set_masks(masks)
    recv[...] = mm(m1x[...].reshape(frame * 24, 256).astype(LOW), weights[1]).reshape(frame, 24, 256)
    pool[...] = jnp.zeros_like(pool)

    def window_of(f, tile):
        return [gx[blk, pl.ds(2 * f, 8)].reshape(128, 256) for blk in BLOCKS[tile]]

    def encode_row(i, carry):
        f = odd_row(i)
        tiles = []
        for tile in range(3):
            vec = ko[f] if tile < 2 else k2[f]
            tiles.append((masks[tile], vec, window_of(f, tile), recv[f, tile * 8 : tile * 8 + 8]))
        done = encode_tiles(tiles, weights[0])
        for tile in range(3):
            senders, mean, rise, total = done[tile]
            pool[f, tile * 8 : tile * 8 + 8] = mean
            if tile < 2:
                sx[f, tile] = senders
                slope[f, tile] = rise
                ssum[f, tile * 8 : tile * 8 + 8] = total
        return carry

    lax.fori_loop(0, odd_rows, encode_row, 0)
    slots = iota((8, 256), 0)
    edge_slots = iota((128, 256), 0) % 8

    def encode_halo(step, carry):
        tiles = []
        for k in range(HALO_ROWS):
            f = f_own + 1 + HALO_ROWS * step + k
            tiles.append((masks[2], k2[f], window_of(f, 2), recv[f, 16:24]))
        done = encode_tiles(tiles, weights[0])
        for k in range(HALO_ROWS):
            r = 1 + HALO_ROWS * step + k
            f = f_own + r
            senders, mean, rise, total = done[k]
            pool[f, 16:24] = mean
            for tile, slot in ((0, 0), (1, 7)):
                part = slice(tile * 8, tile * 8 + 8)
                pool[f, part] = jnp.where(slots == slot, mean, pool_in[r, part])
                ssum[f, part] = jnp.where(slots == slot, total, ssum_in[r, part])
                ours = edge_slots == slot
                sx[f, tile] = jnp.where(ours, senders.astype(WIDE), sx_in[r, tile].astype(WIDE)).astype(LOW)
                slope[f, tile] = jnp.where(ours, rise.astype(WIDE), slope_in[r, tile].astype(WIDE)).astype(LOW)
        return carry

    lax.fori_loop(0, 14 // HALO_ROWS, encode_halo, 0)
    fine = m1x[...].reshape(frame * 24, 256) + mm(pool[...].reshape(frame * 24, 256).astype(LOW), weights[2])
    fine = fine.reshape(frame, 24, 256)
    fx[:, 0:16] = fine[:, 0:16].astype(LOW)
    fx[:, 16:32] = jnp.concatenate([fine[:, 16:24], jnp.zeros((frame, 8, 256), WIDE)], 1).astype(LOW)

    edge = iota((128, 128), 0)
    lanes = iota((128, 128), 1)
    up_mask = jnp.where(lanes == edge, 1.0, 0.0)
    up_places = lanes.astype(WIDE)
    up_ones = jnp.ones((128, 128), LOW)
    m2_flat = m2x[...].reshape(a_frame * 16, 256)
    m2_low = m2_flat.astype(LOW)
    up_recv = mm(m2_low, weights[4]).reshape(a_frame, 16, 256)
    pools = []
    for aa in range(a_frame):
        vec = uv[aa]
        picked = (up_mask.reshape(16, 8, 128) * vec[None]).reshape(128, 128).astype(LOW)
        chosen = jnp.where(mm(picked, up_ones) == up_places, 1.0, 0.0).astype(LOW)
        ohu[aa] = chosen
        senders = mm(chosen, fx[2 * aa : 2 * aa + 4].reshape(128, 256)).astype(LOW)
        su[aa] = senders
        pre = mm(senders, weights[3]).reshape(8, 16, 256) + up_recv[aa][None]
        sig = sigmoid_of(pre)
        act = pre * sig
        pools.append(jnp.sum(act, axis=0) * (1.0 / 8))
        uslope[aa] = (sig + act * (1.0 - sig)).reshape(128, 256)
    up_pool = jnp.concatenate(pools, 0).astype(LOW)
    coarse = (m2_flat + mm(up_pool, weights[5])).astype(LOW)

    c_frame = 2 * a_frame
    nodes = a_frame * 16

    def parent_slot(q):
        return jnp.where(q < 16, q // 2, jnp.where((q == 18) | (q == 19), 15, jnp.where((q == 20) | (q == 21), 8, -1)))

    r_i = iota((c_frame * 32, nodes), 0)
    r_j = iota((c_frame * 32, nodes), 1)
    spread = (r_i // 64 == r_j // 16) & (parent_slot(r_i % 32) == r_j % 16)
    spread = jnp.where(spread, 1.0, 0.0).astype(LOW)
    t_i = iota((nodes, c_frame * 32), 1)
    t_j = iota((nodes, c_frame * 32), 0)
    gather = (t_i // 64 == t_j // 16) & (parent_slot(t_i % 32) == t_j % 16)
    gather = jnp.where(gather, 1.0, 0.0).astype(LOW)
    parents = mm(spread, coarse).astype(LOW)
    fine_mid = fx[1 : 1 + c_frame].reshape(c_frame * 32, 256)
    down_pre = mm(parents, weights[6]) + mm(fine_mid, weights[7])
    sig = sigmoid_of(down_pre)
    act = down_pre * sig
    cot_w = mm_nt(cx[...].reshape(c_frame * 32, 256), weights[8])
    dd[0] = (cot_w * (sig + act * (1.0 - sig))).astype(LOW).reshape(c_frame, 32, 256)
    dd[1] = act.astype(LOW).reshape(c_frame, 32, 256)

    def put_grad(index, value):
        acc_s[...] = value
        keep[index] = acc_s[pl.ds(pl.multiple_of(rep * 128, 128), 128), :]
        send[index] = acc_s[pl.ds(pl.multiple_of((1 - rep) * 128, 128), 128), :].astype(LOW)

    act_own = dd[1, pl.ds(c_own, 16), 0:16].reshape(256, 256)
    delta_own = dd[0, pl.ds(c_own, 16), 0:16].reshape(256, 256)
    fine_own = fx[pl.ds(f_own, 16), 0:16].reshape(256, 256)
    cot_own = cot[...].reshape(256, 256)
    out = fine_own.astype(WIDE) + mm(act_own, weights[8])
    mesh_out[...] = out.astype(LOW).reshape(16, 16, 256)
    put_grad(8, mm_tn(act_own, cot_own))
    put_grad(7, mm_tn(fine_own, delta_own))

    child_sum = mm(gather, dd[0].reshape(c_frame * 32, 256))
    n_i = iota((nodes, 256), 0)
    aa_i, bb_i = n_i // 16, n_i % 16
    is_own = (aa_i >= a_own) & (aa_i < a_own + 8) & (bb_i < 8)
    is_real = (bb_i <= 8) | (bb_i == 15)
    if n_lat != 2:
        above = lat * 8 - 1 + aa_i
        is_real = is_real & (above >= 0) & (above < n_lat * 8)
    sum_high, sum_low = two_parts(child_sum)
    coarse_delta = (mm_nt(sum_high, weights[6]) + mm_nt(sum_low, weights[6])).astype(LOW)
    own_high, own_low = two_parts(jnp.where(is_own, child_sum, 0.0))
    put_grad(6, mm_tn(coarse, own_high) + mm_tn(coarse, own_low))
    own_delta = jnp.where(is_own, coarse_delta.astype(WIDE), 0.0).astype(LOW)
    put_grad(5, mm_tn(up_pool, own_delta))
    pool2 = jnp.where(is_real, mm_nt(coarse_delta, weights[5]) * (1.0 / 8), 0.0)
    own_f = jnp.where(is_own, 1.0, 0.0)
    recv[...] = jnp.zeros_like(recv)
    acc_s[...] = jnp.zeros_like(acc_s)
    node_sums = []
    for aa in range(a_frame):
        d = pool2[aa * 16 : aa * 16 + 16][None] * uslope[aa].reshape(8, 16, 256)
        mine = own_f[aa * 16 : aa * 16 + 16][None]
        up_delta = d.astype(LOW)
        wide = up_delta.astype(WIDE)
        owned = wide * mine
        node_sums.append(jnp.sum(owned, axis=0))
        back = mm_tn(ohu[aa], up_delta.reshape(128, 256)).reshape(4, 32, 256)
        recv[2 * aa : 2 * aa + 4] += back[:, 0:24]
        acc_s[...] += mm_tn(su[aa], owned.reshape(128, 256).astype(LOW))
    put_grad(3, acc_s[...])
    ns_high, ns_low = two_parts(jnp.concatenate(node_sums, 0))
    put_grad(4, mm_tn(m2_low, ns_high) + mm_tn(m2_low, ns_low))
    back_high, back_low = two_parts(recv[pl.ds(f_own, 16), 0:16].reshape(256, 256))
    fine_delta = (
        cot_own.astype(WIDE)
        + mm_nt(delta_own, weights[7])
        + mm_nt(back_high, weights[3])
        + mm_nt(back_low, weights[3])
    )
    fd_s[...] = fine_delta
    fine_delta_b = fine_delta.astype(LOW)

    pool_own = pool[pl.ds(f_own, 16), 0:16].reshape(256, 256).astype(LOW)
    put_grad(2, mm_tn(pool_own, fine_delta_b))
    pool_delta = mm_nt(fine_delta_b, weights[2]) * (1.0 / 16)
    node_delta = pool_delta * ssum[pl.ds(f_own, 16)].reshape(256, 256)
    nd_high, nd_low = two_parts(node_delta)
    m1_own = m1[...].reshape(256, 256)
    put_grad(1, mm_tn(m1_own, nd_high) + mm_tn(m1_own, nd_low))
    grad_in = fd_s[...] + (mm_nt(nd_high, weights[1]) + mm_nt(nd_low, weights[1]))
    mesh1_grad[...] = grad_in.astype(LOW).reshape(16, 16, 256)
    m1x[0:16, 0:16] = pool_delta.reshape(16, 16, 256)
    acc_s[...] = jnp.zeros_like(acc_s)

    def encode_back(r, carry):
        deltas = []
        for tile in range(2):
            d = m1x[r, tile * 8 : tile * 8 + 8][None] * slope[f_own + r, tile].astype(WIDE).reshape(16, 8, 256)
            deltas.append(d.reshape(128, 256).astype(LOW))
        acc_s[...] += mm_tn(sx[f_own + r].reshape(256, 256), jnp.concatenate(deltas, 0))
        return carry

    lax.fori_loop(0, 16, encode_back, 0)
    put_grad(0, acc_s[...])


def flat_main(dirs, n_lat, *refs):
    n_bands = 3 * len(dirs)
    own, refs = refs[:9], refs[9:]
    sides, refs = refs[:2], refs[2:]
    bands, refs = refs[:n_bands], refs[n_bands:]
    weights, refs = refs[0], refs[1:]
    outs, scratch = refs[:4], refs[4:]
    main_kernel(dirs, n_lat, own, sides, bands, weights, outs, scratch)


def sum_over_slice(kept, sent, mesh):
    lat_size, lon_size = mesh.shape["lat"], mesh.shape["lon"]
    rep = lax.axis_index("rep")
    lat, lon = lax.axis_index("lat"), lax.axis_index("lon")
    place = (lat % 2) * 2 + lon % 2

    def between(values, lon_bit, lat_bit):
        return permute(
            values,
            ("lon", "lat"),
            lambda i: ((i // lat_size) ^ lon_bit) * lat_size + ((i % lat_size) ^ lat_bit),
            (lon_size, lat_size),
        )

    def siblings(values):
        return permute(values, "rep", lambda i: i ^ 1, (2,))

    count, rows, cols = kept.shape
    half = kept + siblings(sent).astype(WIDE)
    quarters = half.reshape(count, 4, rows // 4, cols)
    total = lax.dynamic_index_in_dim(quarters, place, 1, keepdims=False)
    for step in (1, 2, 3):
        piece = lax.dynamic_index_in_dim(quarters, place ^ step, 1, keepdims=False).astype(LOW)
        total = total + between(piece, step & 1, step >> 1).astype(WIDE)
    bit = 2
    while bit < lon_size:
        rounded = total.astype(LOW)
        total = rounded.astype(WIDE) + between(rounded, bit, 0).astype(WIDE)
        bit *= 2
    bit = 2
    while bit < lat_size:
        rounded = total.astype(LOW)
        total = rounded.astype(WIDE) + between(rounded, 0, bit).astype(WIDE)
        bit *= 2
    own = total.astype(LOW)
    pieces = [own] + [between(own, step & 1, step >> 1) for step in (1, 2, 3)]
    theirs = [siblings(piece) for piece in pieces]
    mine_all = jnp.stack(pieces, 0)
    theirs_all = jnp.stack(theirs, 0)
    order = jnp.arange(4) ^ place
    mine_half = jnp.take(mine_all, order, axis=0)
    their_half = jnp.take(theirs_all, order, axis=0)
    first = jnp.where(rep == 0, mine_half, their_half)
    second = jnp.where(rep == 0, their_half, mine_half)
    both = jnp.stack([first, second], 0)
    return jnp.moveaxis(both, 2, 0).reshape(count, 2 * rows, cols).astype(WIDE)


def body(mesh, grid_state, mesh1_state, mesh2_state, grid_edges, up_edges, weights, cotangent):
    n_lat, n_lon = mesh.shape["lat"], mesh.shape["lon"]
    glon = grid_state.shape[1] * 2 * n_lon
    m1lon = mesh1_state.shape[1] * 2 * n_lon
    dirs = (None,) if n_lat == 2 else (True, False)
    vmem = pl.BlockSpec(memory_space=pltpu.VMEM)
    params = pltpu.CompilerParams(vmem_limit_bytes=VMEM_BYTES)
    shapes = [48] + [SIDE_ROWS] * 2 + [BAND_ROWS, CORNER_ROWS, CORNER_ROWS] * len(dirs)
    codes, *buffers = pl.pallas_call(
        functools.partial(pack_kernel, dirs, glon, m1lon),
        out_shape=[jax.ShapeDtypeStruct((n, 256), LOW) for n in shapes],
        in_specs=[vmem] * 6,
        out_specs=[vmem] * len(shapes),
        compiler_params=params,
        name="pack_halos",
    )(grid_state, mesh1_state, cotangent, mesh2_state, grid_edges, up_edges)
    inner = pl.pallas_call(
        inner_kernel,
        out_shape=[
            jax.ShapeDtypeStruct((16, 2, 128, 256), LOW),
            jax.ShapeDtypeStruct((16, 2, 128, 256), LOW),
            jax.ShapeDtypeStruct((16, 16, 256), WIDE),
            jax.ShapeDtypeStruct((16, 16, 256), WIDE),
        ],
        in_specs=[vmem] * 4,
        out_specs=[vmem] * 4,
        scratch_shapes=[
            pltpu.VMEM((3, 34, 16, 256), LOW),
            pltpu.VMEM((3, 128, 256), LOW),
            pltpu.VMEM((16, 16, 256), LOW),
            pltpu.VMEM((16, 16, 256), WIDE),
        ],
        compiler_params=params,
        cost_estimate=pl.CostEstimate(flops=4_000_000_000, bytes_accessed=8_000_000, transcendentals=1_000_000),
        name="inner_rows",
    )(grid_state, mesh1_state, codes, weights)
    own = (grid_state, mesh1_state, cotangent, mesh2_state, codes, *inner)

    def beyond(lon, core):
        return ((lon + (1 if core else -1)) % n_lon, 1 - core)

    def send_to(values, other_lat, column):
        def partner(i):
            lon, rest = divmod(i, n_lat * 2)
            row, core = divmod(rest, 2)
            row = other_lat(row)
            if row is None:
                return None
            if column == "sibling":
                core = 1 - core
            elif column == "beyond":
                lon, core = beyond(lon, core)
            return (lon * n_lat + row) * 2 + core

        return permute(values, ("lon", "lat", "rep"), partner, (n_lon, n_lat, 2))

    def shift(sends_bottom):
        if sends_bottom is None:
            return lambda row: row ^ 1
        if sends_bottom:
            return lambda row: row + 1 if row + 1 < n_lat else None
        return lambda row: row - 1 if row else None

    got_sides = [send_to(buffers[0], lambda row: row, "sibling"), send_to(buffers[1], lambda row: row, "beyond")]
    got_bands = []
    for i, sends_bottom in enumerate(dirs):
        for k, column in enumerate(("same", "sibling", "beyond")):
            got_bands.append(send_to(buffers[2 + 3 * i + k], shift(sends_bottom), column))

    frame = 20 if n_lat == 2 else 22
    a_frame = 9 if n_lat == 2 else 10
    c_frame = 2 * a_frame
    g_frame = 2 * frame + 6
    scratch = [
        pltpu.VMEM((3, g_frame, 16, 256), LOW),
        pltpu.VMEM((frame, 24, 256), WIDE),
        pltpu.VMEM((frame, 24, 256), WIDE),
        pltpu.VMEM((frame, 16, 256), LOW),
        pltpu.VMEM((frame, 16, 256), LOW),
        pltpu.VMEM((a_frame, 8, 128), WIDE),
        pltpu.VMEM((frame, 2, 128, 256), LOW),
        pltpu.VMEM((frame, 2, 128, 256), LOW),
        pltpu.VMEM((frame, 16, 256), WIDE),
        pltpu.VMEM((frame, 24, 256), WIDE),
        pltpu.VMEM((frame, 32, 256), LOW),
        pltpu.VMEM((c_frame, 32, 256), LOW),
        pltpu.VMEM((a_frame, 16, 256), WIDE),
        pltpu.VMEM((a_frame, 128, 128), LOW),
        pltpu.VMEM((a_frame, 128, 256), LOW),
        pltpu.VMEM((a_frame, 128, 256), WIDE),
        pltpu.VMEM((2, c_frame, 32, 256), LOW),
        pltpu.VMEM((256, 256), WIDE),
        pltpu.VMEM((256, 256), WIDE),
        pltpu.VMEM((3, 128, 256), LOW),
    ]
    n_in = 9 + 2 + len(got_bands) + 1
    mesh_out, mesh1_grad, kept, sent = pl.pallas_call(
        functools.partial(flat_main, dirs, n_lat),
        out_shape=[
            jax.ShapeDtypeStruct(mesh1_state.shape, LOW),
            jax.ShapeDtypeStruct(mesh1_state.shape, LOW),
            jax.ShapeDtypeStruct((9, 128, 256), WIDE),
            jax.ShapeDtypeStruct((9, 128, 256), LOW),
        ],
        in_specs=[vmem] * n_in,
        out_specs=[vmem] * 4,
        scratch_shapes=scratch,
        compiler_params=params,
        name="sweep",
    )(*own, *got_sides, *got_bands, weights)
    node_total = mesh1_state.shape[0] * mesh1_state.shape[1] * n_lat * n_lon * 2
    weight_grads = sum_over_slice(kept, sent, mesh) * float(node_total) ** (-0.5)
    return (mesh_out, mesh1_grad, weight_grads)


def solution(mesh):
    in_specs = (
        P(("groups", "lat"), ("lon", "rep"), None),
        P(("groups", "lat"), ("lon", "rep"), None),
        P(("groups", "lat"), "lon", None),
        P(None, "lat", ("lon", "rep")),
        P(None, "lat", "lon"),
        P(),
        P(("groups", "lat"), ("lon", "rep"), None),
    )
    out_specs = (
        P(("groups", "lat"), ("lon", "rep"), None),
        P(("groups", "lat"), ("lon", "rep"), None),
        P("groups", None, None),
    )
    return jax.shard_map(
        functools.partial(body, mesh), mesh=mesh, in_specs=in_specs, out_specs=out_specs, check_vma=False
    )
```

```python
import functools

import jax
import jax.numpy as jnp
from jax import lax
from jax.experimental import pallas as pl
from jax.experimental.pallas import tpu as pltpu
from jax.sharding import PartitionSpec as P

LOW = jnp.bfloat16
WIDE = jnp.float32
VMEM_BYTES = 36 * 1024 * 1024
HALO_ROWS = 2

SIDE_ROWS = 416
BAND_ROWS = 352
CORNER_ROWS = 112


def permute(values, axes, partner, sizes):
    total = 1
    for size in sizes:
        total *= size
    pairs = [(i, partner(i)) for i in range(total)]
    return lax.ppermute(values, axes, [(i, j) for i, j in pairs if j is not None])


def mm(left, right):
    return jnp.dot(left, right, preferred_element_type=WIDE)


def mm_nt(left, right):
    return lax.dot_general(left, right, (((1,), (1,)), ((), ())), preferred_element_type=WIDE)


def mm_tn(left, right):
    return lax.dot_general(left, right, (((0,), (0,)), ((), ())), preferred_element_type=WIDE)


def two_parts(value):
    high = value.astype(LOW)
    return high, (value - high.astype(WIDE)).astype(LOW)


def sigmoid_of(value):
    return 0.5 * jnp.tanh(0.5 * value) + 0.5


def iota(shape, dim):
    return lax.broadcasted_iota(jnp.int32, shape, dim)


def in_hbm(value):
    return pltpu.with_memory_space_constraint(value, pltpu.HBM)


def split(value, size):
    if size & (size - 1) == 0:
        return value >> (size.bit_length() - 1), value & (size - 1)
    return value // size, value % size


def wrapped(value, size):
    if size & (size - 1) == 0:
        return value & (size - 1)
    return jnp.mod(value, size)


def edge_codes(edges, glon, lat, col, rows, cols):
    row = iota(edges.shape, 0)
    lane = iota(edges.shape, 1)
    j = lane % 16
    at_row, at_col = split(edges, glon)
    down = at_row - (2 * (lat * rows + row) - 2)
    across = wrapped(at_col - (2 * (col * cols + j) - 2), glon)
    place = 2 * (j % 8) + 6 + across
    own = down * 16 + place + jnp.where(place >= 16, 112, 0)
    base = down * 16 + across + 6
    turned = jnp.where(j < 4, pltpu.roll(base, 256 - 12, 1), pltpu.roll(base, 4, 1))
    sent = turned + 2 * (j - 4) + jnp.where(j < 4, 0, 128)
    return own.astype(WIDE), sent.astype(WIDE)


def up_codes(edges, m1lon, lat, col, rep, rows, cols):
    row = iota(edges.shape, 0)
    l16 = iota(edges.shape, 1) % 16
    low = jnp.where(l16 < 8, edges, pltpu.roll(edges, 8, 1))
    high = jnp.where(l16 < 8, pltpu.roll(edges, 128 - 8, 1), edges)
    edges = jnp.where(rep == 0, low, high)
    b = l16 % 8
    at_row, at_col = split(edges, m1lon)
    down = at_row - (2 * (lat * rows + row) - 1)
    across = wrapped(at_col - (2 * (col * cols + b) - 1), m1lon)
    base = jnp.where(l16 < 8, b, jnp.where(b >= 4, b - 8, b + 8))
    at = 2 * base - 1 + across
    at = jnp.where(at < 0, at + 20, jnp.where(at >= 16, at + 4, at))
    return (down * 32 + at).astype(WIDE)


def pack_kernel(dirs, glon, m1lon, *refs):
    far, (grid, m1, cot, m2, codes), rest = refs[:6], refs[6:11], refs[11:]
    outs, (edges, ups, sems) = rest[:-3], rest[-3:]
    copies = [
        pltpu.make_async_copy(a, b, sems.at[i]) for i, (a, b) in enumerate(zip(far, (grid, m1, cot, m2, edges, ups)))
    ]
    for copy in copies:
        copy.start()
    for copy in copies[::-1]:
        copy.wait()
    rep = lax.axis_index("rep")
    lat = lax.axis_index("lat")
    col = lax.axis_index("lon") * 2 + rep
    sides = outs[:2]
    bands = outs[2:]
    flat = jnp.concatenate([edges[k] for k in range(16)], axis=1)
    own_k, sent_k = edge_codes(flat, glon, lat, col, 16, 16)
    flat = jnp.concatenate([ups[k] for k in range(8)], axis=1)
    up_k = up_codes(flat, m1lon, lat, col, rep, 8, 8)
    up_k = jnp.concatenate([up_k, jnp.zeros_like(up_k)], 1)
    codes[0:16, :] = own_k.astype(LOW)
    codes[16:32, :] = sent_k.astype(LOW)
    codes[32:48, :] = jnp.concatenate([up_k, jnp.zeros_like(up_k)], 0).astype(LOW)
    m2w = m2[...].astype(WIDE)
    m2_half = jnp.where(rep == 0, m2w[:, 0:8], m2w[:, 8:16])
    row8 = iota((8, 256), 0)

    def few(k_rows, last, ghost):
        up = jnp.where(last, up_k[7:8], up_k[0:1])
        rest = jnp.where(row8 == 3, jnp.broadcast_to(up, (8, 256)), 0.0)
        if ghost is not None:
            rest = jnp.where(row8 == 4, jnp.broadcast_to(ghost, (8, 256)), rest)
        return jnp.where(last, jnp.where(row8 >= 5, k_rows[8:16], rest), jnp.where(row8 < 3, k_rows[0:8], rest))

    def last_rows(sends_bottom):
        if sends_bottom is None:
            return lat == 0
        return jnp.bool_(sends_bottom)

    def fill(targets, right):
        side, corners = targets
        g = grid[:, 16:32, :] if right else grid[:, 0:16, :]
        g = g.astype(WIDE)[:, 8:16] if right else g.astype(WIDE)[:, 0:8]
        part = slice(12, 16) if right else slice(0, 4)
        pair = jnp.concatenate([m1[...].astype(WIDE)[:, part], cot[...].astype(WIDE)[:, part]], axis=1)
        edge = 7 if right else 0
        ghosts = jnp.zeros((8, 256), WIDE)
        for a in range(8):
            ghosts = jnp.where(row8 == a, jnp.broadcast_to(m2_half[a, edge : edge + 1], (8, 256)), ghosts)
        side[0:256, :] = g.reshape(256, 256).astype(LOW)
        side[256:384, :] = pair.reshape(128, 256).astype(LOW)
        side[384:400, :] = sent_k.astype(LOW)
        side[400:416, :] = jnp.concatenate([up_k, ghosts], 0).astype(LOW)
        for sends_bottom, corner in corners:
            last = last_rows(sends_bottom)
            corner[0:64, :] = jnp.where(last, g[24:32], g[0:8]).reshape(64, 256).astype(LOW)
            corner[64:96, :] = jnp.where(last, pair[12:16], pair[0:4]).reshape(32, 256).astype(LOW)
            block = few(sent_k, last, jnp.where(last, ghosts[7:8], ghosts[0:1]))
            corner[96:112, :] = jnp.concatenate([block, block], 0).astype(LOW)

    sib = (sides[0], [(d, bands[3 * i + 1]) for i, d in enumerate(dirs)])
    out = (sides[1], [(d, bands[3 * i + 2]) for i, d in enumerate(dirs)])

    @pl.when(rep == 0)
    def _():
        fill(sib, True)
        fill(out, False)

    @pl.when(rep == 1)
    def _():
        fill(sib, False)
        fill(out, True)

    for i, sends_bottom in enumerate(dirs):
        band = bands[3 * i]
        last = last_rows(sends_bottom)
        first = jnp.where(last, 1, 0)
        band[0:256, :] = grid[pl.ds(first * 24, 8)].reshape(256, 256)
        band[256:304, :] = m1[pl.ds(first * 13, 3)].reshape(48, 256)
        band[304:336, :] = cot[pl.ds(first * 14, 2)].reshape(32, 256)
        mt = jnp.where(last, m2_half[7], m2_half[0])
        band[336:352, :] = jnp.concatenate([few(own_k, last, None), mt], 0).astype(LOW)


def set_masks(masks):
    edge = iota((128, 256), 0)
    lanes = iota((128, 256), 1)
    slot = edge % 8
    base = (edge // 8) * 16
    masks[0] = jnp.where(lanes == base + slot, 1.0, 0.0).astype(LOW)
    masks[1] = jnp.where(lanes == base + 8 + slot, 1.0, 0.0).astype(LOW)
    masks[2] = jnp.where(lanes == base + jnp.where(slot < 7, slot, 15), 1.0, 0.0).astype(LOW)


def encode_tiles(tiles, weight):
    count = len(tiles)
    ones = jnp.ones((256, 256), LOW)
    places = iota((128, 256), 1).astype(WIDE)
    picked = [(mask.reshape(8, 16, 256) * codes[None]).reshape(128, 256) for mask, codes, _, _ in tiles]
    found = mm(jnp.concatenate(picked, 0), ones)
    senders = []
    for i, (_, _, window, _) in enumerate(tiles):
        chosen = jnp.where(found[i * 128 : i * 128 + 128] == places, 1.0, 0.0).astype(LOW)
        senders.append(mm(chosen, jnp.concatenate(window, 0)).astype(LOW))
    pre_all = mm(jnp.concatenate(senders, 0), weight)
    results = []
    for i in range(count):
        pre = pre_all[i * 128 : i * 128 + 128].reshape(16, 8, 256) + tiles[i][3][None]
        sig = sigmoid_of(pre)
        act = pre * sig
        rise = sig + act * (1.0 - sig)
        results.append(
            (senders[i], jnp.sum(act, axis=0) * (1.0 / 16), rise.reshape(128, 256).astype(LOW), jnp.sum(rise, axis=0))
        )
    return results


BLOCKS = ((0, 1), (1, 2), (0, 2))


def inner_kernel(grid, m1, codes, far, sx, slope, pool, ssum, weights, gx, masks, ko, recv, sems):
    first = pltpu.make_async_copy(far.at[0:2], weights.at[0:2], sems.at[0])
    others = pltpu.make_async_copy(far.at[2:9], weights.at[2:9], sems.at[1])
    first.start()
    others.start()
    set_masks(masks)

    def place_grid(step, carry):
        r = step * 8
        wide = grid[pl.ds(r, 8)].astype(WIDE)
        edge = jnp.zeros((8, 8, 256), WIDE)
        gx[0, pl.ds(r, 8)] = jnp.concatenate([edge, wide[:, 0:8]], 1).astype(LOW)
        gx[1, pl.ds(r, 8)] = wide[:, 8:24].astype(LOW)
        gx[2, pl.ds(r, 8)] = jnp.concatenate([wide[:, 24:32], edge], 1).astype(LOW)
        return carry

    lax.fori_loop(0, 4, place_grid, 0)
    gx[:, 32:34] = jnp.zeros((3, 2, 16, 256), LOW)
    own = codes[0:16, :].astype(WIDE)
    for r in range(16):
        ko[r] = jnp.broadcast_to(own[r : r + 1], (16, 256)).astype(LOW)
    first.wait()
    recv[...] = mm(m1[...].reshape(256, 256), weights[1]).reshape(16, 16, 256)

    def rows(step, carry):
        tiles = []
        for k in range(2):
            r = 1 + 2 * step + k
            for tile in range(2):
                window = [gx[blk, pl.ds(2 * r - 2, 8)].reshape(128, 256) for blk in BLOCKS[tile]]
                tiles.append((masks[tile], ko[r], window, recv[r, tile * 8 : tile * 8 + 8]))
        done = encode_tiles(tiles, weights[0])
        for k in range(2):
            r = 1 + 2 * step + k
            for tile in range(2):
                senders, mean, rise, total = done[2 * k + tile]
                sx[r, tile] = senders
                slope[r, tile] = rise
                pool[r, tile * 8 : tile * 8 + 8] = mean
                ssum[r, tile * 8 : tile * 8 + 8] = total
        return carry

    lax.fori_loop(0, 7, rows, 0)
    others.wait()


def put_halves(grad, keep, send, index, rep):
    keep[index] = grad[pl.ds(pl.multiple_of(rep * 128, 128), 128), :]
    send[index] = grad[pl.ds(pl.multiple_of((1 - rep) * 128, 128), 128), :].astype(LOW)


def main_kernel(
    dirs, n_lat, own, sides, bands, weights, outs, scratch
):
    grid, m1, cot, m2, codes, pool_in, ssum_in = own
    mesh_out, keep, send, fd_out, pool_out, ssum, sx, slope, hx, hslope = outs
    gx, m1x, recv, ko, k2, uv, pool, fx, cx, m2x, ohu, su, uslope, dd, acc_s, masks = scratch
    rep = lax.axis_index("rep")
    lat = lax.axis_index("lat")
    frame = m1x.shape[0]
    a_frame = m2x.shape[0]
    if n_lat == 2:
        g_own, f_own, c_own, a_own = 4 + 4 * lat, 1 + 2 * lat, 2 * lat, lat
        odd_rows = 5
        odd_row = lambda i: jnp.where(lat == 0, jnp.where(i == 0, 1, 15 + i), jnp.where(i < 4, i, 18))
    else:
        g_own, f_own, c_own, a_own = 8, 3, 2, 1
        odd_rows = 8
        odd_row = lambda i: jnp.where(i < 4, i, 14 + i)

    def left_right(sib, out):
        return jnp.where(rep == 1, sib, out), jnp.where(rep == 1, out, sib)

    zero_rows = jnp.zeros((4, 16, 256), LOW)
    for blk in range(3):
        gx[blk, 0:4] = zero_rows
        gx[blk, gx.shape[1] - 6 : gx.shape[1] - 2] = zero_rows
        gx[blk, gx.shape[1] - 4 :] = zero_rows

    def put_grid(at, mid, sib, out):
        n = mid.shape[0]
        left, right = left_right(sib.astype(WIDE), out.astype(WIDE))
        left = left.reshape(n, 8, 256)
        right = right.reshape(n, 8, 256)
        wide = mid.astype(WIDE)
        gx[0, pl.ds(at, n)] = jnp.concatenate([left, wide[:, 0:8]], 1).astype(LOW)
        gx[1, pl.ds(at, n)] = wide[:, 8:24].astype(LOW)
        gx[2, pl.ds(at, n)] = jnp.concatenate([wide[:, 24:32], right], 1).astype(LOW)

    def own_grid(step, carry):
        r = step * 8
        r8 = pl.multiple_of(step * 64, 64)
        put_grid(g_own + r, grid[pl.ds(r, 8)], sides[0][pl.ds(r8, 64), :], sides[1][pl.ds(r8, 64), :])
        return carry

    lax.fori_loop(0, 4, own_grid, 0)

    def put_fine(sib, out, n, mid):
        left, right = left_right(sib.astype(WIDE), out.astype(WIDE))
        left = left.reshape(n, 8, 256)
        right = right.reshape(n, 8, 256)
        slot = iota((n, 8, 256), 1)
        states = jnp.concatenate([left[:, 0:4], right[:, 0:4]], 1)
        states = jnp.where(slot == 0, mid[:, 0:8], jnp.where(slot == 7, mid[:, 8:16], states))
        cots = jnp.concatenate([left[:, 4:8], right[:, 4:8]], 1)
        return states, cots

    m1x[...] = jnp.zeros_like(m1x)
    cx[...] = jnp.zeros_like(cx)
    m1_wide = m1[...].astype(WIDE)
    states, cots = put_fine(sides[0][256:384, :], sides[1][256:384, :], 16, m1_wide)
    m1x[pl.ds(f_own, 16), 0:16] = m1_wide
    m1x[pl.ds(f_own, 16), 16:24] = states
    cx[pl.ds(c_own, 16), 0:16] = cot[...]
    cx[pl.ds(c_own, 16), 16:32] = jnp.concatenate([cots, jnp.zeros_like(cots)], 1).astype(LOW)

    def put_m2(at, mid, sib, out, n):
        left, right = left_right(sib, out)
        slot = iota((8, 256), 0)
        for a in range(n):
            l_a = jnp.broadcast_to(left[a : a + 1], (8, 256))
            r_a = jnp.broadcast_to(right[a : a + 1], (8, 256))
            ghost = jnp.where(slot == 7, l_a, jnp.where(slot == 0, r_a, 0.0))
            m2x[at + a] = jnp.concatenate([mid[a], ghost], 0)

    m2w = m2[...].astype(WIDE)
    m2_half = jnp.where(rep == 0, m2w[:, 0:8], m2w[:, 8:16])
    side_few = [side[384:416, :].astype(WIDE) for side in sides]
    put_m2(a_own, m2_half, side_few[0][24:32], side_few[1][24:32], 8)

    def codes_of(mid, sib, out):
        left, right = left_right(sib, out)
        l16 = iota(mid.shape, 1) % 16
        return jnp.where((l16 == 0) | (l16 == 15), mid, jnp.where(l16 < 4, left, right))

    def ups_of(mid, sib, out):
        left, right = left_right(sib, out)
        l16 = iota(mid.shape, 1) % 16
        return jnp.where(l16 < 8, mid, jnp.where(l16 < 12, right, left))[:, 0:128]

    def put_codes(f_at, a_at, own_rows, halo_rows, up_rows):
        for r in range(own_rows.shape[0]):
            ko[f_at + r] = jnp.broadcast_to(own_rows[r : r + 1], (16, 256)).astype(LOW)
            k2[f_at + r] = jnp.broadcast_to(halo_rows[r : r + 1], (16, 256)).astype(LOW)
        for r in range(up_rows.shape[0]):
            uv[a_at + r] = jnp.broadcast_to(up_rows[r : r + 1], (8, 128))

    own_codes = codes[...].astype(WIDE)
    put_codes(
        f_own, a_own, own_codes[0:16],
        codes_of(own_codes[0:16], side_few[0][0:16], side_few[1][0:16]),
        ups_of(own_codes[32:40], side_few[0][16:24], side_few[1][16:24]),
    )
    for i, sends_bottom in enumerate(dirs):
        band, corner_sib, corner_out = bands[3 * i : 3 * i + 3]
        if sends_bottom is None:
            top = lat
        else:
            top = 1 if sends_bottom else 0
        below = 1 - top
        put_grid(
            below * (g_own + 32), band[0:256, :].reshape(8, 32, 256), corner_sib[0:64, :], corner_out[0:64, :]
        )
        is_top = top == 1
        mids = band[256:304, :].astype(WIDE).reshape(3, 16, 256)
        mids4 = jnp.where(is_top, jnp.concatenate([mids[0:1], mids], 0), jnp.concatenate([mids, mids[2:3]], 0))
        states, cots = put_fine(corner_sib[64:96, :], corner_out[64:96, :], 4, mids4)
        f_at = below * (f_own + 16)
        c_at = below * (c_own + 16)
        a_at = below * (a_own + 8)
        m1x[pl.ds(f_at, 3), 0:16] = mids
        m1x[pl.ds(f_at, 3), 16:24] = jnp.where(is_top, states[1:4], states[0:3])
        cx[pl.ds(c_at, 2), 0:16] = band[304:336, :].reshape(2, 16, 256)
        cots = jnp.where(is_top, cots[2:4], cots[0:2])
        cx[pl.ds(c_at, 2), 16:32] = jnp.concatenate([cots, jnp.zeros_like(cots)], 1).astype(LOW)
        band_few = band[336:352, :].astype(WIDE)
        sib_few = corner_sib[96:112, :].astype(WIDE)[0:8]
        out_few = corner_out[96:112, :].astype(WIDE)[0:8]
        put_m2(a_at, band_few[8:16].reshape(1, 8, 256), sib_few[4:5], out_few[4:5], 1)
        own_k = band_few[0:8]
        halo_k = codes_of(own_k, sib_few, out_few)
        up_k = ups_of(own_k, sib_few, out_few)
        put_codes(
            f_at, a_at,
            jnp.where(is_top, own_k[5:8], own_k[0:3]),
            jnp.where(is_top, halo_k[5:8], halo_k[0:3]),
            up_k[3:4],
        )

    set_masks(masks)
    recv[...] = mm(m1x[...].reshape(frame * 24, 256).astype(LOW), weights[1]).reshape(frame, 24, 256)
    pool[...] = jnp.zeros_like(pool)

    def window_of(f, tile):
        return [gx[blk, pl.ds(2 * f, 8)].reshape(128, 256) for blk in BLOCKS[tile]]

    def encode_row(i, carry):
        f = odd_row(i)
        tiles = []
        for tile in range(3):
            vec = ko[f] if tile < 2 else k2[f]
            tiles.append((masks[tile], vec, window_of(f, tile), recv[f, tile * 8 : tile * 8 + 8]))
        done = encode_tiles(tiles, weights[0])
        row = f - f_own
        kept_at = jnp.where(row == 0, 0, jnp.where(row == 15, 1, 2))
        row = jnp.where(kept_at == 2, 16, row)
        for tile in range(3):
            senders, mean, rise, total = done[tile]
            pool[f, tile * 8 : tile * 8 + 8] = mean
            if tile < 2:
                sx[kept_at, tile] = senders
                slope[kept_at, tile] = rise
                ssum[row, tile * 8 : tile * 8 + 8] = total
        return carry

    lax.fori_loop(0, odd_rows, encode_row, 0)
    slots = iota((8, 256), 0)

    def encode_halo(step, carry):
        tiles = []
        for k in range(HALO_ROWS):
            f = f_own + 1 + HALO_ROWS * step + k
            tiles.append((masks[2], k2[f], window_of(f, 2), recv[f, 16:24]))
        done = encode_tiles(tiles, weights[0])
        for k in range(HALO_ROWS):
            r = 1 + HALO_ROWS * step + k
            f = f_own + r
            senders, mean, rise, total = done[k]
            pool[f, 16:24] = mean
            hx[r - 1] = senders
            hslope[r - 1] = rise
            for tile, slot in ((0, 0), (1, 7)):
                part = slice(tile * 8, tile * 8 + 8)
                pool[f, part] = jnp.where(slots == slot, mean, pool_in[r, part])
                ssum[r, part] = jnp.where(slots == slot, total, ssum_in[r, part])
        return carry

    lax.fori_loop(0, 14 // HALO_ROWS, encode_halo, 0)
    fine = m1x[...].reshape(frame * 24, 256) + mm(pool[...].reshape(frame * 24, 256).astype(LOW), weights[2])
    fine = fine.reshape(frame, 24, 256)
    fx[:, 0:16] = fine[:, 0:16].astype(LOW)
    fx[:, 16:32] = jnp.concatenate([fine[:, 16:24], jnp.zeros((frame, 8, 256), WIDE)], 1).astype(LOW)

    edge = iota((128, 128), 0)
    lanes = iota((128, 128), 1)
    up_mask = jnp.where(lanes == edge, 1.0, 0.0)
    up_places = lanes.astype(WIDE)
    up_ones = jnp.ones((128, 128), LOW)
    m2_flat = m2x[...].reshape(a_frame * 16, 256)
    m2_low = m2_flat.astype(LOW)
    up_recv = mm(m2_low, weights[4]).reshape(a_frame, 16, 256)
    pools = []
    for aa in range(a_frame):
        vec = uv[aa]
        picked = (up_mask.reshape(16, 8, 128) * vec[None]).reshape(128, 128).astype(LOW)
        chosen = jnp.where(mm(picked, up_ones) == up_places, 1.0, 0.0).astype(LOW)
        ohu[aa] = chosen
        senders = mm(chosen, fx[2 * aa : 2 * aa + 4].reshape(128, 256)).astype(LOW)
        su[aa] = senders
        pre = mm(senders, weights[3]).reshape(8, 16, 256) + up_recv[aa][None]
        sig = sigmoid_of(pre)
        act = pre * sig
        pools.append(jnp.sum(act, axis=0) * (1.0 / 8))
        uslope[aa] = (sig + act * (1.0 - sig)).reshape(128, 256)
    up_pool = jnp.concatenate(pools, 0).astype(LOW)
    coarse = (m2_flat + mm(up_pool, weights[5])).astype(LOW)

    c_frame = 2 * a_frame
    nodes = a_frame * 16

    def parent_slot(q):
        return jnp.where(q < 16, q // 2, jnp.where((q == 18) | (q == 19), 15, jnp.where((q == 20) | (q == 21), 8, -1)))

    r_i = iota((c_frame * 32, nodes), 0)
    r_j = iota((c_frame * 32, nodes), 1)
    spread = (r_i // 64 == r_j // 16) & (parent_slot(r_i % 32) == r_j % 16)
    spread = jnp.where(spread, 1.0, 0.0).astype(LOW)
    t_i = iota((nodes, c_frame * 32), 1)
    t_j = iota((nodes, c_frame * 32), 0)
    gather = (t_i // 64 == t_j // 16) & (parent_slot(t_i % 32) == t_j % 16)
    gather = jnp.where(gather, 1.0, 0.0).astype(LOW)
    parents = mm(spread, coarse).astype(LOW)
    fine_mid = fx[1 : 1 + c_frame].reshape(c_frame * 32, 256)
    down_pre = mm(parents, weights[6]) + mm(fine_mid, weights[7])
    sig = sigmoid_of(down_pre)
    act = down_pre * sig
    cot_w = mm_nt(cx[...].reshape(c_frame * 32, 256), weights[8])
    dd[0] = (cot_w * (sig + act * (1.0 - sig))).astype(LOW).reshape(c_frame, 32, 256)
    dd[1] = act.astype(LOW).reshape(c_frame, 32, 256)

    def put_grad(index, value):
        acc_s[...] = value
        put_halves(acc_s, keep, send, index - 3, rep)

    act_own = dd[1, pl.ds(c_own, 16), 0:16].reshape(256, 256)
    delta_own = dd[0, pl.ds(c_own, 16), 0:16].reshape(256, 256)
    fine_own = fx[pl.ds(f_own, 16), 0:16].reshape(256, 256)
    cot_own = cot[...].reshape(256, 256)
    out = fine_own.astype(WIDE) + mm(act_own, weights[8])
    mesh_out[...] = out.astype(LOW).reshape(16, 16, 256)
    put_grad(8, mm_tn(act_own, cot_own))
    put_grad(7, mm_tn(fine_own, delta_own))

    child_sum = mm(gather, dd[0].reshape(c_frame * 32, 256))
    n_i = iota((nodes, 256), 0)
    aa_i, bb_i = n_i // 16, n_i % 16
    is_own = (aa_i >= a_own) & (aa_i < a_own + 8) & (bb_i < 8)
    is_real = (bb_i <= 8) | (bb_i == 15)
    if n_lat != 2:
        above = lat * 8 - 1 + aa_i
        is_real = is_real & (above >= 0) & (above < n_lat * 8)
    sum_high, sum_low = two_parts(child_sum)
    coarse_delta = (mm_nt(sum_high, weights[6]) + mm_nt(sum_low, weights[6])).astype(LOW)
    own_high, own_low = two_parts(jnp.where(is_own, child_sum, 0.0))
    put_grad(6, mm_tn(coarse, own_high) + mm_tn(coarse, own_low))
    own_delta = jnp.where(is_own, coarse_delta.astype(WIDE), 0.0).astype(LOW)
    put_grad(5, mm_tn(up_pool, own_delta))
    pool2 = jnp.where(is_real, mm_nt(coarse_delta, weights[5]) * (1.0 / 8), 0.0)
    own_f = jnp.where(is_own, 1.0, 0.0)
    recv[...] = jnp.zeros_like(recv)
    acc_s[...] = jnp.zeros_like(acc_s)
    node_sums = []
    for aa in range(a_frame):
        d = pool2[aa * 16 : aa * 16 + 16][None] * uslope[aa].reshape(8, 16, 256)
        mine = own_f[aa * 16 : aa * 16 + 16][None]
        up_delta = d.astype(LOW)
        wide = up_delta.astype(WIDE)
        owned = wide * mine
        node_sums.append(jnp.sum(owned, axis=0))
        back = mm_tn(ohu[aa], up_delta.reshape(128, 256)).reshape(4, 32, 256)
        recv[2 * aa : 2 * aa + 4] += back[:, 0:24]
        acc_s[...] += mm_tn(su[aa], owned.reshape(128, 256).astype(LOW))
    put_grad(3, acc_s[...])
    ns_high, ns_low = two_parts(jnp.concatenate(node_sums, 0))
    put_grad(4, mm_tn(m2_low, ns_high) + mm_tn(m2_low, ns_low))
    back_high, back_low = two_parts(recv[pl.ds(f_own, 16), 0:16].reshape(256, 256))
    fine_delta = (
        cot_own.astype(WIDE)
        + mm_nt(delta_own, weights[7])
        + mm_nt(back_high, weights[3])
        + mm_nt(back_low, weights[3])
    )
    fd_out[...] = fine_delta
    pool_out[...] = pool[pl.ds(f_own, 16), 0:16].reshape(256, 256).astype(LOW)


def back_kernel(
    m1, weights, fine_delta, pool, ssum, sx_in, slope_in, sx_edge, slope_edge, hx, hslope, mesh1_grad, keep, send, pd, acc
):
    rep = lax.axis_index("rep")
    delta_b = fine_delta[...].astype(LOW)
    pool_delta = mm_nt(delta_b, weights[2]) * (1.0 / 16)
    pd[...] = pool_delta.reshape(16, 16, 256)
    node_delta = pool_delta * ssum[0:16].reshape(256, 256)
    high, low = two_parts(node_delta)
    m1_own = m1[...].reshape(256, 256)
    grad_in = fine_delta[...] + (mm_nt(high, weights[1]) + mm_nt(low, weights[1]))
    mesh1_grad[...] = grad_in.astype(LOW).reshape(16, 16, 256)
    acc[...] = mm_tn(pool[...], delta_b)
    put_halves(acc, keep, send, 2, rep)
    acc[...] = mm_tn(m1_own, high) + mm_tn(m1_own, low)
    put_halves(acc, keep, send, 1, rep)

    def deltas_of(r, tile, rise):
        d = pd[r, tile * 8 : tile * 8 + 8][None] * rise.reshape(16, 8, 256)
        return d.reshape(128, 256).astype(LOW)

    senders, deltas = [], []
    for i, r in enumerate((0, 15)):
        senders.append(sx_edge[i].reshape(256, 256))
        for tile in range(2):
            deltas.append(deltas_of(r, tile, slope_edge[i, tile].astype(WIDE)))
    acc[...] = mm_tn(jnp.concatenate(senders, 0), jnp.concatenate(deltas, 0))
    slots = iota((128, 256), 0) % 8

    def rows(step, carry):
        senders, deltas = [], []
        for k in range(2):
            r = 1 + 2 * step + k
            halo = hx[r - 1].astype(WIDE)
            halo_rise = hslope[r - 1].astype(WIDE)
            for tile, slot in ((0, 0), (1, 7)):
                ours = slots == slot
                senders.append(jnp.where(ours, halo, sx_in[r, tile].astype(WIDE)).astype(LOW))
                deltas.append(deltas_of(r, tile, jnp.where(ours, halo_rise, slope_in[r, tile].astype(WIDE))))
        acc[...] += mm_tn(jnp.concatenate(senders, 0), jnp.concatenate(deltas, 0))
        return carry

    lax.fori_loop(0, 7, rows, 0)
    put_halves(acc, keep, send, 0, rep)


def spread_kernel(first, scale, *refs):
    mine, theirs = refs[:4], refs[4:8]
    out, stage, sem = refs[-3:]
    count = stage.shape[0]
    rep = lax.axis_index("rep")
    place = (lax.axis_index("lat") % 2) * 2 + lax.axis_index("lon") % 2
    for step in range(4):
        at = (place ^ step) * 32
        for half, pieces in ((rep, mine), (1 - rep, theirs)):
            rows = pl.ds(pl.multiple_of(half * 128 + at, 32), 32)
            stage[:, rows, :] = pieces[step][...].astype(WIDE) * scale
    copy = pltpu.make_async_copy(stage, out.at[first : first + count], sem)
    copy.start()
    copy.wait()


def flat_main(dirs, n_lat, *refs):
    n_bands = 3 * len(dirs)
    own, refs = refs[:7], refs[7:]
    sides, refs = refs[:2], refs[2:]
    bands, refs = refs[:n_bands], refs[n_bands:]
    weights, refs = refs[0], refs[1:]
    outs, scratch = refs[:10], refs[10:]
    main_kernel(dirs, n_lat, own, sides, bands, weights, outs, scratch)


def sum_over_slice(kept, sent, mesh, then=None):
    lat_size, lon_size = mesh.shape["lat"], mesh.shape["lon"]
    rep = lax.axis_index("rep")
    lat, lon = lax.axis_index("lat"), lax.axis_index("lon")
    place = (lat % 2) * 2 + lon % 2

    def between(values, lon_bit, lat_bit):
        return permute(
            values,
            ("lon", "lat"),
            lambda i: ((i // lat_size) ^ lon_bit) * lat_size + ((i % lat_size) ^ lat_bit),
            (lon_size, lat_size),
        )

    def siblings(values):
        return permute(values, "rep", lambda i: i ^ 1, (2,))

    half = kept + siblings(sent).astype(WIDE)
    if then is not None:
        half, value = lax.optimization_barrier((half, then))
    count, rows, cols = half.shape
    quarters = half.reshape(count, 4, rows // 4, cols)
    total = lax.dynamic_index_in_dim(quarters, place, 1, keepdims=False)
    for step in (1, 2, 3):
        piece = lax.dynamic_index_in_dim(quarters, place ^ step, 1, keepdims=False).astype(LOW)
        total = total + between(piece, step & 1, step >> 1).astype(WIDE)
    bit = 2
    while bit < lon_size:
        rounded = total.astype(LOW)
        total = rounded.astype(WIDE) + between(rounded, bit, 0).astype(WIDE)
        bit *= 2
    bit = 2
    while bit < lat_size:
        rounded = total.astype(LOW)
        total = rounded.astype(WIDE) + between(rounded, 0, bit).astype(WIDE)
        bit *= 2
    own = total.astype(LOW)
    pieces = [own] + [between(own, step & 1, step >> 1) for step in (1, 2, 3)]
    pieces = pieces + [siblings(piece) for piece in pieces]
    return pieces if then is None else (pieces, value)


def body(mesh, grid_state, mesh1_state, mesh2_state, grid_edges, up_edges, weights, cotangent):
    n_lat, n_lon = mesh.shape["lat"], mesh.shape["lon"]
    glon = grid_state.shape[1] * 2 * n_lon
    m1lon = mesh1_state.shape[1] * 2 * n_lon
    dirs = (None,) if n_lat == 2 else (True, False)
    vmem = pl.BlockSpec(memory_space=pltpu.VMEM)
    params = pltpu.CompilerParams(vmem_limit_bytes=VMEM_BYTES)
    shapes = [48] + [SIDE_ROWS] * 2 + [BAND_ROWS, CORNER_ROWS, CORNER_ROWS] * len(dirs)
    hbm = pl.BlockSpec(memory_space=pltpu.HBM)
    states = (grid_state, mesh1_state, cotangent, mesh2_state)
    grid_state, mesh1_state, cotangent, mesh2_state, codes, *buffers = pl.pallas_call(
        functools.partial(pack_kernel, dirs, glon, m1lon),
        out_shape=[jax.ShapeDtypeStruct(state.shape, state.dtype) for state in states]
        + [jax.ShapeDtypeStruct((n, 256), LOW) for n in shapes],
        in_specs=[hbm] * 6,
        out_specs=[vmem] * (4 + len(shapes)),
        scratch_shapes=[
            pltpu.VMEM(grid_edges.shape, grid_edges.dtype),
            pltpu.VMEM(up_edges.shape, up_edges.dtype),
            pltpu.SemaphoreType.DMA((6,)),
        ],
        compiler_params=params,
        name="pack_halos",
    )(*(in_hbm(value) for value in (*states, grid_edges, up_edges)))
    inner = pl.pallas_call(
        inner_kernel,
        out_shape=[
            jax.ShapeDtypeStruct((16, 2, 128, 256), LOW),
            jax.ShapeDtypeStruct((16, 2, 128, 256), LOW),
            jax.ShapeDtypeStruct((16, 16, 256), WIDE),
            jax.ShapeDtypeStruct((16, 16, 256), WIDE),
            jax.ShapeDtypeStruct(weights.shape, LOW),
        ],
        in_specs=[vmem] * 3 + [hbm],
        out_specs=[vmem] * 5,
        scratch_shapes=[
            pltpu.VMEM((3, 34, 16, 256), LOW),
            pltpu.VMEM((3, 128, 256), LOW),
            pltpu.VMEM((16, 16, 256), LOW),
            pltpu.VMEM((16, 16, 256), WIDE),
            pltpu.SemaphoreType.DMA((2,)),
        ],
        compiler_params=params,
        cost_estimate=pl.CostEstimate(flops=4_000_000_000, bytes_accessed=8_000_000, transcendentals=1_000_000),
        name="inner_rows",
    )(grid_state, mesh1_state, codes, in_hbm(weights))
    sx_in, slope_in, pool_in, ssum_in, weights = inner
    own = (grid_state, mesh1_state, cotangent, mesh2_state, codes, pool_in, ssum_in)

    def beyond(lon, core):
        return ((lon + (1 if core else -1)) % n_lon, 1 - core)

    def send_to(values, other_lat, column):
        def partner(i):
            lon, rest = divmod(i, n_lat * 2)
            row, core = divmod(rest, 2)
            row = other_lat(row)
            if row is None:
                return None
            if column == "sibling":
                core = 1 - core
            elif column == "beyond":
                lon, core = beyond(lon, core)
            return (lon * n_lat + row) * 2 + core

        return permute(values, ("lon", "lat", "rep"), partner, (n_lon, n_lat, 2))

    def shift(sends_bottom):
        if sends_bottom is None:
            return lambda row: row ^ 1
        if sends_bottom:
            return lambda row: row + 1 if row + 1 < n_lat else None
        return lambda row: row - 1 if row else None

    got_sides = [send_to(buffers[0], lambda row: row, "sibling"), send_to(buffers[1], lambda row: row, "beyond")]
    got_bands = []
    for i, sends_bottom in enumerate(dirs):
        for k, column in enumerate(("same", "sibling", "beyond")):
            got_bands.append(send_to(buffers[2 + 3 * i + k], shift(sends_bottom), column))

    frame = 20 if n_lat == 2 else 22
    a_frame = 9 if n_lat == 2 else 10
    c_frame = 2 * a_frame
    g_frame = 2 * frame + 6
    scratch = [
        pltpu.VMEM((3, g_frame, 16, 256), LOW),
        pltpu.VMEM((frame, 24, 256), WIDE),
        pltpu.VMEM((frame, 24, 256), WIDE),
        pltpu.VMEM((frame, 16, 256), LOW),
        pltpu.VMEM((frame, 16, 256), LOW),
        pltpu.VMEM((a_frame, 8, 128), WIDE),
        pltpu.VMEM((frame, 24, 256), WIDE),
        pltpu.VMEM((frame, 32, 256), LOW),
        pltpu.VMEM((c_frame, 32, 256), LOW),
        pltpu.VMEM((a_frame, 16, 256), WIDE),
        pltpu.VMEM((a_frame, 128, 128), LOW),
        pltpu.VMEM((a_frame, 128, 256), LOW),
        pltpu.VMEM((a_frame, 128, 256), WIDE),
        pltpu.VMEM((2, c_frame, 32, 256), LOW),
        pltpu.VMEM((256, 256), WIDE),
        pltpu.VMEM((3, 128, 256), LOW),
    ]
    n_in = 7 + 2 + len(got_bands) + 1
    mesh_out, kept, sent, fine_delta, pool, ssum, sx_edge, slope_edge, hx, hslope = pl.pallas_call(
        functools.partial(flat_main, dirs, n_lat),
        out_shape=[
            jax.ShapeDtypeStruct(mesh1_state.shape, LOW),
            jax.ShapeDtypeStruct((6, 128, 256), WIDE),
            jax.ShapeDtypeStruct((6, 128, 256), LOW),
            jax.ShapeDtypeStruct((256, 256), WIDE),
            jax.ShapeDtypeStruct((256, 256), LOW),
            jax.ShapeDtypeStruct((17, 16, 256), WIDE),
            jax.ShapeDtypeStruct((3, 2, 128, 256), LOW),
            jax.ShapeDtypeStruct((3, 2, 128, 256), LOW),
            jax.ShapeDtypeStruct((14, 128, 256), LOW),
            jax.ShapeDtypeStruct((14, 128, 256), LOW),
        ],
        in_specs=[vmem] * n_in,
        out_specs=[vmem] * 10,
        scratch_shapes=scratch,
        compiler_params=params,
        name="sweep",
    )(*own, *got_sides, *got_bands, weights)
    pieces, fine_delta = sum_over_slice(kept, sent, mesh, fine_delta)
    mesh1_grad, kept_first, sent_first = pl.pallas_call(
        back_kernel,
        out_shape=[
            jax.ShapeDtypeStruct(mesh1_state.shape, LOW),
            jax.ShapeDtypeStruct((3, 128, 256), WIDE),
            jax.ShapeDtypeStruct((3, 128, 256), LOW),
        ],
        in_specs=[vmem] * 11,
        out_specs=[vmem] * 3,
        scratch_shapes=[pltpu.VMEM((16, 16, 256), WIDE), pltpu.VMEM((256, 256), WIDE)],
        compiler_params=params,
        cost_estimate=pl.CostEstimate(flops=3_000_000_000, bytes_accessed=8_000_000, transcendentals=0),
        name="encoder_back",
    )(mesh1_state, weights, fine_delta, pool, ssum, sx_in, slope_in, sx_edge, slope_edge, hx, hslope)
    node_total = mesh1_state.shape[0] * mesh1_state.shape[1] * n_lat * n_lon * 2
    scale = float(node_total) ** (-0.5)
    pieces_first = sum_over_slice(kept_first, sent_first, mesh)

    def spread(pieces, first, before):
        count = pieces[0].shape[0]
        more = [] if before is None else [before]
        return pl.pallas_call(
            functools.partial(spread_kernel, first, scale),
            out_shape=jax.ShapeDtypeStruct((9, 256, 256), WIDE),
            in_specs=[vmem] * 8 + [hbm] * len(more),
            out_specs=hbm,
            scratch_shapes=[pltpu.VMEM((count, 256, 256), WIDE), pltpu.SemaphoreType.DMA],
            input_output_aliases={8: 0} if more else {},
            compiler_params=params,
            name="spread_%d" % first,
        )(*pieces, *more)

    weight_grads = spread(pieces_first, 0, spread(pieces, 3, None))
    return (mesh_out, mesh1_grad, weight_grads)


def solution(mesh):
    in_specs = (
        P(("groups", "lat"), ("lon", "rep"), None),
        P(("groups", "lat"), ("lon", "rep"), None),
        P(("groups", "lat"), "lon", None),
        P(None, "lat", ("lon", "rep")),
        P(None, "lat", "lon"),
        P(),
        P(("groups", "lat"), ("lon", "rep"), None),
    )
    out_specs = (
        P(("groups", "lat"), ("lon", "rep"), None),
        P(("groups", "lat"), ("lon", "rep"), None),
        P("groups", None, None),
    )
    return jax.shard_map(
        functools.partial(body, mesh), mesh=mesh, in_specs=in_specs, out_specs=out_specs, check_vma=False
    )
```

```python
import functools

import jax
import jax.numpy as jnp
from jax import lax
from jax.experimental import pallas as pl
from jax.experimental.pallas import tpu as pltpu
from jax.sharding import PartitionSpec as P

LOW = jnp.bfloat16
WIDE = jnp.float32
VMEM_BYTES = 24 * 1024 * 1024
HALO_ROWS = 7

SIDE_ROWS = 416
BAND_ROWS = 352
CORNER_ROWS = 112


def permute(values, axes, partner, sizes):
    total = 1
    for size in sizes:
        total *= size
    pairs = [(i, partner(i)) for i in range(total)]
    return lax.ppermute(values, axes, [(i, j) for i, j in pairs if j is not None])


def mm(left, right):
    return jnp.dot(left, right, preferred_element_type=WIDE)


def mm_nt(left, right):
    return lax.dot_general(left, right, (((1,), (1,)), ((), ())), preferred_element_type=WIDE)


def mm_tn(left, right):
    return lax.dot_general(left, right, (((0,), (0,)), ((), ())), preferred_element_type=WIDE)


def two_parts(value):
    high = value.astype(LOW)
    return high, (value - high.astype(WIDE)).astype(LOW)


def sigmoid_of(value):
    return 0.5 * jnp.tanh(0.5 * value) + 0.5


def iota(shape, dim):
    return lax.broadcasted_iota(jnp.int32, shape, dim)


def in_hbm(value):
    return pltpu.with_memory_space_constraint(value, pltpu.HBM)


def split(value, size):
    if size & (size - 1) == 0:
        return value >> (size.bit_length() - 1), value & (size - 1)
    return value // size, value % size


def wrapped(value, size):
    if size & (size - 1) == 0:
        return value & (size - 1)
    return jnp.mod(value, size)


def edge_codes(edges, glon, lat, col, rows, cols):
    row = iota(edges.shape, 0)
    lane = iota(edges.shape, 1)
    j = lane % 16
    at_row, at_col = split(edges, glon)
    down = at_row - (2 * (lat * rows + row) - 2)
    across = wrapped(at_col - (2 * (col * cols + j) - 2), glon)
    place = 2 * (j % 8) + 6 + across
    own = down * 16 + place + jnp.where(place >= 16, 112, 0)
    base = down * 16 + across + 6
    turned = jnp.where(j < 4, pltpu.roll(base, 256 - 12, 1), pltpu.roll(base, 4, 1))
    sent = turned + 2 * (j - 4) + jnp.where(j < 4, 0, 128)
    return own.astype(WIDE), sent.astype(WIDE)


def up_codes(edges, m1lon, lat, col, rep, rows, cols):
    row = iota(edges.shape, 0)
    l16 = iota(edges.shape, 1) % 16
    low = jnp.where(l16 < 8, edges, pltpu.roll(edges, 8, 1))
    high = jnp.where(l16 < 8, pltpu.roll(edges, 128 - 8, 1), edges)
    edges = jnp.where(rep == 0, low, high)
    b = l16 % 8
    at_row, at_col = split(edges, m1lon)
    down = at_row - (2 * (lat * rows + row) - 1)
    across = wrapped(at_col - (2 * (col * cols + b) - 1), m1lon)
    base = jnp.where(l16 < 8, b, jnp.where(b >= 4, b - 8, b + 8))
    at = 2 * base - 1 + across
    at = jnp.where(at < 0, at + 20, jnp.where(at >= 16, at + 4, at))
    return (down * 32 + at).astype(WIDE)


def pack_kernel(dirs, glon, m1lon, *refs):
    far, (grid, m1, cot, m2, codes), rest = refs[:6], refs[6:11], refs[11:]
    outs, (edges, ups, sems) = rest[:-3], rest[-3:]
    copies = [
        pltpu.make_async_copy(a, b, sems.at[i]) for i, (a, b) in enumerate(zip(far, (grid, m1, cot, m2, edges, ups)))
    ]
    for copy in copies:
        copy.start()
    for copy in copies[::-1]:
        copy.wait()
    rep = lax.axis_index("rep")
    lat = lax.axis_index("lat")
    col = lax.axis_index("lon") * 2 + rep
    sides = outs[:2]
    bands = outs[2:]
    flat = jnp.concatenate([edges[k] for k in range(16)], axis=1)
    own_k, sent_k = edge_codes(flat, glon, lat, col, 16, 16)
    flat = jnp.concatenate([ups[k] for k in range(8)], axis=1)
    up_k = up_codes(flat, m1lon, lat, col, rep, 8, 8)
    up_k = jnp.concatenate([up_k, jnp.zeros_like(up_k)], 1)
    codes[0:16, :] = own_k.astype(LOW)
    codes[16:32, :] = sent_k.astype(LOW)
    codes[32:48, :] = jnp.concatenate([up_k, jnp.zeros_like(up_k)], 0).astype(LOW)
    m2w = m2[...].astype(WIDE)
    m2_half = jnp.where(rep == 0, m2w[:, 0:8], m2w[:, 8:16])
    row8 = iota((8, 256), 0)

    def few(k_rows, last, ghost):
        up = jnp.where(last, up_k[7:8], up_k[0:1])
        rest = jnp.where(row8 == 3, jnp.broadcast_to(up, (8, 256)), 0.0)
        if ghost is not None:
            rest = jnp.where(row8 == 4, jnp.broadcast_to(ghost, (8, 256)), rest)
        return jnp.where(last, jnp.where(row8 >= 5, k_rows[8:16], rest), jnp.where(row8 < 3, k_rows[0:8], rest))

    def last_rows(sends_bottom):
        if sends_bottom is None:
            return lat == 0
        return jnp.bool_(sends_bottom)

    def fill(targets, right):
        side, corners = targets
        g = grid[:, 16:32, :] if right else grid[:, 0:16, :]
        g = g.astype(WIDE)[:, 8:16] if right else g.astype(WIDE)[:, 0:8]
        part = slice(12, 16) if right else slice(0, 4)
        pair = jnp.concatenate([m1[...].astype(WIDE)[:, part], cot[...].astype(WIDE)[:, part]], axis=1)
        edge = 7 if right else 0
        ghosts = jnp.zeros((8, 256), WIDE)
        for a in range(8):
            ghosts = jnp.where(row8 == a, jnp.broadcast_to(m2_half[a, edge : edge + 1], (8, 256)), ghosts)
        side[0:256, :] = g.reshape(256, 256).astype(LOW)
        side[256:384, :] = pair.reshape(128, 256).astype(LOW)
        side[384:400, :] = sent_k.astype(LOW)
        side[400:416, :] = jnp.concatenate([up_k, ghosts], 0).astype(LOW)
        for sends_bottom, corner in corners:
            last = last_rows(sends_bottom)
            corner[0:64, :] = jnp.where(last, g[24:32], g[0:8]).reshape(64, 256).astype(LOW)
            corner[64:96, :] = jnp.where(last, pair[12:16], pair[0:4]).reshape(32, 256).astype(LOW)
            block = few(sent_k, last, jnp.where(last, ghosts[7:8], ghosts[0:1]))
            corner[96:112, :] = jnp.concatenate([block, block], 0).astype(LOW)

    sib = (sides[0], [(d, bands[3 * i + 1]) for i, d in enumerate(dirs)])
    out = (sides[1], [(d, bands[3 * i + 2]) for i, d in enumerate(dirs)])

    @pl.when(rep == 0)
    def _():
        fill(sib, True)
        fill(out, False)

    @pl.when(rep == 1)
    def _():
        fill(sib, False)
        fill(out, True)

    for i, sends_bottom in enumerate(dirs):
        band = bands[3 * i]
        last = last_rows(sends_bottom)
        first = jnp.where(last, 1, 0)
        band[0:256, :] = grid[pl.ds(first * 24, 8)].reshape(256, 256)
        band[256:304, :] = m1[pl.ds(first * 13, 3)].reshape(48, 256)
        band[304:336, :] = cot[pl.ds(first * 14, 2)].reshape(32, 256)
        mt = jnp.where(last, m2_half[7], m2_half[0])
        band[336:352, :] = jnp.concatenate([few(own_k, last, None), mt], 0).astype(LOW)


def set_masks(masks):
    edge = iota((128, 256), 0)
    lanes = iota((128, 256), 1)
    slot = edge % 8
    base = (edge // 8) * 16
    masks[0] = jnp.where(lanes == base + slot, 1.0, 0.0).astype(LOW)
    masks[1] = jnp.where(lanes == base + 8 + slot, 1.0, 0.0).astype(LOW)
    masks[2] = jnp.where(lanes == base + jnp.where(slot < 7, slot, 15), 1.0, 0.0).astype(LOW)


def encode_tiles(tiles, weight):
    count = len(tiles)
    ones = jnp.ones((256, 256), LOW)
    places = iota((128, 256), 1).astype(WIDE)
    picked = [(mask.reshape(8, 16, 256) * codes[None]).reshape(128, 256) for mask, codes, _, _ in tiles]
    found = mm(jnp.concatenate(picked, 0), ones)
    senders = []
    for i, (_, _, window, _) in enumerate(tiles):
        chosen = jnp.where(found[i * 128 : i * 128 + 128] == places, 1.0, 0.0).astype(LOW)
        senders.append(mm(chosen, jnp.concatenate(window, 0)).astype(LOW))
    pre_all = mm(jnp.concatenate(senders, 0), weight)
    results = []
    for i in range(count):
        pre = pre_all[i * 128 : i * 128 + 128].reshape(16, 8, 256) + tiles[i][3][None]
        sig = sigmoid_of(pre)
        act = pre * sig
        rise = sig + act * (1.0 - sig)
        results.append(
            (senders[i], jnp.sum(act, axis=0) * (1.0 / 16), rise.reshape(128, 256).astype(LOW), jnp.sum(rise, axis=0))
        )
    return results


BLOCKS = ((0, 1), (1, 2), (0, 2))


def inner_kernel(grid, m1, codes, far, sx, slope, pool, ssum, weights, gx, masks, ko, recv, sems):
    first = pltpu.make_async_copy(far.at[0:2], weights.at[0:2], sems.at[0])
    others = pltpu.make_async_copy(far.at[2:9], weights.at[2:9], sems.at[1])
    first.start()
    others.start()
    set_masks(masks)

    def place_grid(step, carry):
        r = step * 8
        wide = grid[pl.ds(r, 8)].astype(WIDE)
        edge = jnp.zeros((8, 8, 256), WIDE)
        gx[0, pl.ds(r, 8)] = jnp.concatenate([edge, wide[:, 0:8]], 1).astype(LOW)
        gx[1, pl.ds(r, 8)] = wide[:, 8:24].astype(LOW)
        gx[2, pl.ds(r, 8)] = jnp.concatenate([wide[:, 24:32], edge], 1).astype(LOW)
        return carry

    lax.fori_loop(0, 4, place_grid, 0)
    gx[:, 32:34] = jnp.zeros((3, 2, 16, 256), LOW)
    own = codes[0:16, :].astype(WIDE)
    for r in range(16):
        ko[r] = jnp.broadcast_to(own[r : r + 1], (16, 256)).astype(LOW)
    first.wait()
    recv[...] = mm(m1[...].reshape(256, 256), weights[1]).reshape(16, 16, 256)

    def rows(step, carry):
        tiles = []
        for k in range(2):
            r = 1 + 2 * step + k
            for tile in range(2):
                window = [gx[blk, pl.ds(2 * r - 2, 8)].reshape(128, 256) for blk in BLOCKS[tile]]
                tiles.append((masks[tile], ko[r], window, recv[r, tile * 8 : tile * 8 + 8]))
        done = encode_tiles(tiles, weights[0])
        for k in range(2):
            r = 1 + 2 * step + k
            for tile in range(2):
                senders, mean, rise, total = done[2 * k + tile]
                sx[r, tile] = senders
                slope[r, tile] = rise
                pool[r, tile * 8 : tile * 8 + 8] = mean
                ssum[r, tile * 8 : tile * 8 + 8] = total
        return carry

    lax.fori_loop(0, 7, rows, 0)
    others.wait()


def put_halves(grad, keep, send, index, rep):
    keep[index] = grad[pl.ds(pl.multiple_of(rep * 128, 128), 128), :]
    send[index] = grad[pl.ds(pl.multiple_of((1 - rep) * 128, 128), 128), :].astype(LOW)


def main_kernel(
    dirs, n_lat, own, sides, bands, weights, outs, scratch
):
    grid, m1, cot, m2, codes, pool_in, ssum_in = own
    mesh_out, keep, send, fd_out, pool_out, ssum, sx, slope, hx, hslope = outs
    gx, m1x, recv, ko, k2, uv, pool, fx, cx, m2x, ohu, su, uslope, dd, acc_s, masks = scratch
    rep = lax.axis_index("rep")
    lat = lax.axis_index("lat")
    frame = m1x.shape[0]
    a_frame = m2x.shape[0]
    if n_lat == 2:
        g_own, f_own, c_own, a_own = 4 + 4 * lat, 1 + 2 * lat, 2 * lat, lat
        odd_rows = 5
        odd_row = lambda i: jnp.where(lat == 0, jnp.where(i == 0, 1, 15 + i), jnp.where(i < 4, i, 18))
    else:
        g_own, f_own, c_own, a_own = 8, 3, 2, 1
        odd_rows = 8
        odd_row = lambda i: jnp.where(i < 4, i, 14 + i)

    def left_right(sib, out):
        return jnp.where(rep == 1, sib, out), jnp.where(rep == 1, out, sib)

    zero_rows = jnp.zeros((4, 16, 256), LOW)
    for blk in range(3):
        gx[blk, 0:4] = zero_rows
        gx[blk, gx.shape[1] - 6 : gx.shape[1] - 2] = zero_rows
        gx[blk, gx.shape[1] - 4 :] = zero_rows

    def put_grid(at, mid, sib, out):
        n = mid.shape[0]
        left, right = left_right(sib.astype(WIDE), out.astype(WIDE))
        left = left.reshape(n, 8, 256)
        right = right.reshape(n, 8, 256)
        wide = mid.astype(WIDE)
        gx[0, pl.ds(at, n)] = jnp.concatenate([left, wide[:, 0:8]], 1).astype(LOW)
        gx[1, pl.ds(at, n)] = wide[:, 8:24].astype(LOW)
        gx[2, pl.ds(at, n)] = jnp.concatenate([wide[:, 24:32], right], 1).astype(LOW)

    def own_grid(step, carry):
        r = step * 8
        r8 = pl.multiple_of(step * 64, 64)
        put_grid(g_own + r, grid[pl.ds(r, 8)], sides[0][pl.ds(r8, 64), :], sides[1][pl.ds(r8, 64), :])
        return carry

    lax.fori_loop(0, 4, own_grid, 0)

    def put_fine(sib, out, n, mid):
        left, right = left_right(sib.astype(WIDE), out.astype(WIDE))
        left = left.reshape(n, 8, 256)
        right = right.reshape(n, 8, 256)
        slot = iota((n, 8, 256), 1)
        states = jnp.concatenate([left[:, 0:4], right[:, 0:4]], 1)
        states = jnp.where(slot == 0, mid[:, 0:8], jnp.where(slot == 7, mid[:, 8:16], states))
        cots = jnp.concatenate([left[:, 4:8], right[:, 4:8]], 1)
        return states, cots

    m1x[...] = jnp.zeros_like(m1x)
    cx[...] = jnp.zeros_like(cx)
    m1_wide = m1[...].astype(WIDE)
    states, cots = put_fine(sides[0][256:384, :], sides[1][256:384, :], 16, m1_wide)
    m1x[pl.ds(f_own, 16), 0:16] = m1_wide
    m1x[pl.ds(f_own, 16), 16:24] = states
    cx[pl.ds(c_own, 16), 0:16] = cot[...]
    cx[pl.ds(c_own, 16), 16:32] = jnp.concatenate([cots, jnp.zeros_like(cots)], 1).astype(LOW)

    def put_m2(at, mid, sib, out, n):
        left, right = left_right(sib, out)
        slot = iota((8, 256), 0)
        for a in range(n):
            l_a = jnp.broadcast_to(left[a : a + 1], (8, 256))
            r_a = jnp.broadcast_to(right[a : a + 1], (8, 256))
            ghost = jnp.where(slot == 7, l_a, jnp.where(slot == 0, r_a, 0.0))
            m2x[at + a] = jnp.concatenate([mid[a], ghost], 0)

    m2w = m2[...].astype(WIDE)
    m2_half = jnp.where(rep == 0, m2w[:, 0:8], m2w[:, 8:16])
    side_few = [side[384:416, :].astype(WIDE) for side in sides]
    put_m2(a_own, m2_half, side_few[0][24:32], side_few[1][24:32], 8)

    def codes_of(mid, sib, out):
        left, right = left_right(sib, out)
        l16 = iota(mid.shape, 1) % 16
        return jnp.where((l16 == 0) | (l16 == 15), mid, jnp.where(l16 < 4, left, right))

    def ups_of(mid, sib, out):
        left, right = left_right(sib, out)
        l16 = iota(mid.shape, 1) % 16
        return jnp.where(l16 < 8, mid, jnp.where(l16 < 12, right, left))[:, 0:128]

    def put_codes(f_at, a_at, own_rows, halo_rows, up_rows):
        for r in range(own_rows.shape[0]):
            ko[f_at + r] = jnp.broadcast_to(own_rows[r : r + 1], (16, 256)).astype(LOW)
            k2[f_at + r] = jnp.broadcast_to(halo_rows[r : r + 1], (16, 256)).astype(LOW)
        for r in range(up_rows.shape[0]):
            uv[a_at + r] = jnp.broadcast_to(up_rows[r : r + 1], (8, 128))

    own_codes = codes[...].astype(WIDE)
    put_codes(
        f_own, a_own, own_codes[0:16],
        codes_of(own_codes[0:16], side_few[0][0:16], side_few[1][0:16]),
        ups_of(own_codes[32:40], side_few[0][16:24], side_few[1][16:24]),
    )
    for i, sends_bottom in enumerate(dirs):
        band, corner_sib, corner_out = bands[3 * i : 3 * i + 3]
        if sends_bottom is None:
            top = lat
        else:
            top = 1 if sends_bottom else 0
        below = 1 - top
        put_grid(
            below * (g_own + 32), band[0:256, :].reshape(8, 32, 256), corner_sib[0:64, :], corner_out[0:64, :]
        )
        is_top = top == 1
        mids = band[256:304, :].astype(WIDE).reshape(3, 16, 256)
        mids4 = jnp.where(is_top, jnp.concatenate([mids[0:1], mids], 0), jnp.concatenate([mids, mids[2:3]], 0))
        states, cots = put_fine(corner_sib[64:96, :], corner_out[64:96, :], 4, mids4)
        f_at = below * (f_own + 16)
        c_at = below * (c_own + 16)
        a_at = below * (a_own + 8)
        m1x[pl.ds(f_at, 3), 0:16] = mids
        m1x[pl.ds(f_at, 3), 16:24] = jnp.where(is_top, states[1:4], states[0:3])
        cx[pl.ds(c_at, 2), 0:16] = band[304:336, :].reshape(2, 16, 256)
        cots = jnp.where(is_top, cots[2:4], cots[0:2])
        cx[pl.ds(c_at, 2), 16:32] = jnp.concatenate([cots, jnp.zeros_like(cots)], 1).astype(LOW)
        band_few = band[336:352, :].astype(WIDE)
        sib_few = corner_sib[96:112, :].astype(WIDE)[0:8]
        out_few = corner_out[96:112, :].astype(WIDE)[0:8]
        put_m2(a_at, band_few[8:16].reshape(1, 8, 256), sib_few[4:5], out_few[4:5], 1)
        own_k = band_few[0:8]
        halo_k = codes_of(own_k, sib_few, out_few)
        up_k = ups_of(own_k, sib_few, out_few)
        put_codes(
            f_at, a_at,
            jnp.where(is_top, own_k[5:8], own_k[0:3]),
            jnp.where(is_top, halo_k[5:8], halo_k[0:3]),
            up_k[3:4],
        )

    set_masks(masks)
    recv[...] = mm(m1x[...].reshape(frame * 24, 256).astype(LOW), weights[1]).reshape(frame, 24, 256)
    pool[...] = jnp.zeros_like(pool)

    def window_of(f, tile):
        return [gx[blk, pl.ds(2 * f, 8)].reshape(128, 256) for blk in BLOCKS[tile]]

    def encode_row(i, carry):
        f = odd_row(i)
        tiles = []
        for tile in range(3):
            vec = ko[f] if tile < 2 else k2[f]
            tiles.append((masks[tile], vec, window_of(f, tile), recv[f, tile * 8 : tile * 8 + 8]))
        done = encode_tiles(tiles, weights[0])
        row = f - f_own
        kept_at = jnp.where(row == 0, 0, jnp.where(row == 15, 1, 2))
        row = jnp.where(kept_at == 2, 16, row)
        for tile in range(3):
            senders, mean, rise, total = done[tile]
            pool[f, tile * 8 : tile * 8 + 8] = mean
            if tile < 2:
                sx[kept_at, tile] = senders
                slope[kept_at, tile] = rise
                ssum[row, tile * 8 : tile * 8 + 8] = total
        return carry

    lax.fori_loop(0, odd_rows, encode_row, 0)
    slots = iota((8, 256), 0)

    def encode_halo(step, carry):
        tiles = []
        for k in range(HALO_ROWS):
            f = f_own + 1 + HALO_ROWS * step + k
            tiles.append((masks[2], k2[f], window_of(f, 2), recv[f, 16:24]))
        done = encode_tiles(tiles, weights[0])
        for k in range(HALO_ROWS):
            r = 1 + HALO_ROWS * step + k
            f = f_own + r
            senders, mean, rise, total = done[k]
            pool[f, 16:24] = mean
            hx[r - 1] = senders
            hslope[r - 1] = rise
            for tile, slot in ((0, 0), (1, 7)):
                part = slice(tile * 8, tile * 8 + 8)
                pool[f, part] = jnp.where(slots == slot, mean, pool_in[r, part])
                ssum[r, part] = jnp.where(slots == slot, total, ssum_in[r, part])
        return carry

    lax.fori_loop(0, 14 // HALO_ROWS, encode_halo, 0)
    fine = m1x[...].reshape(frame * 24, 256) + mm(pool[...].reshape(frame * 24, 256).astype(LOW), weights[2])
    fine = fine.reshape(frame, 24, 256)
    fx[:, 0:16] = fine[:, 0:16].astype(LOW)
    fx[:, 16:32] = jnp.concatenate([fine[:, 16:24], jnp.zeros((frame, 8, 256), WIDE)], 1).astype(LOW)

    edge = iota((128, 128), 0)
    lanes = iota((128, 128), 1)
    up_mask = jnp.where(lanes == edge, 1.0, 0.0)
    up_places = lanes.astype(WIDE)
    up_ones = jnp.ones((128, 128), LOW)
    m2_flat = m2x[...].reshape(a_frame * 16, 256)
    m2_low = m2_flat.astype(LOW)
    up_recv = mm(m2_low, weights[4]).reshape(a_frame, 16, 256)
    pools = []
    for aa in range(a_frame):
        vec = uv[aa]
        picked = (up_mask.reshape(16, 8, 128) * vec[None]).reshape(128, 128).astype(LOW)
        chosen = jnp.where(mm(picked, up_ones) == up_places, 1.0, 0.0).astype(LOW)
        ohu[aa] = chosen
        senders = mm(chosen, fx[2 * aa : 2 * aa + 4].reshape(128, 256)).astype(LOW)
        su[aa] = senders
        pre = mm(senders, weights[3]).reshape(8, 16, 256) + up_recv[aa][None]
        sig = sigmoid_of(pre)
        act = pre * sig
        pools.append(jnp.sum(act, axis=0) * (1.0 / 8))
        uslope[aa] = (sig + act * (1.0 - sig)).reshape(128, 256)
    up_pool = jnp.concatenate(pools, 0).astype(LOW)
    coarse = (m2_flat + mm(up_pool, weights[5])).astype(LOW)

    c_frame = 2 * a_frame
    nodes = a_frame * 16

    def parent_slot(q):
        return jnp.where(q < 16, q // 2, jnp.where((q == 18) | (q == 19), 15, jnp.where((q == 20) | (q == 21), 8, -1)))

    r_i = iota((c_frame * 32, nodes), 0)
    r_j = iota((c_frame * 32, nodes), 1)
    spread = (r_i // 64 == r_j // 16) & (parent_slot(r_i % 32) == r_j % 16)
    spread = jnp.where(spread, 1.0, 0.0).astype(LOW)
    t_i = iota((nodes, c_frame * 32), 1)
    t_j = iota((nodes, c_frame * 32), 0)
    gather = (t_i // 64 == t_j // 16) & (parent_slot(t_i % 32) == t_j % 16)
    gather = jnp.where(gather, 1.0, 0.0).astype(LOW)
    parents = mm(spread, coarse).astype(LOW)
    fine_mid = fx[1 : 1 + c_frame].reshape(c_frame * 32, 256)
    down_pre = mm(parents, weights[6]) + mm(fine_mid, weights[7])
    sig = sigmoid_of(down_pre)
    act = down_pre * sig
    cot_w = mm_nt(cx[...].reshape(c_frame * 32, 256), weights[8])
    dd[0] = (cot_w * (sig + act * (1.0 - sig))).astype(LOW).reshape(c_frame, 32, 256)
    dd[1] = act.astype(LOW).reshape(c_frame, 32, 256)

    def put_grad(index, value):
        acc_s[...] = value
        put_halves(acc_s, keep, send, index - 3, rep)

    act_own = dd[1, pl.ds(c_own, 16), 0:16].reshape(256, 256)
    delta_own = dd[0, pl.ds(c_own, 16), 0:16].reshape(256, 256)
    fine_own = fx[pl.ds(f_own, 16), 0:16].reshape(256, 256)
    cot_own = cot[...].reshape(256, 256)
    out = fine_own.astype(WIDE) + mm(act_own, weights[8])
    mesh_out[...] = out.astype(LOW).reshape(16, 16, 256)
    put_grad(8, mm_tn(act_own, cot_own))
    put_grad(7, mm_tn(fine_own, delta_own))

    child_sum = mm(gather, dd[0].reshape(c_frame * 32, 256))
    n_i = iota((nodes, 256), 0)
    aa_i, bb_i = n_i // 16, n_i % 16
    is_own = (aa_i >= a_own) & (aa_i < a_own + 8) & (bb_i < 8)
    is_real = (bb_i <= 8) | (bb_i == 15)
    if n_lat != 2:
        above = lat * 8 - 1 + aa_i
        is_real = is_real & (above >= 0) & (above < n_lat * 8)
    sum_high, sum_low = two_parts(child_sum)
    coarse_delta = (mm_nt(sum_high, weights[6]) + mm_nt(sum_low, weights[6])).astype(LOW)
    own_high, own_low = two_parts(jnp.where(is_own, child_sum, 0.0))
    put_grad(6, mm_tn(coarse, own_high) + mm_tn(coarse, own_low))
    own_delta = jnp.where(is_own, coarse_delta.astype(WIDE), 0.0).astype(LOW)
    put_grad(5, mm_tn(up_pool, own_delta))
    pool2 = jnp.where(is_real, mm_nt(coarse_delta, weights[5]) * (1.0 / 8), 0.0)
    own_f = jnp.where(is_own, 1.0, 0.0)
    recv[...] = jnp.zeros_like(recv)
    acc_s[...] = jnp.zeros_like(acc_s)
    node_sums = []
    for aa in range(a_frame):
        d = pool2[aa * 16 : aa * 16 + 16][None] * uslope[aa].reshape(8, 16, 256)
        mine = own_f[aa * 16 : aa * 16 + 16][None]
        up_delta = d.astype(LOW)
        wide = up_delta.astype(WIDE)
        owned = wide * mine
        node_sums.append(jnp.sum(owned, axis=0))
        back = mm_tn(ohu[aa], up_delta.reshape(128, 256)).reshape(4, 32, 256)
        recv[2 * aa : 2 * aa + 4] += back[:, 0:24]
        acc_s[...] += mm_tn(su[aa], owned.reshape(128, 256).astype(LOW))
    put_grad(3, acc_s[...])
    ns_high, ns_low = two_parts(jnp.concatenate(node_sums, 0))
    put_grad(4, mm_tn(m2_low, ns_high) + mm_tn(m2_low, ns_low))
    back_high, back_low = two_parts(recv[pl.ds(f_own, 16), 0:16].reshape(256, 256))
    fine_delta = (
        cot_own.astype(WIDE)
        + mm_nt(delta_own, weights[7])
        + mm_nt(back_high, weights[3])
        + mm_nt(back_low, weights[3])
    )
    fd_out[...] = fine_delta
    pool_out[...] = pool[pl.ds(f_own, 16), 0:16].reshape(256, 256).astype(LOW)


def back_kernel(
    m1, weights, fine_delta, pool, ssum, sx_in, slope_in, sx_edge, slope_edge, hx, hslope, mesh1_grad, keep, send, pd, acc
):
    rep = lax.axis_index("rep")
    delta_b = fine_delta[...].astype(LOW)
    pool_delta = mm_nt(delta_b, weights[2]) * (1.0 / 16)
    pd[...] = pool_delta.reshape(16, 16, 256)
    node_delta = pool_delta * ssum[0:16].reshape(256, 256)
    high, low = two_parts(node_delta)
    m1_own = m1[...].reshape(256, 256)
    grad_in = fine_delta[...] + (mm_nt(high, weights[1]) + mm_nt(low, weights[1]))
    mesh1_grad[...] = grad_in.astype(LOW).reshape(16, 16, 256)
    acc[...] = mm_tn(pool[...], delta_b)
    put_halves(acc, keep, send, 2, rep)
    acc[...] = mm_tn(m1_own, high) + mm_tn(m1_own, low)
    put_halves(acc, keep, send, 1, rep)

    def deltas_of(r, tile, rise):
        d = pd[r, tile * 8 : tile * 8 + 8][None] * rise.reshape(16, 8, 256)
        return d.reshape(128, 256).astype(LOW)

    senders, deltas = [], []
    for i, r in enumerate((0, 15)):
        senders.append(sx_edge[i].reshape(256, 256))
        for tile in range(2):
            deltas.append(deltas_of(r, tile, slope_edge[i, tile].astype(WIDE)))
    acc[...] = mm_tn(jnp.concatenate(senders, 0), jnp.concatenate(deltas, 0))
    slots = iota((128, 256), 0) % 8

    def rows(step, carry):
        senders, deltas = [], []
        for k in range(2):
            r = 1 + 2 * step + k
            halo = hx[r - 1].astype(WIDE)
            halo_rise = hslope[r - 1].astype(WIDE)
            for tile, slot in ((0, 0), (1, 7)):
                ours = slots == slot
                senders.append(jnp.where(ours, halo, sx_in[r, tile].astype(WIDE)).astype(LOW))
                deltas.append(deltas_of(r, tile, jnp.where(ours, halo_rise, slope_in[r, tile].astype(WIDE))))
        acc[...] += mm_tn(jnp.concatenate(senders, 0), jnp.concatenate(deltas, 0))
        return carry

    lax.fori_loop(0, 7, rows, 0)
    put_halves(acc, keep, send, 0, rep)


def block_place():
    return (lax.axis_index("lat") % 2) * 2 + lax.axis_index("lon") % 2


def quarters_kernel(kept_first, got_first, kept, got, own, *pieces):
    place = block_place()
    for step in range(4):
        rows = pl.ds(pl.multiple_of((place ^ step) * 32, 32), 32)
        for first, mine, other in ((0, kept_first, got_first), (3, kept, got)):
            total = mine[:, rows, :] + other[:, rows, :].astype(WIDE)
            at = slice(first, first + mine.shape[0])
            if step == 0:
                own[at] = total
            else:
                pieces[step - 1][at] = total.astype(LOW)


def add_kernel(*refs):
    total = refs[0][...].astype(WIDE)
    for ref in refs[1:-1]:
        total = total + ref[...].astype(WIDE)
    refs[-1][...] = total.astype(LOW)


def small_kernel(kernel, out_shape, name, *values):
    vmem = pl.BlockSpec(memory_space=pltpu.VMEM)
    return pl.pallas_call(
        kernel,
        out_shape=out_shape,
        in_specs=[vmem] * len(values),
        out_specs=jax.tree.map(lambda _: vmem, out_shape),
        compiler_params=pltpu.CompilerParams(vmem_limit_bytes=8 * 1024 * 1024),
        name=name,
    )(*values)


def spread_kernel(scale, *refs):
    pieces, (out, stage, sems) = refs[:8], refs[8:]
    rep = lax.axis_index("rep")
    place = block_place()
    copies = []
    for k in range(9):
        for step in range(4):
            at = (place ^ step) * 32
            for half, piece in ((rep, pieces[step]), (1 - rep, pieces[4 + step])):
                rows = pl.ds(pl.multiple_of(half * 128 + at, 32), 32)
                stage[k, rows, :] = piece[k].astype(WIDE) * scale
        copies.append(pltpu.make_async_copy(stage.at[k], out.at[k], sems.at[k]))
        copies[-1].start()
    for copy in copies:
        copy.wait()


def flat_main(dirs, n_lat, *refs):
    n_bands = 3 * len(dirs)
    own, refs = refs[:7], refs[7:]
    sides, refs = refs[:2], refs[2:]
    bands, refs = refs[:n_bands], refs[n_bands:]
    weights, refs = refs[0], refs[1:]
    outs, scratch = refs[:10], refs[10:]
    main_kernel(dirs, n_lat, own, sides, bands, weights, outs, scratch)


class Reduction:
    def __init__(self, mesh):
        self.sizes = (mesh.shape["lon"], mesh.shape["lat"])

    def between(self, values, lon_bit, lat_bit):
        lat_size = self.sizes[1]
        return permute(
            values,
            ("lon", "lat"),
            lambda i: ((i // lat_size) ^ lon_bit) * lat_size + ((i % lat_size) ^ lat_bit),
            self.sizes,
        )

    def siblings(self, values):
        return permute(values, "rep", lambda i: i ^ 1, (2,))

    def quarters(self, *halves):
        _, rows, cols = halves[0].shape
        shape = (9, rows // 4, cols)
        shapes = [jax.ShapeDtypeStruct(shape, WIDE)] + [jax.ShapeDtypeStruct(shape, LOW)] * 3
        return small_kernel(quarters_kernel, shapes, "quarters", *halves)

    def block(self, quarters):
        own, *others = quarters
        got = [self.between(piece, step & 1, step >> 1) for step, piece in zip((1, 2, 3), others)]
        shape = jax.ShapeDtypeStruct(own.shape, LOW)
        return small_kernel(add_kernel, shape, "block_sum", own, *got)

    def total(self, total):
        shape = jax.ShapeDtypeStruct(total.shape, LOW)
        for which, size in enumerate(self.sizes):
            bit = 2
            while bit < size:
                other = self.between(total, *((bit, 0) if which == 0 else (0, bit)))
                total = small_kernel(add_kernel, shape, "pair_sum", total, other)
                bit *= 2
        return total

    def pieces(self, own):
        mine = [own] + [self.between(own, step & 1, step >> 1) for step in (1, 2, 3)]
        return mine + [self.siblings(piece) for piece in mine]


def body(mesh, grid_state, mesh1_state, mesh2_state, grid_edges, up_edges, weights, cotangent):
    n_lat, n_lon = mesh.shape["lat"], mesh.shape["lon"]
    glon = grid_state.shape[1] * 2 * n_lon
    m1lon = mesh1_state.shape[1] * 2 * n_lon
    dirs = (None,) if n_lat == 2 else (True, False)
    vmem = pl.BlockSpec(memory_space=pltpu.VMEM)
    params = pltpu.CompilerParams(vmem_limit_bytes=VMEM_BYTES)
    shapes = [48] + [SIDE_ROWS] * 2 + [BAND_ROWS, CORNER_ROWS, CORNER_ROWS] * len(dirs)
    hbm = pl.BlockSpec(memory_space=pltpu.HBM)
    states = (grid_state, mesh1_state, cotangent, mesh2_state)
    grid_state, mesh1_state, cotangent, mesh2_state, codes, *buffers = pl.pallas_call(
        functools.partial(pack_kernel, dirs, glon, m1lon),
        out_shape=[jax.ShapeDtypeStruct(state.shape, state.dtype) for state in states]
        + [jax.ShapeDtypeStruct((n, 256), LOW) for n in shapes],
        in_specs=[hbm] * 6,
        out_specs=[vmem] * (4 + len(shapes)),
        scratch_shapes=[
            pltpu.VMEM(grid_edges.shape, grid_edges.dtype),
            pltpu.VMEM(up_edges.shape, up_edges.dtype),
            pltpu.SemaphoreType.DMA((6,)),
        ],
        compiler_params=params,
        name="pack_halos",
    )(*(in_hbm(value) for value in (*states, grid_edges, up_edges)))
    inner = pl.pallas_call(
        inner_kernel,
        out_shape=[
            jax.ShapeDtypeStruct((16, 2, 128, 256), LOW),
            jax.ShapeDtypeStruct((16, 2, 128, 256), LOW),
            jax.ShapeDtypeStruct((16, 16, 256), WIDE),
            jax.ShapeDtypeStruct((16, 16, 256), WIDE),
            jax.ShapeDtypeStruct(weights.shape, LOW),
        ],
        in_specs=[vmem] * 3 + [hbm],
        out_specs=[vmem] * 5,
        scratch_shapes=[
            pltpu.VMEM((3, 34, 16, 256), LOW),
            pltpu.VMEM((3, 128, 256), LOW),
            pltpu.VMEM((16, 16, 256), LOW),
            pltpu.VMEM((16, 16, 256), WIDE),
            pltpu.SemaphoreType.DMA((2,)),
        ],
        compiler_params=params,
        cost_estimate=pl.CostEstimate(flops=4_000_000_000, bytes_accessed=8_000_000, transcendentals=1_000_000),
        name="inner_rows",
    )(grid_state, mesh1_state, codes, in_hbm(weights))
    sx_in, slope_in, pool_in, ssum_in, weights = inner
    own = (grid_state, mesh1_state, cotangent, mesh2_state, codes, pool_in, ssum_in)

    def beyond(lon, core):
        return ((lon + (1 if core else -1)) % n_lon, 1 - core)

    def send_to(values, other_lat, column):
        def partner(i):
            lon, rest = divmod(i, n_lat * 2)
            row, core = divmod(rest, 2)
            row = other_lat(row)
            if row is None:
                return None
            if column == "sibling":
                core = 1 - core
            elif column == "beyond":
                lon, core = beyond(lon, core)
            return (lon * n_lat + row) * 2 + core

        return permute(values, ("lon", "lat", "rep"), partner, (n_lon, n_lat, 2))

    def shift(sends_bottom):
        if sends_bottom is None:
            return lambda row: row ^ 1
        if sends_bottom:
            return lambda row: row + 1 if row + 1 < n_lat else None
        return lambda row: row - 1 if row else None

    got_sides = [send_to(buffers[0], lambda row: row, "sibling"), send_to(buffers[1], lambda row: row, "beyond")]
    got_bands = []
    for i, sends_bottom in enumerate(dirs):
        for k, column in enumerate(("same", "sibling", "beyond")):
            got_bands.append(send_to(buffers[2 + 3 * i + k], shift(sends_bottom), column))

    frame = 20 if n_lat == 2 else 22
    a_frame = 9 if n_lat == 2 else 10
    c_frame = 2 * a_frame
    g_frame = 2 * frame + 6
    scratch = [
        pltpu.VMEM((3, g_frame, 16, 256), LOW),
        pltpu.VMEM((frame, 24, 256), WIDE),
        pltpu.VMEM((frame, 24, 256), WIDE),
        pltpu.VMEM((frame, 16, 256), LOW),
        pltpu.VMEM((frame, 16, 256), LOW),
        pltpu.VMEM((a_frame, 8, 128), WIDE),
        pltpu.VMEM((frame, 24, 256), WIDE),
        pltpu.VMEM((frame, 32, 256), LOW),
        pltpu.VMEM((c_frame, 32, 256), LOW),
        pltpu.VMEM((a_frame, 16, 256), WIDE),
        pltpu.VMEM((a_frame, 128, 128), LOW),
        pltpu.VMEM((a_frame, 128, 256), LOW),
        pltpu.VMEM((a_frame, 128, 256), WIDE),
        pltpu.VMEM((2, c_frame, 32, 256), LOW),
        pltpu.VMEM((256, 256), WIDE),
        pltpu.VMEM((3, 128, 256), LOW),
    ]
    n_in = 7 + 2 + len(got_bands) + 1
    mesh_out, kept, sent, fine_delta, pool, ssum, sx_edge, slope_edge, hx, hslope = pl.pallas_call(
        functools.partial(flat_main, dirs, n_lat),
        out_shape=[
            jax.ShapeDtypeStruct(mesh1_state.shape, LOW),
            jax.ShapeDtypeStruct((6, 128, 256), WIDE),
            jax.ShapeDtypeStruct((6, 128, 256), LOW),
            jax.ShapeDtypeStruct((256, 256), WIDE),
            jax.ShapeDtypeStruct((256, 256), LOW),
            jax.ShapeDtypeStruct((17, 16, 256), WIDE),
            jax.ShapeDtypeStruct((3, 2, 128, 256), LOW),
            jax.ShapeDtypeStruct((3, 2, 128, 256), LOW),
            jax.ShapeDtypeStruct((14, 128, 256), LOW),
            jax.ShapeDtypeStruct((14, 128, 256), LOW),
        ],
        in_specs=[vmem] * n_in,
        out_specs=[vmem] * 10,
        scratch_shapes=scratch,
        compiler_params=params,
        name="sweep",
    )(*own, *got_sides, *got_bands, weights)
    reduction = Reduction(mesh)
    got = reduction.siblings(sent)
    mesh1_grad, kept_first, sent_first = pl.pallas_call(
        back_kernel,
        out_shape=[
            jax.ShapeDtypeStruct(mesh1_state.shape, LOW),
            jax.ShapeDtypeStruct((3, 128, 256), WIDE),
            jax.ShapeDtypeStruct((3, 128, 256), LOW),
        ],
        in_specs=[vmem] * 11,
        out_specs=[vmem] * 3,
        scratch_shapes=[pltpu.VMEM((16, 16, 256), WIDE), pltpu.VMEM((256, 256), WIDE)],
        compiler_params=params,
        cost_estimate=pl.CostEstimate(flops=3_000_000_000, bytes_accessed=8_000_000, transcendentals=0),
        name="encoder_back",
    )(mesh1_state, weights, fine_delta, pool, ssum, sx_in, slope_in, sx_edge, slope_edge, hx, hslope)
    node_total = mesh1_state.shape[0] * mesh1_state.shape[1] * n_lat * n_lon * 2
    scale = float(node_total) ** (-0.5)
    quarters = reduction.quarters(kept_first, reduction.siblings(sent_first), kept, got)
    pieces = reduction.pieces(reduction.total(reduction.block(quarters)))
    weight_grads = pl.pallas_call(
        functools.partial(spread_kernel, scale),
        out_shape=jax.ShapeDtypeStruct((9, 256, 256), WIDE),
        in_specs=[vmem] * 8,
        out_specs=hbm,
        scratch_shapes=[pltpu.VMEM((9, 256, 256), WIDE), pltpu.SemaphoreType.DMA((9,))],
        compiler_params=params,
        name="spread_gradients",
    )(*pieces)
    return (mesh_out, mesh1_grad, weight_grads)


def solution(mesh):
    in_specs = (
        P(("groups", "lat"), ("lon", "rep"), None),
        P(("groups", "lat"), ("lon", "rep"), None),
        P(("groups", "lat"), "lon", None),
        P(None, "lat", ("lon", "rep")),
        P(None, "lat", "lon"),
        P(),
        P(("groups", "lat"), ("lon", "rep"), None),
    )
    out_specs = (
        P(("groups", "lat"), ("lon", "rep"), None),
        P(("groups", "lat"), ("lon", "rep"), None),
        P("groups", None, None),
    )
    return jax.shard_map(
        functools.partial(body, mesh), mesh=mesh, in_specs=in_specs, out_specs=out_specs, check_vma=False
    )
```

```python
import functools

import jax
import jax.numpy as jnp
from jax import lax
from jax.experimental import pallas as pl
from jax.experimental.pallas import tpu as pltpu
from jax.sharding import PartitionSpec as P

LOW = jnp.bfloat16
WIDE = jnp.float32
VMEM_BYTES = 24 * 1024 * 1024
HALO_ROWS = 14
BACK_ROWS = 14
INNER_ROWS = 7
CODE = LOW

SIDE_ROWS = 416
BAND_ROWS = 352
CORNER_ROWS = 112


def permute(values, axes, partner, sizes):
    total = 1
    for size in sizes:
        total *= size
    pairs = [(i, partner(i)) for i in range(total)]
    return lax.ppermute(values, axes, [(i, j) for i, j in pairs if j is not None])


def mm(left, right):
    return jnp.dot(left, right, preferred_element_type=WIDE)


def mm_nt(left, right):
    return lax.dot_general(left, right, (((1,), (1,)), ((), ())), preferred_element_type=WIDE)


def mm_tn(left, right):
    return lax.dot_general(left, right, (((0,), (0,)), ((), ())), preferred_element_type=WIDE)


def two_parts(value):
    high = value.astype(LOW)
    return high, (value - high.astype(WIDE)).astype(LOW)


def silu_of(half):
    t = jnp.tanh(half)
    up = 1.0 + t
    act = half * up
    return act, up + act * (1.0 - t)


def halved(weight):
    return (weight.astype(WIDE) * 0.5).astype(LOW)


def iota(shape, dim):
    return lax.broadcasted_iota(jnp.int32, shape, dim)


def in_hbm(value):
    return pltpu.with_memory_space_constraint(value, pltpu.HBM)


def split(value, size):
    if size & (size - 1) == 0:
        return value >> (size.bit_length() - 1), value & (size - 1)
    return value // size, value % size


def wrapped(value, size):
    if size & (size - 1) == 0:
        return value & (size - 1)
    return jnp.mod(value, size)


def edge_codes(edges, glon, lat, col, rows, cols):
    row = iota(edges.shape, 0)
    lane = iota(edges.shape, 1)
    j = lane % 16
    at_row, at_col = split(edges, glon)
    down = at_row - (2 * (lat * rows + row) - 2)
    across = wrapped(at_col - (2 * (col * cols + j) - 2), glon)
    place = 2 * (j % 8) + 6 + across
    own = down * 16 + place + jnp.where(place >= 16, 112, 0)
    base = down * 16 + across + 6
    turned = jnp.where(j < 4, pltpu.roll(base, 256 - 12, 1), pltpu.roll(base, 4, 1))
    sent = turned + 2 * (j - 4) + jnp.where(j < 4, 0, 128)
    return own.astype(WIDE), sent.astype(WIDE)


def up_codes(edges, m1lon, lat, col, rep, rows, cols):
    row = iota(edges.shape, 0)
    l16 = iota(edges.shape, 1) % 16
    low = jnp.where(l16 < 8, edges, pltpu.roll(edges, 8, 1))
    high = jnp.where(l16 < 8, pltpu.roll(edges, 128 - 8, 1), edges)
    edges = jnp.where(rep == 0, low, high)
    b = l16 % 8
    at_row, at_col = split(edges, m1lon)
    down = at_row - (2 * (lat * rows + row) - 1)
    across = wrapped(at_col - (2 * (col * cols + b) - 1), m1lon)
    base = jnp.where(l16 < 8, b, jnp.where(b >= 4, b - 8, b + 8))
    at = 2 * base - 1 + across
    at = jnp.where(at < 0, at + 20, jnp.where(at >= 16, at + 4, at))
    return (down * 32 + at).astype(WIDE)


def pack_kernel(dirs, glon, m1lon, *refs):
    far, (grid, m1, cot, m2, codes), rest = refs[:6], refs[6:11], refs[11:]
    outs, (edges, ups, sems) = rest[:-3], rest[-3:]
    copies = [
        pltpu.make_async_copy(a, b, sems.at[i]) for i, (a, b) in enumerate(zip(far, (grid, m1, cot, m2, edges, ups)))
    ]
    for copy in copies:
        copy.start()
    for copy in copies[::-1]:
        copy.wait()
    rep = lax.axis_index("rep")
    lat = lax.axis_index("lat")
    col = lax.axis_index("lon") * 2 + rep
    sides = outs[:2]
    bands = outs[2:]
    flat = jnp.concatenate([edges[k] for k in range(16)], axis=1)
    own_k, sent_k = edge_codes(flat, glon, lat, col, 16, 16)
    flat = jnp.concatenate([ups[k] for k in range(8)], axis=1)
    up_k = up_codes(flat, m1lon, lat, col, rep, 8, 8)
    up_k = jnp.concatenate([up_k, jnp.zeros_like(up_k)], 1)
    codes[0:16, :] = own_k.astype(LOW)
    codes[16:32, :] = sent_k.astype(LOW)
    codes[32:48, :] = jnp.concatenate([up_k, jnp.zeros_like(up_k)], 0).astype(LOW)
    m2w = m2[...].astype(WIDE)
    m2_half = jnp.where(rep == 0, m2w[:, 0:8], m2w[:, 8:16])
    row8 = iota((8, 256), 0)

    def few(k_rows, last, ghost):
        up = jnp.where(last, up_k[7:8], up_k[0:1])
        rest = jnp.where(row8 == 3, jnp.broadcast_to(up, (8, 256)), 0.0)
        if ghost is not None:
            rest = jnp.where(row8 == 4, jnp.broadcast_to(ghost, (8, 256)), rest)
        return jnp.where(last, jnp.where(row8 >= 5, k_rows[8:16], rest), jnp.where(row8 < 3, k_rows[0:8], rest))

    def last_rows(sends_bottom):
        if sends_bottom is None:
            return lat == 0
        return jnp.bool_(sends_bottom)

    def fill(targets, right):
        side, corners = targets
        g = grid[:, 16:32, :] if right else grid[:, 0:16, :]
        g = g.astype(WIDE)[:, 8:16] if right else g.astype(WIDE)[:, 0:8]
        part = slice(12, 16) if right else slice(0, 4)
        pair = jnp.concatenate([m1[...].astype(WIDE)[:, part], cot[...].astype(WIDE)[:, part]], axis=1)
        edge = 7 if right else 0
        ghosts = jnp.zeros((8, 256), WIDE)
        for a in range(8):
            ghosts = jnp.where(row8 == a, jnp.broadcast_to(m2_half[a, edge : edge + 1], (8, 256)), ghosts)
        side[0:256, :] = g.reshape(256, 256).astype(LOW)
        side[256:384, :] = pair.reshape(128, 256).astype(LOW)
        side[384:400, :] = sent_k.astype(LOW)
        side[400:416, :] = jnp.concatenate([up_k, ghosts], 0).astype(LOW)
        for sends_bottom, corner in corners:
            last = last_rows(sends_bottom)
            corner[0:64, :] = jnp.where(last, g[24:32], g[0:8]).reshape(64, 256).astype(LOW)
            corner[64:96, :] = jnp.where(last, pair[12:16], pair[0:4]).reshape(32, 256).astype(LOW)
            block = few(sent_k, last, jnp.where(last, ghosts[7:8], ghosts[0:1]))
            corner[96:112, :] = jnp.concatenate([block, block], 0).astype(LOW)

    sib = (sides[0], [(d, bands[3 * i + 1]) for i, d in enumerate(dirs)])
    out = (sides[1], [(d, bands[3 * i + 2]) for i, d in enumerate(dirs)])

    @pl.when(rep == 0)
    def _():
        fill(sib, True)
        fill(out, False)

    @pl.when(rep == 1)
    def _():
        fill(sib, False)
        fill(out, True)

    for i, sends_bottom in enumerate(dirs):
        band = bands[3 * i]
        last = last_rows(sends_bottom)
        first = jnp.where(last, 1, 0)
        band[0:256, :] = grid[pl.ds(first * 24, 8)].reshape(256, 256)
        band[256:304, :] = m1[pl.ds(first * 13, 3)].reshape(48, 256)
        band[304:336, :] = cot[pl.ds(first * 14, 2)].reshape(32, 256)
        mt = jnp.where(last, m2_half[7], m2_half[0])
        band[336:352, :] = jnp.concatenate([few(own_k, last, None), mt], 0).astype(LOW)


def set_masks(masks):
    edge = iota((128, 256), 0)
    lanes = iota((128, 256), 1)
    slot = edge % 8
    base = (edge // 8) * 16
    masks[0] = jnp.where(lanes == base + slot, 1.0, 0.0).astype(LOW)
    masks[1] = jnp.where(lanes == base + 8 + slot, 1.0, 0.0).astype(LOW)
    masks[2] = jnp.where(lanes == base + jnp.where(slot < 7, slot, 15), 1.0, 0.0).astype(LOW)


def encode_tiles(tiles, weight):
    ones = jnp.ones((256, 256), LOW)
    places = iota((128, 256), 1).astype(WIDE).astype(CODE)
    one, zero = jnp.ones((128, 256), LOW), jnp.zeros((128, 256), LOW)
    picked = [(mask.reshape(8, 16, 256) * codes[None]).reshape(128, 256) for mask, codes, _, _ in tiles]
    found = mm(jnp.concatenate(picked, 0), ones).astype(CODE)
    senders = []
    for i, (_, _, window, _) in enumerate(tiles):
        chosen = jnp.where(found[i * 128 : i * 128 + 128] == places, one, zero)
        senders.append(mm(chosen, jnp.concatenate(window, 0)).astype(LOW))
    pre_all = mm(jnp.concatenate(senders, 0), weight)
    results = []
    for i, (_, _, _, received) in enumerate(tiles):
        act, rise = silu_of(pre_all[i * 128 : i * 128 + 128].reshape(16, 8, 256) + received[None])
        results.append(
            (senders[i], jnp.sum(act, axis=0) * (1.0 / 16), rise.reshape(128, 256).astype(LOW), jnp.sum(rise, axis=0))
        )
    return results


BLOCKS = ((0, 1), (1, 2), (0, 2))


def inner_kernel(grid, m1, codes, far, sx, slope, pool, ssum, weights, masks, spread, gather, gx, ko, recv, sems):
    first = pltpu.make_async_copy(far.at[0:2], weights.at[0:2], sems.at[0])
    others = pltpu.make_async_copy(far.at[2:9], weights.at[2:9], sems.at[1])
    first.start()
    others.start()
    set_masks(masks)

    def place_grid(step, carry):
        r = step * 8
        wide = grid[pl.ds(r, 8)].astype(WIDE)
        edge = jnp.zeros((8, 8, 256), WIDE)
        gx[0, pl.ds(r, 8)] = jnp.concatenate([edge, wide[:, 0:8]], 1).astype(LOW)
        gx[1, pl.ds(r, 8)] = wide[:, 8:24].astype(LOW)
        gx[2, pl.ds(r, 8)] = jnp.concatenate([wide[:, 24:32], edge], 1).astype(LOW)
        return carry

    lax.fori_loop(0, 4, place_grid, 0)
    gx[:, 32:34] = jnp.zeros((3, 2, 16, 256), LOW)
    own = codes[0:16, :].astype(WIDE)
    for r in range(16):
        ko[r] = jnp.broadcast_to(own[r : r + 1], (16, 256)).astype(LOW)
    first.wait()
    recv[...] = mm(m1[...].reshape(256, 256), weights[1]).reshape(16, 16, 256) * 0.5
    weight = halved(weights[0])

    def rows(step, carry):
        spots = [(1 + INNER_ROWS * step + k, tile) for k in range(INNER_ROWS) for tile in range(2)]
        tiles = []
        for r, tile in spots:
            window = [gx[blk, pl.ds(2 * r - 2, 8)].reshape(128, 256) for blk in BLOCKS[tile]]
            tiles.append((masks[tile], ko[r], window, recv[r, tile * 8 : tile * 8 + 8]))
        for (r, tile), (senders, mean, rise, total) in zip(spots, encode_tiles(tiles, weight)):
            sx[r, tile] = senders
            slope[r, tile] = rise
            pool[r, tile * 8 : tile * 8 + 8] = mean
            ssum[r, tile * 8 : tile * 8 + 8] = total
        return carry

    def family(node, state):
        q = state % 32
        slot = jnp.where(q < 16, q // 2, jnp.where((q == 18) | (q == 19), 15, jnp.where((q == 20) | (q == 21), 8, -1)))
        return jnp.where((state // 64 == node // 16) & (slot == node % 16), 1.0, 0.0).astype(LOW)

    spread[...] = family(iota(spread.shape, 1), iota(spread.shape, 0))
    gather[...] = family(iota(gather.shape, 0), iota(gather.shape, 1))
    lax.fori_loop(0, 14 // INNER_ROWS, rows, 0)
    others.wait()


def put_halves(grad, keep, send, index, rep):
    keep[index] = grad[pl.ds(pl.multiple_of(rep * 128, 128), 128), :]
    send[index] = grad[pl.ds(pl.multiple_of((1 - rep) * 128, 128), 128), :].astype(LOW)


def main_kernel(
    dirs, n_lat, own, sides, bands, weights, outs, scratch
):
    grid, m1, cot, m2, codes, pool_in, ssum_in, masks, spread, gather = own
    mesh_out, keep, send, fd_out, pool_out, ssum, sx, slope, hx, hslope = outs
    gx, m1x, recv, ko, k2, uv, pool, fx, cx, m2x, ohu, su, uslope, dd, acc_s = scratch
    rep = lax.axis_index("rep")
    lat = lax.axis_index("lat")
    frame = m1x.shape[0]
    a_frame = m2x.shape[0]
    if n_lat == 2:
        g_own, f_own, c_own, a_own = 4 + 4 * lat, 1 + 2 * lat, 2 * lat, lat
        odd_rows = 5
        odd_row = lambda i: jnp.where(lat == 0, jnp.where(i == 0, 1, 15 + i), jnp.where(i < 4, i, 18))
    else:
        g_own, f_own, c_own, a_own = 8, 3, 2, 1
        odd_rows = 8
        odd_row = lambda i: jnp.where(i < 4, i, 14 + i)

    def left_right(sib, out):
        return jnp.where(rep == 1, sib, out), jnp.where(rep == 1, out, sib)

    zero_rows = jnp.zeros((4, 16, 256), LOW)
    for blk in range(3):
        gx[blk, 0:4] = zero_rows
        gx[blk, gx.shape[1] - 6 : gx.shape[1] - 2] = zero_rows
        gx[blk, gx.shape[1] - 4 :] = zero_rows

    def put_grid(at, mid, sib, out):
        n = mid.shape[0]
        left, right = left_right(sib.astype(WIDE), out.astype(WIDE))
        left = left.reshape(n, 8, 256)
        right = right.reshape(n, 8, 256)
        wide = mid.astype(WIDE)
        gx[0, pl.ds(at, n)] = jnp.concatenate([left, wide[:, 0:8]], 1).astype(LOW)
        gx[1, pl.ds(at, n)] = wide[:, 8:24].astype(LOW)
        gx[2, pl.ds(at, n)] = jnp.concatenate([wide[:, 24:32], right], 1).astype(LOW)

    def own_grid(step, carry):
        r = step * 8
        r8 = pl.multiple_of(step * 64, 64)
        put_grid(g_own + r, grid[pl.ds(r, 8)], sides[0][pl.ds(r8, 64), :], sides[1][pl.ds(r8, 64), :])
        return carry

    lax.fori_loop(0, 4, own_grid, 0)

    def put_fine(sib, out, n, mid):
        left, right = left_right(sib.astype(WIDE), out.astype(WIDE))
        left = left.reshape(n, 8, 256)
        right = right.reshape(n, 8, 256)
        slot = iota((n, 8, 256), 1)
        states = jnp.concatenate([left[:, 0:4], right[:, 0:4]], 1)
        states = jnp.where(slot == 0, mid[:, 0:8], jnp.where(slot == 7, mid[:, 8:16], states))
        cots = jnp.concatenate([left[:, 4:8], right[:, 4:8]], 1)
        return states, cots

    m1x[...] = jnp.zeros_like(m1x)
    cx[...] = jnp.zeros_like(cx)
    m1_wide = m1[...].astype(WIDE)
    states, cots = put_fine(sides[0][256:384, :], sides[1][256:384, :], 16, m1_wide)
    m1x[pl.ds(f_own, 16), 0:16] = m1_wide
    m1x[pl.ds(f_own, 16), 16:24] = states
    cx[pl.ds(c_own, 16), 0:16] = cot[...]
    cx[pl.ds(c_own, 16), 16:32] = jnp.concatenate([cots, jnp.zeros_like(cots)], 1).astype(LOW)

    def put_m2(at, mid, sib, out, n):
        left, right = left_right(sib, out)
        slot = iota((8, 256), 0)
        for a in range(n):
            l_a = jnp.broadcast_to(left[a : a + 1], (8, 256))
            r_a = jnp.broadcast_to(right[a : a + 1], (8, 256))
            ghost = jnp.where(slot == 7, l_a, jnp.where(slot == 0, r_a, 0.0))
            m2x[at + a] = jnp.concatenate([mid[a], ghost], 0)

    m2w = m2[...].astype(WIDE)
    m2_half = jnp.where(rep == 0, m2w[:, 0:8], m2w[:, 8:16])
    side_few = [side[384:416, :].astype(WIDE) for side in sides]
    put_m2(a_own, m2_half, side_few[0][24:32], side_few[1][24:32], 8)

    def codes_of(mid, sib, out):
        left, right = left_right(sib, out)
        l16 = iota(mid.shape, 1) % 16
        return jnp.where((l16 == 0) | (l16 == 15), mid, jnp.where(l16 < 4, left, right))

    def ups_of(mid, sib, out):
        left, right = left_right(sib, out)
        l16 = iota(mid.shape, 1) % 16
        return jnp.where(l16 < 8, mid, jnp.where(l16 < 12, right, left))[:, 0:128]

    def put_codes(f_at, a_at, own_rows, halo_rows, up_rows):
        for r in range(own_rows.shape[0]):
            ko[f_at + r] = jnp.broadcast_to(own_rows[r : r + 1], (16, 256)).astype(LOW)
            k2[f_at + r] = jnp.broadcast_to(halo_rows[r : r + 1], (16, 256)).astype(LOW)
        for r in range(up_rows.shape[0]):
            uv[a_at + r] = jnp.broadcast_to(up_rows[r : r + 1], (8, 128))

    own_codes = codes[...].astype(WIDE)
    put_codes(
        f_own, a_own, own_codes[0:16],
        codes_of(own_codes[0:16], side_few[0][0:16], side_few[1][0:16]),
        ups_of(own_codes[32:40], side_few[0][16:24], side_few[1][16:24]),
    )
    for i, sends_bottom in enumerate(dirs):
        band, corner_sib, corner_out = bands[3 * i : 3 * i + 3]
        if sends_bottom is None:
            top = lat
        else:
            top = 1 if sends_bottom else 0
        below = 1 - top
        put_grid(
            below * (g_own + 32), band[0:256, :].reshape(8, 32, 256), corner_sib[0:64, :], corner_out[0:64, :]
        )
        is_top = top == 1
        mids = band[256:304, :].astype(WIDE).reshape(3, 16, 256)
        mids4 = jnp.where(is_top, jnp.concatenate([mids[0:1], mids], 0), jnp.concatenate([mids, mids[2:3]], 0))
        states, cots = put_fine(corner_sib[64:96, :], corner_out[64:96, :], 4, mids4)
        f_at = below * (f_own + 16)
        c_at = below * (c_own + 16)
        a_at = below * (a_own + 8)
        m1x[pl.ds(f_at, 3), 0:16] = mids
        m1x[pl.ds(f_at, 3), 16:24] = jnp.where(is_top, states[1:4], states[0:3])
        cx[pl.ds(c_at, 2), 0:16] = band[304:336, :].reshape(2, 16, 256)
        cots = jnp.where(is_top, cots[2:4], cots[0:2])
        cx[pl.ds(c_at, 2), 16:32] = jnp.concatenate([cots, jnp.zeros_like(cots)], 1).astype(LOW)
        band_few = band[336:352, :].astype(WIDE)
        sib_few = corner_sib[96:112, :].astype(WIDE)[0:8]
        out_few = corner_out[96:112, :].astype(WIDE)[0:8]
        put_m2(a_at, band_few[8:16].reshape(1, 8, 256), sib_few[4:5], out_few[4:5], 1)
        own_k = band_few[0:8]
        halo_k = codes_of(own_k, sib_few, out_few)
        up_k = ups_of(own_k, sib_few, out_few)
        put_codes(
            f_at, a_at,
            jnp.where(is_top, own_k[5:8], own_k[0:3]),
            jnp.where(is_top, halo_k[5:8], halo_k[0:3]),
            up_k[3:4],
        )

    recv[...] = mm(m1x[...].reshape(frame * 24, 256).astype(LOW), weights[1]).reshape(frame, 24, 256) * 0.5
    weight = halved(weights[0])
    pool[...] = jnp.zeros_like(pool)

    def window_of(f, tile):
        return [gx[blk, pl.ds(2 * f, 8)].reshape(128, 256) for blk in BLOCKS[tile]]

    batch = 5 if odd_rows == 5 else 4

    def encode_rows(step, carry):
        spots = [(odd_row(step * batch + k), tile) for k in range(batch) for tile in range(3)]
        tiles = []
        for f, tile in spots:
            vec = ko[f] if tile < 2 else k2[f]
            tiles.append((masks[tile], vec, window_of(f, tile), recv[f, tile * 8 : tile * 8 + 8]))
        for (f, tile), (senders, mean, rise, total) in zip(spots, encode_tiles(tiles, weight)):
            row = f - f_own
            kept_at = jnp.where(row == 0, 0, jnp.where(row == 15, 1, 2))
            row = jnp.where(kept_at == 2, 16, row)
            pool[f, tile * 8 : tile * 8 + 8] = mean
            if tile < 2:
                sx[kept_at, tile] = senders
                slope[kept_at, tile] = rise
                ssum[row, tile * 8 : tile * 8 + 8] = total
        return carry

    lax.fori_loop(0, odd_rows // batch, encode_rows, 0)
    slots = iota((8, 256), 0)

    def encode_halo(step, carry):
        tiles = []
        for k in range(HALO_ROWS):
            f = f_own + 1 + HALO_ROWS * step + k
            tiles.append((masks[2], k2[f], window_of(f, 2), recv[f, 16:24]))
        done = encode_tiles(tiles, weight)
        for k in range(HALO_ROWS):
            r = 1 + HALO_ROWS * step + k
            f = f_own + r
            senders, mean, rise, total = done[k]
            pool[f, 16:24] = mean
            hx[r - 1] = senders
            hslope[r - 1] = rise
            for tile, slot in ((0, 0), (1, 7)):
                part = slice(tile * 8, tile * 8 + 8)
                pool[f, part] = jnp.where(slots == slot, mean, pool_in[r, part])
                ssum[r, part] = jnp.where(slots == slot, total, ssum_in[r, part])
        return carry

    lax.fori_loop(0, 14 // HALO_ROWS, encode_halo, 0)
    fine = m1x[...].reshape(frame * 24, 256) + mm(pool[...].reshape(frame * 24, 256).astype(LOW), weights[2])
    fine = fine.reshape(frame, 24, 256)
    fx[:, 0:16] = fine[:, 0:16].astype(LOW)
    fx[:, 16:32] = jnp.concatenate([fine[:, 16:24], jnp.zeros((frame, 8, 256), WIDE)], 1).astype(LOW)

    edge = iota((128, 128), 0)
    lanes = iota((128, 128), 1)
    up_mask = jnp.where(lanes == edge, 1.0, 0.0)
    up_places = lanes.astype(WIDE)
    up_ones = jnp.ones((128, 128), LOW)
    m2_flat = m2x[...].reshape(a_frame * 16, 256)
    m2_low = m2_flat.astype(LOW)
    up_recv = mm(m2_low, weights[4]).reshape(a_frame, 16, 256) * 0.5
    weight = halved(weights[3])
    pools = []
    for aa in range(a_frame):
        vec = uv[aa]
        picked = (up_mask.reshape(16, 8, 128) * vec[None]).reshape(128, 128).astype(LOW)
        chosen = jnp.where(mm(picked, up_ones) == up_places, 1.0, 0.0).astype(LOW)
        ohu[aa] = chosen
        senders = mm(chosen, fx[2 * aa : 2 * aa + 4].reshape(128, 256)).astype(LOW)
        su[aa] = senders
        act, rise = silu_of(mm(senders, weight).reshape(8, 16, 256) + up_recv[aa][None])
        pools.append(jnp.sum(act, axis=0) * (1.0 / 8))
        uslope[aa] = rise.reshape(128, 256)
    up_pool = jnp.concatenate(pools, 0).astype(LOW)
    coarse = (m2_flat + mm(up_pool, weights[5])).astype(LOW)

    c_frame = 2 * a_frame
    nodes = a_frame * 16

    parents = mm(spread[...], coarse).astype(LOW)
    fine_mid = fx[1 : 1 + c_frame].reshape(c_frame * 32, 256)
    act, rise = silu_of((mm(parents, weights[6]) + mm(fine_mid, weights[7])) * 0.5)
    cot_w = mm_nt(cx[...].reshape(c_frame * 32, 256), weights[8])
    dd[0] = (cot_w * 0.5 * rise).astype(LOW).reshape(c_frame, 32, 256)
    dd[1] = act.astype(LOW).reshape(c_frame, 32, 256)

    def put_grad(index, value):
        acc_s[...] = value
        put_halves(acc_s, keep, send, index - 3, rep)

    act_own = dd[1, pl.ds(c_own, 16), 0:16].reshape(256, 256)
    delta_own = dd[0, pl.ds(c_own, 16), 0:16].reshape(256, 256)
    fine_own = fx[pl.ds(f_own, 16), 0:16].reshape(256, 256)
    cot_own = cot[...].reshape(256, 256)
    out = fine_own.astype(WIDE) + mm(act_own, weights[8])
    mesh_out[...] = out.astype(LOW).reshape(16, 16, 256)
    put_grad(8, mm_tn(act_own, cot_own))
    put_grad(7, mm_tn(fine_own, delta_own))

    child_sum = mm(gather[...], dd[0].reshape(c_frame * 32, 256))
    n_i = iota((nodes, 256), 0)
    aa_i, bb_i = n_i // 16, n_i % 16
    is_own = (aa_i >= a_own) & (aa_i < a_own + 8) & (bb_i < 8)
    is_real = (bb_i <= 8) | (bb_i == 15)
    if n_lat != 2:
        above = lat * 8 - 1 + aa_i
        is_real = is_real & (above >= 0) & (above < n_lat * 8)
    sum_high, sum_low = two_parts(child_sum)
    coarse_delta = (mm_nt(sum_high, weights[6]) + mm_nt(sum_low, weights[6])).astype(LOW)
    own_high, own_low = two_parts(jnp.where(is_own, child_sum, 0.0))
    put_grad(6, mm_tn(coarse, own_high) + mm_tn(coarse, own_low))
    own_delta = jnp.where(is_own, coarse_delta.astype(WIDE), 0.0).astype(LOW)
    put_grad(5, mm_tn(up_pool, own_delta))
    pool2 = jnp.where(is_real, mm_nt(coarse_delta, weights[5]) * (1.0 / 16), 0.0)
    own_f = jnp.where(is_own, 1.0, 0.0)
    recv[...] = jnp.zeros_like(recv)
    acc_s[...] = jnp.zeros_like(acc_s)
    node_sums = []
    for aa in range(a_frame):
        d = pool2[aa * 16 : aa * 16 + 16][None] * uslope[aa].reshape(8, 16, 256)
        mine = own_f[aa * 16 : aa * 16 + 16][None]
        up_delta = d.astype(LOW)
        wide = up_delta.astype(WIDE)
        owned = wide * mine
        node_sums.append(jnp.sum(owned, axis=0))
        back = mm_tn(ohu[aa], up_delta.reshape(128, 256)).reshape(4, 32, 256)
        recv[2 * aa : 2 * aa + 4] += back[:, 0:24]
        acc_s[...] += mm_tn(su[aa], owned.reshape(128, 256).astype(LOW))
    put_grad(3, acc_s[...])
    ns_high, ns_low = two_parts(jnp.concatenate(node_sums, 0))
    put_grad(4, mm_tn(m2_low, ns_high) + mm_tn(m2_low, ns_low))
    back_high, back_low = two_parts(recv[pl.ds(f_own, 16), 0:16].reshape(256, 256))
    fine_delta = (
        cot_own.astype(WIDE)
        + mm_nt(delta_own, weights[7])
        + mm_nt(back_high, weights[3])
        + mm_nt(back_low, weights[3])
    )
    fd_out[...] = fine_delta
    pool_out[...] = pool[pl.ds(f_own, 16), 0:16].reshape(256, 256).astype(LOW)


def back_kernel(
    m1, weights, fine_delta, pool, ssum, sx_in, slope_in, sx_edge, slope_edge, hx, hslope, mesh1_grad, keep, send, pd, acc
):
    rep = lax.axis_index("rep")
    delta_b = fine_delta[...].astype(LOW)
    pool_delta = mm_nt(delta_b, weights[2]) * (1.0 / 32)
    pd[...] = pool_delta.reshape(16, 16, 256)
    node_delta = pool_delta * ssum[0:16].reshape(256, 256)
    high, low = two_parts(node_delta)
    m1_own = m1[...].reshape(256, 256)
    grad_in = fine_delta[...] + (mm_nt(high, weights[1]) + mm_nt(low, weights[1]))
    mesh1_grad[...] = grad_in.astype(LOW).reshape(16, 16, 256)
    acc[...] = mm_tn(pool[...], delta_b)
    put_halves(acc, keep, send, 2, rep)
    acc[...] = mm_tn(m1_own, high) + mm_tn(m1_own, low)
    put_halves(acc, keep, send, 1, rep)

    def deltas_of(r, tile, rise):
        d = pd[r, tile * 8 : tile * 8 + 8][None] * rise.reshape(16, 8, 256)
        return d.reshape(128, 256).astype(LOW)

    senders, deltas = [], []
    for i, r in enumerate((0, 15)):
        senders.append(sx_edge[i].reshape(256, 256))
        for tile in range(2):
            deltas.append(deltas_of(r, tile, slope_edge[i, tile].astype(WIDE)))
    acc[...] = mm_tn(jnp.concatenate(senders, 0), jnp.concatenate(deltas, 0))
    slots = iota((128, 256), 0) % 8

    def rows(step, carry):
        senders, deltas = [], []
        for k in range(BACK_ROWS):
            r = 1 + BACK_ROWS * step + k
            halo = hx[r - 1].astype(WIDE)
            halo_rise = hslope[r - 1].astype(WIDE)
            for tile, slot in ((0, 0), (1, 7)):
                ours = slots == slot
                senders.append(jnp.where(ours, halo, sx_in[r, tile].astype(WIDE)).astype(LOW))
                deltas.append(deltas_of(r, tile, jnp.where(ours, halo_rise, slope_in[r, tile].astype(WIDE))))
        acc[...] += mm_tn(jnp.concatenate(senders, 0), jnp.concatenate(deltas, 0))
        return carry

    lax.fori_loop(0, 14 // BACK_ROWS, rows, 0)
    put_halves(acc, keep, send, 0, rep)


def block_place():
    return (lax.axis_index("lat") % 2) * 2 + lax.axis_index("lon") % 2


def quarters_kernel(kept_first, got_first, kept, got, own, *pieces):
    place = block_place()
    for step in range(4):
        rows = pl.ds(pl.multiple_of((place ^ step) * 32, 32), 32)
        for first, mine, other in ((0, kept_first, got_first), (3, kept, got)):
            total = mine[:, rows, :] + other[:, rows, :].astype(WIDE)
            at = slice(first, first + mine.shape[0])
            if step == 0:
                own[at] = total
            else:
                pieces[step - 1][at] = total.astype(LOW)


def add_kernel(*refs):
    total = refs[0][...].astype(WIDE)
    for ref in refs[1:-1]:
        total = total + ref[...].astype(WIDE)
    refs[-1][...] = total.astype(LOW)


def small_kernel(kernel, out_shape, name, *values):
    vmem = pl.BlockSpec(memory_space=pltpu.VMEM)
    return pl.pallas_call(
        kernel,
        out_shape=out_shape,
        in_specs=[vmem] * len(values),
        out_specs=jax.tree.map(lambda _: vmem, out_shape),
        compiler_params=pltpu.CompilerParams(vmem_limit_bytes=8 * 1024 * 1024),
        name=name,
    )(*values)


def spread_kernel(scale, *refs):
    pieces, (out, stage, sems) = refs[:8], refs[8:]
    rep = lax.axis_index("rep")
    place = block_place()
    copies = []
    for k in range(9):
        for step in range(4):
            at = (place ^ step) * 32
            for half, piece in ((rep, pieces[step]), (1 - rep, pieces[4 + step])):
                rows = pl.ds(pl.multiple_of(half * 128 + at, 32), 32)
                stage[k, rows, :] = piece[k].astype(WIDE) * scale
        copies.append(pltpu.make_async_copy(stage.at[k], out.at[k], sems.at[k]))
        copies[-1].start()
    for copy in copies:
        copy.wait()


def flat_main(dirs, n_lat, *refs):
    n_bands = 3 * len(dirs)
    own, refs = refs[:10], refs[10:]
    sides, refs = refs[:2], refs[2:]
    bands, refs = refs[:n_bands], refs[n_bands:]
    weights, refs = refs[0], refs[1:]
    outs, scratch = refs[:10], refs[10:]
    main_kernel(dirs, n_lat, own, sides, bands, weights, outs, scratch)


class Reduction:
    def __init__(self, mesh):
        self.sizes = (mesh.shape["lon"], mesh.shape["lat"])

    def between(self, values, lon_bit, lat_bit):
        lat_size = self.sizes[1]
        return permute(
            values,
            ("lon", "lat"),
            lambda i: ((i // lat_size) ^ lon_bit) * lat_size + ((i % lat_size) ^ lat_bit),
            self.sizes,
        )

    def siblings(self, values):
        return permute(values, "rep", lambda i: i ^ 1, (2,))

    def quarters(self, *halves):
        _, rows, cols = halves[0].shape
        shape = (9, rows // 4, cols)
        shapes = [jax.ShapeDtypeStruct(shape, WIDE)] + [jax.ShapeDtypeStruct(shape, LOW)] * 3
        return small_kernel(quarters_kernel, shapes, "quarters", *halves)

    def block(self, quarters):
        own, *others = quarters
        got = [self.between(piece, step & 1, step >> 1) for step, piece in zip((1, 2, 3), others)]
        shape = jax.ShapeDtypeStruct(own.shape, LOW)
        return small_kernel(add_kernel, shape, "block_sum", own, *got)

    def total(self, total):
        shape = jax.ShapeDtypeStruct(total.shape, LOW)
        for which, size in enumerate(self.sizes):
            bit = 2
            while bit < size:
                other = self.between(total, *((bit, 0) if which == 0 else (0, bit)))
                total = small_kernel(add_kernel, shape, "pair_sum", total, other)
                bit *= 2
        return total

    def pieces(self, own):
        mine = [own] + [self.between(own, step & 1, step >> 1) for step in (1, 2, 3)]
        return mine + [self.siblings(piece) for piece in mine]


def body(mesh, grid_state, mesh1_state, mesh2_state, grid_edges, up_edges, weights, cotangent):
    n_lat, n_lon = mesh.shape["lat"], mesh.shape["lon"]
    glon = grid_state.shape[1] * 2 * n_lon
    m1lon = mesh1_state.shape[1] * 2 * n_lon
    dirs = (None,) if n_lat == 2 else (True, False)
    vmem = pl.BlockSpec(memory_space=pltpu.VMEM)
    params = pltpu.CompilerParams(vmem_limit_bytes=VMEM_BYTES)
    shapes = [48] + [SIDE_ROWS] * 2 + [BAND_ROWS, CORNER_ROWS, CORNER_ROWS] * len(dirs)
    hbm = pl.BlockSpec(memory_space=pltpu.HBM)
    states = (grid_state, mesh1_state, cotangent, mesh2_state)
    grid_state, mesh1_state, cotangent, mesh2_state, codes, *buffers = pl.pallas_call(
        functools.partial(pack_kernel, dirs, glon, m1lon),
        out_shape=[jax.ShapeDtypeStruct(state.shape, state.dtype) for state in states]
        + [jax.ShapeDtypeStruct((n, 256), LOW) for n in shapes],
        in_specs=[hbm] * 6,
        out_specs=[vmem] * (4 + len(shapes)),
        scratch_shapes=[
            pltpu.VMEM(grid_edges.shape, grid_edges.dtype),
            pltpu.VMEM(up_edges.shape, up_edges.dtype),
            pltpu.SemaphoreType.DMA((6,)),
        ],
        compiler_params=params,
        name="pack_halos",
    )(*(in_hbm(value) for value in (*states, grid_edges, up_edges)))
    frame = 20 if n_lat == 2 else 22
    a_frame = 9 if n_lat == 2 else 10
    c_frame = 2 * a_frame
    g_frame = 2 * frame + 6
    inner = pl.pallas_call(
        inner_kernel,
        out_shape=[
            jax.ShapeDtypeStruct((16, 2, 128, 256), LOW),
            jax.ShapeDtypeStruct((16, 2, 128, 256), LOW),
            jax.ShapeDtypeStruct((16, 16, 256), WIDE),
            jax.ShapeDtypeStruct((16, 16, 256), WIDE),
            jax.ShapeDtypeStruct(weights.shape, LOW),
            jax.ShapeDtypeStruct((3, 128, 256), LOW),
            jax.ShapeDtypeStruct((c_frame * 32, a_frame * 16), LOW),
            jax.ShapeDtypeStruct((a_frame * 16, c_frame * 32), LOW),
        ],
        in_specs=[vmem] * 3 + [hbm],
        out_specs=[vmem] * 8,
        scratch_shapes=[
            pltpu.VMEM((3, 34, 16, 256), LOW),
            pltpu.VMEM((16, 16, 256), LOW),
            pltpu.VMEM((16, 16, 256), WIDE),
            pltpu.SemaphoreType.DMA((2,)),
        ],
        compiler_params=params,
        cost_estimate=pl.CostEstimate(flops=1_000_000_000, bytes_accessed=1_000, transcendentals=0),
        name="inner_rows",
    )(grid_state, mesh1_state, codes, in_hbm(weights))
    sx_in, slope_in, pool_in, ssum_in, weights, *tables = inner
    own = (grid_state, mesh1_state, cotangent, mesh2_state, codes, pool_in, ssum_in, *tables)

    def beyond(lon, core):
        return ((lon + (1 if core else -1)) % n_lon, 1 - core)

    def send_to(values, other_lat, column):
        def partner(i):
            lon, rest = divmod(i, n_lat * 2)
            row, core = divmod(rest, 2)
            row = other_lat(row)
            if row is None:
                return None
            if column == "sibling":
                core = 1 - core
            elif column == "beyond":
                lon, core = beyond(lon, core)
            return (lon * n_lat + row) * 2 + core

        return permute(values, ("lon", "lat", "rep"), partner, (n_lon, n_lat, 2))

    def shift(sends_bottom):
        if sends_bottom is None:
            return lambda row: row ^ 1
        if sends_bottom:
            return lambda row: row + 1 if row + 1 < n_lat else None
        return lambda row: row - 1 if row else None

    got_sides = [send_to(buffers[0], lambda row: row, "sibling"), send_to(buffers[1], lambda row: row, "beyond")]
    got_bands = []
    for i, sends_bottom in enumerate(dirs):
        for k, column in enumerate(("same", "sibling", "beyond")):
            got_bands.append(send_to(buffers[2 + 3 * i + k], shift(sends_bottom), column))

    scratch = [
        pltpu.VMEM((3, g_frame, 16, 256), LOW),
        pltpu.VMEM((frame, 24, 256), WIDE),
        pltpu.VMEM((frame, 24, 256), WIDE),
        pltpu.VMEM((frame, 16, 256), LOW),
        pltpu.VMEM((frame, 16, 256), LOW),
        pltpu.VMEM((a_frame, 8, 128), WIDE),
        pltpu.VMEM((frame, 24, 256), WIDE),
        pltpu.VMEM((frame, 32, 256), LOW),
        pltpu.VMEM((c_frame, 32, 256), LOW),
        pltpu.VMEM((a_frame, 16, 256), WIDE),
        pltpu.VMEM((a_frame, 128, 128), LOW),
        pltpu.VMEM((a_frame, 128, 256), LOW),
        pltpu.VMEM((a_frame, 128, 256), WIDE),
        pltpu.VMEM((2, c_frame, 32, 256), LOW),
        pltpu.VMEM((256, 256), WIDE),
    ]
    n_in = 10 + 2 + len(got_bands) + 1
    mesh_out, kept, sent, fine_delta, pool, ssum, sx_edge, slope_edge, hx, hslope = pl.pallas_call(
        functools.partial(flat_main, dirs, n_lat),
        out_shape=[
            jax.ShapeDtypeStruct(mesh1_state.shape, LOW),
            jax.ShapeDtypeStruct((6, 128, 256), WIDE),
            jax.ShapeDtypeStruct((6, 128, 256), LOW),
            jax.ShapeDtypeStruct((256, 256), WIDE),
            jax.ShapeDtypeStruct((256, 256), LOW),
            jax.ShapeDtypeStruct((17, 16, 256), WIDE),
            jax.ShapeDtypeStruct((3, 2, 128, 256), LOW),
            jax.ShapeDtypeStruct((3, 2, 128, 256), LOW),
            jax.ShapeDtypeStruct((14, 128, 256), LOW),
            jax.ShapeDtypeStruct((14, 128, 256), LOW),
        ],
        in_specs=[vmem] * n_in,
        out_specs=[vmem] * 10,
        scratch_shapes=scratch,
        compiler_params=params,
        name="sweep",
    )(*own, *got_sides, *got_bands, weights)
    reduction = Reduction(mesh)
    got = reduction.siblings(sent)
    mesh1_grad, kept_first, sent_first = pl.pallas_call(
        back_kernel,
        out_shape=[
            jax.ShapeDtypeStruct(mesh1_state.shape, LOW),
            jax.ShapeDtypeStruct((3, 128, 256), WIDE),
            jax.ShapeDtypeStruct((3, 128, 256), LOW),
        ],
        in_specs=[vmem] * 11,
        out_specs=[vmem] * 3,
        scratch_shapes=[pltpu.VMEM((16, 16, 256), WIDE), pltpu.VMEM((256, 256), WIDE)],
        compiler_params=params,
        cost_estimate=pl.CostEstimate(flops=3_000_000_000, bytes_accessed=8_000_000, transcendentals=0),
        name="encoder_back",
    )(mesh1_state, weights, fine_delta, pool, ssum, sx_in, slope_in, sx_edge, slope_edge, hx, hslope)
    node_total = mesh1_state.shape[0] * mesh1_state.shape[1] * n_lat * n_lon * 2
    scale = float(node_total) ** (-0.5)
    quarters = reduction.quarters(kept_first, reduction.siblings(sent_first), kept, got)
    pieces = reduction.pieces(reduction.total(reduction.block(quarters)))
    weight_grads = pl.pallas_call(
        functools.partial(spread_kernel, scale),
        out_shape=jax.ShapeDtypeStruct((9, 256, 256), WIDE),
        in_specs=[vmem] * 8,
        out_specs=hbm,
        scratch_shapes=[pltpu.VMEM((9, 256, 256), WIDE), pltpu.SemaphoreType.DMA((9,))],
        compiler_params=params,
        name="spread_gradients",
    )(*pieces)
    return (mesh_out, mesh1_grad, weight_grads)


def solution(mesh):
    in_specs = (
        P(("groups", "lat"), ("lon", "rep"), None),
        P(("groups", "lat"), ("lon", "rep"), None),
        P(("groups", "lat"), "lon", None),
        P(None, "lat", ("lon", "rep")),
        P(None, "lat", "lon"),
        P(),
        P(("groups", "lat"), ("lon", "rep"), None),
    )
    out_specs = (
        P(("groups", "lat"), ("lon", "rep"), None),
        P(("groups", "lat"), ("lon", "rep"), None),
        P("groups", None, None),
    )
    return jax.shard_map(
        functools.partial(body, mesh), mesh=mesh, in_specs=in_specs, out_specs=out_specs, check_vma=False
    )
```

```python
import functools

import jax
import jax.numpy as jnp
from jax import lax
from jax.experimental import pallas as pl
from jax.experimental.pallas import tpu as pltpu
from jax.sharding import PartitionSpec as P

LOW = jnp.bfloat16
WIDE = jnp.float32
VMEM_BYTES = 24 * 1024 * 1024
HALO_ROWS = 14
INNER_ROWS = 7
CODE = LOW

SIDE_ROWS = 416
BAND_ROWS = 352
CORNER_ROWS = 112


def permute(values, axes, partner, sizes):
    total = 1
    for size in sizes:
        total *= size
    pairs = [(i, partner(i)) for i in range(total)]
    return lax.ppermute(values, axes, [(i, j) for i, j in pairs if j is not None])


def mm(left, right):
    return jnp.dot(left, right, preferred_element_type=WIDE)


def mm_nt(left, right):
    return lax.dot_general(left, right, (((1,), (1,)), ((), ())), preferred_element_type=WIDE)


def mm_tn(left, right):
    return lax.dot_general(left, right, (((0,), (0,)), ((), ())), preferred_element_type=WIDE)


def two_parts(value):
    high = value.astype(LOW)
    return high, (value - high.astype(WIDE)).astype(LOW)


def silu_of(half):
    t = jnp.tanh(half)
    up = 1.0 + t
    act = half * up
    return act, up + act * (1.0 - t)


def halved(weight):
    return (weight.astype(WIDE) * 0.5).astype(LOW)


def iota(shape, dim):
    return lax.broadcasted_iota(jnp.int32, shape, dim)


def in_hbm(value):
    return pltpu.with_memory_space_constraint(value, pltpu.HBM)


def split(value, size):
    if size & (size - 1) == 0:
        return value >> (size.bit_length() - 1), value & (size - 1)
    return value // size, value % size


def wrapped(value, size):
    if size & (size - 1) == 0:
        return value & (size - 1)
    return jnp.mod(value, size)


def edge_codes(edges, glon, lat, col, rows, cols):
    row = iota(edges.shape, 0)
    lane = iota(edges.shape, 1)
    j = lane % 16
    at_row, at_col = split(edges, glon)
    down = at_row - (2 * (lat * rows + row) - 2)
    across = wrapped(at_col - (2 * (col * cols + j) - 2), glon)
    place = 2 * (j % 8) + 6 + across
    own = down * 16 + place + jnp.where(place >= 16, 112, 0)
    base = down * 16 + across + 6
    turned = jnp.where(j < 4, pltpu.roll(base, 256 - 12, 1), pltpu.roll(base, 4, 1))
    sent = turned + 2 * (j - 4) + jnp.where(j < 4, 0, 128)
    return own.astype(WIDE), sent.astype(WIDE)


def up_codes(edges, m1lon, lat, col, rep, rows, cols):
    row = iota(edges.shape, 0)
    l16 = iota(edges.shape, 1) % 16
    low = jnp.where(l16 < 8, edges, pltpu.roll(edges, 8, 1))
    high = jnp.where(l16 < 8, pltpu.roll(edges, 128 - 8, 1), edges)
    edges = jnp.where(rep == 0, low, high)
    b = l16 % 8
    at_row, at_col = split(edges, m1lon)
    down = at_row - (2 * (lat * rows + row) - 1)
    across = wrapped(at_col - (2 * (col * cols + b) - 1), m1lon)
    base = jnp.where(l16 < 8, b, jnp.where(b >= 4, b - 8, b + 8))
    at = 2 * base - 1 + across
    at = jnp.where(at < 0, at + 20, jnp.where(at >= 16, at + 4, at))
    return (down * 32 + at).astype(WIDE)


def pack_kernel(dirs, glon, m1lon, *refs):
    far, (grid, m1, cot, m2, codes), rest = refs[:6], refs[6:11], refs[11:]
    outs, (edges, ups, sems) = rest[:-3], rest[-3:]
    copies = [
        pltpu.make_async_copy(a, b, sems.at[i]) for i, (a, b) in enumerate(zip(far, (grid, m1, cot, m2, edges, ups)))
    ]
    for copy in copies:
        copy.start()
    for copy in copies[::-1]:
        copy.wait()
    rep = lax.axis_index("rep")
    lat = lax.axis_index("lat")
    col = lax.axis_index("lon") * 2 + rep
    sides = outs[:2]
    bands = outs[2:]
    flat = jnp.concatenate([edges[k] for k in range(16)], axis=1)
    own_k, sent_k = edge_codes(flat, glon, lat, col, 16, 16)
    flat = jnp.concatenate([ups[k] for k in range(8)], axis=1)
    up_k = up_codes(flat, m1lon, lat, col, rep, 8, 8)
    up_k = jnp.concatenate([up_k, jnp.zeros_like(up_k)], 1)
    codes[0:16, :] = own_k.astype(LOW)
    codes[16:32, :] = sent_k.astype(LOW)
    codes[32:48, :] = jnp.concatenate([up_k, jnp.zeros_like(up_k)], 0).astype(LOW)
    m2w = m2[...].astype(WIDE)
    m2_half = jnp.where(rep == 0, m2w[:, 0:8], m2w[:, 8:16])
    row8 = iota((8, 256), 0)

    def few(k_rows, last, ghost):
        up = jnp.where(last, up_k[7:8], up_k[0:1])
        rest = jnp.where(row8 == 3, jnp.broadcast_to(up, (8, 256)), 0.0)
        if ghost is not None:
            rest = jnp.where(row8 == 4, jnp.broadcast_to(ghost, (8, 256)), rest)
        return jnp.where(last, jnp.where(row8 >= 5, k_rows[8:16], rest), jnp.where(row8 < 3, k_rows[0:8], rest))

    def last_rows(sends_bottom):
        if sends_bottom is None:
            return lat == 0
        return jnp.bool_(sends_bottom)

    def fill(targets, right):
        side, corners = targets
        g = grid[:, 16:32, :] if right else grid[:, 0:16, :]
        g = g.astype(WIDE)[:, 8:16] if right else g.astype(WIDE)[:, 0:8]
        part = slice(12, 16) if right else slice(0, 4)
        pair = jnp.concatenate([m1[...].astype(WIDE)[:, part], cot[...].astype(WIDE)[:, part]], axis=1)
        edge = 7 if right else 0
        ghosts = jnp.zeros((8, 256), WIDE)
        for a in range(8):
            ghosts = jnp.where(row8 == a, jnp.broadcast_to(m2_half[a, edge : edge + 1], (8, 256)), ghosts)
        side[0:256, :] = g.reshape(256, 256).astype(LOW)
        side[256:384, :] = pair.reshape(128, 256).astype(LOW)
        side[384:400, :] = sent_k.astype(LOW)
        side[400:416, :] = jnp.concatenate([up_k, ghosts], 0).astype(LOW)
        for sends_bottom, corner in corners:
            last = last_rows(sends_bottom)
            corner[0:64, :] = jnp.where(last, g[24:32], g[0:8]).reshape(64, 256).astype(LOW)
            corner[64:96, :] = jnp.where(last, pair[12:16], pair[0:4]).reshape(32, 256).astype(LOW)
            block = few(sent_k, last, jnp.where(last, ghosts[7:8], ghosts[0:1]))
            corner[96:112, :] = jnp.concatenate([block, block], 0).astype(LOW)

    sib = (sides[0], [(d, bands[3 * i + 1]) for i, d in enumerate(dirs)])
    out = (sides[1], [(d, bands[3 * i + 2]) for i, d in enumerate(dirs)])

    @pl.when(rep == 0)
    def _():
        fill(sib, True)
        fill(out, False)

    @pl.when(rep == 1)
    def _():
        fill(sib, False)
        fill(out, True)

    for i, sends_bottom in enumerate(dirs):
        band = bands[3 * i]
        last = last_rows(sends_bottom)
        first = jnp.where(last, 1, 0)
        band[0:256, :] = grid[pl.ds(first * 24, 8)].reshape(256, 256)
        band[256:304, :] = m1[pl.ds(first * 13, 3)].reshape(48, 256)
        band[304:336, :] = cot[pl.ds(first * 14, 2)].reshape(32, 256)
        mt = jnp.where(last, m2_half[7], m2_half[0])
        band[336:352, :] = jnp.concatenate([few(own_k, last, None), mt], 0).astype(LOW)


def set_masks(masks):
    edge = iota((128, 256), 0)
    lanes = iota((128, 256), 1)
    slot = edge % 8
    base = (edge // 8) * 16
    masks[0] = jnp.where(lanes == base + slot, 1.0, 0.0).astype(LOW)
    masks[1] = jnp.where(lanes == base + 8 + slot, 1.0, 0.0).astype(LOW)
    masks[2] = jnp.where(lanes == base + jnp.where(slot < 7, slot, 15), 1.0, 0.0).astype(LOW)


def encode_tiles(tiles, weight):
    ones = jnp.ones((256, 256), LOW)
    places = iota((128, 256), 1).astype(WIDE).astype(CODE)
    one, zero = jnp.ones((128, 256), LOW), jnp.zeros((128, 256), LOW)
    picked = [(mask.reshape(8, 16, 256) * codes[None]).reshape(128, 256) for mask, codes, _, _ in tiles]
    found = mm(jnp.concatenate(picked, 0), ones).astype(CODE)
    senders = []
    for i, (_, _, window, _) in enumerate(tiles):
        chosen = jnp.where(found[i * 128 : i * 128 + 128] == places, one, zero)
        senders.append(mm(chosen, jnp.concatenate(window, 0)).astype(LOW))
    pre_all = mm(jnp.concatenate(senders, 0), weight)
    results = []
    for i, (_, _, _, received) in enumerate(tiles):
        act, rise = silu_of(pre_all[i * 128 : i * 128 + 128].reshape(16, 8, 256) + received[None])
        results.append(
            (senders[i], jnp.sum(act, axis=0) * (1.0 / 16), rise.reshape(128, 256).astype(LOW), jnp.sum(rise, axis=0))
        )
    return results


BLOCKS = ((0, 1), (1, 2), (0, 2))


def inner_kernel(grid, m1, codes, far, sx, slope, pool, ssum, weights, masks, spread, gather, gx, ko, recv, sems):
    first = pltpu.make_async_copy(far.at[0:2], weights.at[0:2], sems.at[0])
    others = pltpu.make_async_copy(far.at[2:9], weights.at[2:9], sems.at[1])
    first.start()
    others.start()
    set_masks(masks)

    def place_grid(step, carry):
        r = step * 8
        wide = grid[pl.ds(r, 8)].astype(WIDE)
        edge = jnp.zeros((8, 8, 256), WIDE)
        gx[0, pl.ds(r, 8)] = jnp.concatenate([edge, wide[:, 0:8]], 1).astype(LOW)
        gx[1, pl.ds(r, 8)] = wide[:, 8:24].astype(LOW)
        gx[2, pl.ds(r, 8)] = jnp.concatenate([wide[:, 24:32], edge], 1).astype(LOW)
        return carry

    lax.fori_loop(0, 4, place_grid, 0)
    gx[:, 32:34] = jnp.zeros((3, 2, 16, 256), LOW)
    own = codes[0:16, :].astype(WIDE)
    for r in range(16):
        ko[r] = jnp.broadcast_to(own[r : r + 1], (16, 256)).astype(LOW)
    first.wait()
    recv[...] = mm(m1[...].reshape(256, 256), weights[1]).reshape(16, 16, 256) * 0.5
    weight = halved(weights[0])

    def rows(step, carry):
        spots = [(1 + INNER_ROWS * step + k, tile) for k in range(INNER_ROWS) for tile in range(2)]
        tiles = []
        for r, tile in spots:
            window = [gx[blk, pl.ds(2 * r - 2, 8)].reshape(128, 256) for blk in BLOCKS[tile]]
            tiles.append((masks[tile], ko[r], window, recv[r, tile * 8 : tile * 8 + 8]))
        for (r, tile), (senders, mean, rise, total) in zip(spots, encode_tiles(tiles, weight)):
            sx[r, tile] = senders
            slope[r, tile] = rise
            pool[r, tile * 8 : tile * 8 + 8] = mean
            ssum[r, tile * 8 : tile * 8 + 8] = total
        return carry

    def family(node, state):
        q = state % 32
        slot = jnp.where(q < 16, q // 2, jnp.where((q == 18) | (q == 19), 15, jnp.where((q == 20) | (q == 21), 8, -1)))
        return jnp.where((state // 64 == node // 16) & (slot == node % 16), 1.0, 0.0).astype(LOW)

    spread[...] = family(iota(spread.shape, 1), iota(spread.shape, 0))
    gather[...] = family(iota(gather.shape, 0), iota(gather.shape, 1))
    lax.fori_loop(0, 14 // INNER_ROWS, rows, 0)
    others.wait()


def put_halves(grad, keep, send, index, rep):
    first, second = grad[0:128], grad[128:256]
    keep[index] = jnp.where(rep == 0, first, second)
    send[index] = jnp.where(rep == 0, second, first).astype(LOW)


def main_kernel(
    dirs, n_lat, own, sides, bands, weights, outs, scratch
):
    grid, m1, cot, m2, codes, pool_in, ssum_in, masks, spread, gather = own
    mesh_out, keep, send, fd_out, pool_out, ssum, sx, slope, hx, hslope = outs
    gx, m1x, recv, ko, k2, uv, pool, fx, cx, m2x, ohu, su, uslope, dd = scratch
    rep = lax.axis_index("rep")
    lat = lax.axis_index("lat")
    frame = m1x.shape[0]
    a_frame = m2x.shape[0]
    if n_lat == 2:
        g_own, f_own, c_own, a_own = 4 + 4 * lat, 1 + 2 * lat, 2 * lat, lat
        odd_rows = 5
        odd_row = lambda i: jnp.where(lat == 0, jnp.where(i == 0, 1, 15 + i), jnp.where(i < 4, i, 18))
    else:
        g_own, f_own, c_own, a_own = 8, 3, 2, 1
        odd_rows = 8
        odd_row = lambda i: jnp.where(i < 4, i, 14 + i)

    def left_right(sib, out):
        return jnp.where(rep == 1, sib, out), jnp.where(rep == 1, out, sib)

    zero_rows = jnp.zeros((4, 16, 256), LOW)
    for blk in range(3):
        gx[blk, 0:4] = zero_rows
        gx[blk, gx.shape[1] - 6 : gx.shape[1] - 2] = zero_rows
        gx[blk, gx.shape[1] - 4 :] = zero_rows

    def put_grid(at, mid, sib, out):
        n = mid.shape[0]
        left, right = left_right(sib.astype(WIDE), out.astype(WIDE))
        left = left.reshape(n, 8, 256)
        right = right.reshape(n, 8, 256)
        wide = mid.astype(WIDE)
        gx[0, pl.ds(at, n)] = jnp.concatenate([left, wide[:, 0:8]], 1).astype(LOW)
        gx[1, pl.ds(at, n)] = wide[:, 8:24].astype(LOW)
        gx[2, pl.ds(at, n)] = jnp.concatenate([wide[:, 24:32], right], 1).astype(LOW)

    def own_grid(step, carry):
        r = step * 8
        r8 = pl.multiple_of(step * 64, 64)
        put_grid(g_own + r, grid[pl.ds(r, 8)], sides[0][pl.ds(r8, 64), :], sides[1][pl.ds(r8, 64), :])
        return carry

    lax.fori_loop(0, 4, own_grid, 0)

    def put_fine(sib, out, n, mid):
        left, right = left_right(sib.astype(WIDE), out.astype(WIDE))
        left = left.reshape(n, 8, 256)
        right = right.reshape(n, 8, 256)
        slot = iota((n, 8, 256), 1)
        states = jnp.concatenate([left[:, 0:4], right[:, 0:4]], 1)
        states = jnp.where(slot == 0, mid[:, 0:8], jnp.where(slot == 7, mid[:, 8:16], states))
        cots = jnp.concatenate([left[:, 4:8], right[:, 4:8]], 1)
        return states, cots

    m1x[...] = jnp.zeros_like(m1x)
    cx[...] = jnp.zeros_like(cx)
    m1_wide = m1[...].astype(WIDE)
    states, cots = put_fine(sides[0][256:384, :], sides[1][256:384, :], 16, m1_wide)
    m1x[pl.ds(f_own, 16), 0:16] = m1_wide
    m1x[pl.ds(f_own, 16), 16:24] = states
    cx[pl.ds(c_own, 16), 0:16] = cot[...]
    cx[pl.ds(c_own, 16), 16:32] = jnp.concatenate([cots, jnp.zeros_like(cots)], 1).astype(LOW)

    def put_m2(at, mid, sib, out, n):
        left, right = left_right(sib, out)
        slot = iota((8, 256), 0)
        for a in range(n):
            l_a = jnp.broadcast_to(left[a : a + 1], (8, 256))
            r_a = jnp.broadcast_to(right[a : a + 1], (8, 256))
            ghost = jnp.where(slot == 7, l_a, jnp.where(slot == 0, r_a, 0.0))
            m2x[at + a] = jnp.concatenate([mid[a], ghost], 0)

    m2w = m2[...].astype(WIDE)
    m2_half = jnp.where(rep == 0, m2w[:, 0:8], m2w[:, 8:16])
    side_few = [side[384:416, :].astype(WIDE) for side in sides]
    put_m2(a_own, m2_half, side_few[0][24:32], side_few[1][24:32], 8)

    def codes_of(mid, sib, out):
        left, right = left_right(sib, out)
        l16 = iota(mid.shape, 1) % 16
        return jnp.where((l16 == 0) | (l16 == 15), mid, jnp.where(l16 < 4, left, right))

    def ups_of(mid, sib, out):
        left, right = left_right(sib, out)
        l16 = iota(mid.shape, 1) % 16
        return jnp.where(l16 < 8, mid, jnp.where(l16 < 12, right, left))[:, 0:128]

    def put_codes(f_at, a_at, own_rows, halo_rows, up_rows):
        for r in range(own_rows.shape[0]):
            ko[f_at + r] = jnp.broadcast_to(own_rows[r : r + 1], (16, 256)).astype(LOW)
            k2[f_at + r] = jnp.broadcast_to(halo_rows[r : r + 1], (16, 256)).astype(LOW)
        for r in range(up_rows.shape[0]):
            uv[a_at + r] = jnp.broadcast_to(up_rows[r : r + 1], (8, 128))

    own_codes = codes[...].astype(WIDE)
    put_codes(
        f_own, a_own, own_codes[0:16],
        codes_of(own_codes[0:16], side_few[0][0:16], side_few[1][0:16]),
        ups_of(own_codes[32:40], side_few[0][16:24], side_few[1][16:24]),
    )
    for i, sends_bottom in enumerate(dirs):
        band, corner_sib, corner_out = bands[3 * i : 3 * i + 3]
        if sends_bottom is None:
            top = lat
        else:
            top = 1 if sends_bottom else 0
        below = 1 - top
        put_grid(
            below * (g_own + 32), band[0:256, :].reshape(8, 32, 256), corner_sib[0:64, :], corner_out[0:64, :]
        )
        is_top = top == 1
        mids = band[256:304, :].astype(WIDE).reshape(3, 16, 256)
        mids4 = jnp.where(is_top, jnp.concatenate([mids[0:1], mids], 0), jnp.concatenate([mids, mids[2:3]], 0))
        states, cots = put_fine(corner_sib[64:96, :], corner_out[64:96, :], 4, mids4)
        f_at = below * (f_own + 16)
        c_at = below * (c_own + 16)
        a_at = below * (a_own + 8)
        m1x[pl.ds(f_at, 3), 0:16] = mids
        m1x[pl.ds(f_at, 3), 16:24] = jnp.where(is_top, states[1:4], states[0:3])
        cx[pl.ds(c_at, 2), 0:16] = band[304:336, :].reshape(2, 16, 256)
        cots = jnp.where(is_top, cots[2:4], cots[0:2])
        cx[pl.ds(c_at, 2), 16:32] = jnp.concatenate([cots, jnp.zeros_like(cots)], 1).astype(LOW)
        band_few = band[336:352, :].astype(WIDE)
        sib_few = corner_sib[96:112, :].astype(WIDE)[0:8]
        out_few = corner_out[96:112, :].astype(WIDE)[0:8]
        put_m2(a_at, band_few[8:16].reshape(1, 8, 256), sib_few[4:5], out_few[4:5], 1)
        own_k = band_few[0:8]
        halo_k = codes_of(own_k, sib_few, out_few)
        up_k = ups_of(own_k, sib_few, out_few)
        put_codes(
            f_at, a_at,
            jnp.where(is_top, own_k[5:8], own_k[0:3]),
            jnp.where(is_top, halo_k[5:8], halo_k[0:3]),
            up_k[3:4],
        )

    recv[...] = mm(m1x[...].reshape(frame * 24, 256).astype(LOW), weights[1]).reshape(frame, 24, 256) * 0.5
    weight = halved(weights[0])
    pool[...] = jnp.zeros_like(pool)

    def window_of(f, tile):
        return [gx[blk, pl.ds(2 * f, 8)].reshape(128, 256) for blk in BLOCKS[tile]]

    batch = 5 if odd_rows == 5 else 4

    def encode_rows(step, carry):
        spots = [(odd_row(step * batch + k), tile) for k in range(batch) for tile in range(3)]
        tiles = []
        for f, tile in spots:
            vec = ko[f] if tile < 2 else k2[f]
            tiles.append((masks[tile], vec, window_of(f, tile), recv[f, tile * 8 : tile * 8 + 8]))
        for (f, tile), (senders, mean, rise, total) in zip(spots, encode_tiles(tiles, weight)):
            row = f - f_own
            kept_at = jnp.where(row == 0, 0, jnp.where(row == 15, 1, 2))
            row = jnp.where(kept_at == 2, 16, row)
            pool[f, tile * 8 : tile * 8 + 8] = mean
            if tile < 2:
                sx[kept_at, tile] = senders
                slope[kept_at, tile] = rise
                ssum[row, tile * 8 : tile * 8 + 8] = total
        return carry

    lax.fori_loop(0, odd_rows // batch, encode_rows, 0)
    slots = iota((8, 256), 0)

    def encode_halo(step, carry):
        tiles = []
        for k in range(HALO_ROWS):
            f = f_own + 1 + HALO_ROWS * step + k
            tiles.append((masks[2], k2[f], window_of(f, 2), recv[f, 16:24]))
        done = encode_tiles(tiles, weight)
        for k in range(HALO_ROWS):
            r = 1 + HALO_ROWS * step + k
            f = f_own + r
            senders, mean, rise, total = done[k]
            pool[f, 16:24] = mean
            hx[r - 1] = senders
            hslope[r - 1] = rise
            for tile, slot in ((0, 0), (1, 7)):
                part = slice(tile * 8, tile * 8 + 8)
                pool[f, part] = jnp.where(slots == slot, mean, pool_in[r, part])
                ssum[r, part] = jnp.where(slots == slot, total, ssum_in[r, part])
        return carry

    lax.fori_loop(0, 14 // HALO_ROWS, encode_halo, 0)
    fine = m1x[...].reshape(frame * 24, 256) + mm(pool[...].reshape(frame * 24, 256).astype(LOW), weights[2])
    fine = fine.reshape(frame, 24, 256)
    fx[:, 0:16] = fine[:, 0:16].astype(LOW)
    fx[:, 16:32] = jnp.concatenate([fine[:, 16:24], jnp.zeros((frame, 8, 256), WIDE)], 1).astype(LOW)

    edge = iota((128, 128), 0)
    lanes = iota((128, 128), 1)
    up_mask = jnp.where(lanes == edge, 1.0, 0.0)
    up_places = lanes.astype(WIDE)
    up_ones = jnp.ones((128, 128), LOW)
    m2_flat = m2x[...].reshape(a_frame * 16, 256)
    m2_low = m2_flat.astype(LOW)
    up_recv = mm(m2_low, weights[4]).reshape(a_frame, 16, 256) * 0.5
    weight = halved(weights[3])
    pools = []
    for aa in range(a_frame):
        vec = uv[aa]
        picked = (up_mask.reshape(16, 8, 128) * vec[None]).reshape(128, 128).astype(LOW)
        chosen = jnp.where(mm(picked, up_ones) == up_places, 1.0, 0.0).astype(LOW)
        ohu[aa] = chosen
        senders = mm(chosen, fx[2 * aa : 2 * aa + 4].reshape(128, 256)).astype(LOW)
        su[aa] = senders
        act, rise = silu_of(mm(senders, weight).reshape(8, 16, 256) + up_recv[aa][None])
        pools.append(jnp.sum(act, axis=0) * (1.0 / 8))
        uslope[aa] = rise.reshape(128, 256)
    up_pool = jnp.concatenate(pools, 0).astype(LOW)
    coarse = (m2_flat + mm(up_pool, weights[5])).astype(LOW)

    c_frame = 2 * a_frame
    nodes = a_frame * 16

    parents = mm(spread[...], coarse).astype(LOW)
    fine_mid = fx[1 : 1 + c_frame].reshape(c_frame * 32, 256)
    act, rise = silu_of((mm(parents, weights[6]) + mm(fine_mid, weights[7])) * 0.5)
    cot_w = mm_nt(cx[...].reshape(c_frame * 32, 256), weights[8])
    dd[0] = (cot_w * 0.5 * rise).astype(LOW).reshape(c_frame, 32, 256)
    dd[1] = act.astype(LOW).reshape(c_frame, 32, 256)

    def put_grad(index, value):
        put_halves(value, keep, send, index - 3, rep)

    act_own = dd[1, pl.ds(c_own, 16), 0:16].reshape(256, 256)
    delta_own = dd[0, pl.ds(c_own, 16), 0:16].reshape(256, 256)
    fine_own = fx[pl.ds(f_own, 16), 0:16].reshape(256, 256)
    cot_own = cot[...].reshape(256, 256)
    out = fine_own.astype(WIDE) + mm(act_own, weights[8])
    mesh_out[...] = out.astype(LOW).reshape(16, 16, 256)
    put_grad(8, mm_tn(act_own, cot_own))
    put_grad(7, mm_tn(fine_own, delta_own))

    child_sum = mm(gather[...], dd[0].reshape(c_frame * 32, 256))
    n_i = iota((nodes, 256), 0)
    aa_i, bb_i = n_i // 16, n_i % 16
    is_own = (aa_i >= a_own) & (aa_i < a_own + 8) & (bb_i < 8)
    is_real = (bb_i <= 8) | (bb_i == 15)
    if n_lat != 2:
        above = lat * 8 - 1 + aa_i
        is_real = is_real & (above >= 0) & (above < n_lat * 8)
    sum_high, sum_low = two_parts(child_sum)
    coarse_delta = (mm_nt(sum_high, weights[6]) + mm_nt(sum_low, weights[6])).astype(LOW)
    own_high, own_low = two_parts(jnp.where(is_own, child_sum, 0.0))
    put_grad(6, mm_tn(coarse, own_high) + mm_tn(coarse, own_low))
    own_delta = jnp.where(is_own, coarse_delta.astype(WIDE), 0.0).astype(LOW)
    put_grad(5, mm_tn(up_pool, own_delta))
    pool2 = jnp.where(is_real, mm_nt(coarse_delta, weights[5]) * (1.0 / 16), 0.0)
    own_f = jnp.where(is_own, 1.0, 0.0)
    node_sums, own_deltas, backs = [], [], []
    for aa in range(a_frame):
        d = pool2[aa * 16 : aa * 16 + 16][None] * uslope[aa].reshape(8, 16, 256)
        mine = own_f[aa * 16 : aa * 16 + 16][None]
        up_delta = d.astype(LOW)
        owned = up_delta.astype(WIDE) * mine
        node_sums.append(jnp.sum(owned, axis=0))
        own_deltas.append(owned.reshape(128, 256).astype(LOW))
        backs.append(mm_tn(ohu[aa], up_delta.reshape(128, 256)).reshape(4, 32, 256))
    for pair in range(a_frame + 1):
        parts = [backs[pair][0:2]] if pair < a_frame else []
        parts += [backs[pair - 1][2:4]] if pair else []
        recv[2 * pair : 2 * pair + 2] = sum(parts[1:], parts[0])[:, 0:24]
    put_grad(3, mm_tn(su[...].reshape(a_frame * 128, 256), jnp.concatenate(own_deltas, 0)))
    ns_high, ns_low = two_parts(jnp.concatenate(node_sums, 0))
    put_grad(4, mm_tn(m2_low, ns_high) + mm_tn(m2_low, ns_low))
    back_high, back_low = two_parts(recv[pl.ds(f_own, 16), 0:16].reshape(256, 256))
    fine_delta = (
        cot_own.astype(WIDE)
        + mm_nt(delta_own, weights[7])
        + mm_nt(back_high, weights[3])
        + mm_nt(back_low, weights[3])
    )
    fd_out[...] = fine_delta
    pool_out[...] = pool[pl.ds(f_own, 16), 0:16].reshape(256, 256).astype(LOW)


def back_kernel(
    m1, weights, fine_delta, pool, ssum, sx_in, slope_in, sx_edge, slope_edge, hx, hslope, mesh1_grad, keep, send, pd
):
    rep = lax.axis_index("rep")
    delta_b = fine_delta[...].astype(LOW)
    pool_delta = mm_nt(delta_b, weights[2]) * (1.0 / 32)
    pd[...] = pool_delta.reshape(16, 16, 256)
    node_delta = pool_delta * ssum[0:16].reshape(256, 256)
    high, low = two_parts(node_delta)
    m1_own = m1[...].reshape(256, 256)
    grad_in = fine_delta[...] + (mm_nt(high, weights[1]) + mm_nt(low, weights[1]))
    mesh1_grad[...] = grad_in.astype(LOW).reshape(16, 16, 256)
    put_halves(mm_tn(pool[...], delta_b), keep, send, 2, rep)
    put_halves(mm_tn(m1_own, high) + mm_tn(m1_own, low), keep, send, 1, rep)

    def deltas_of(r, tile, rise):
        d = pd[r, tile * 8 : tile * 8 + 8][None] * rise.reshape(16, 8, 256)
        return d.reshape(128, 256).astype(LOW)

    senders, deltas = [], []
    for i, r in enumerate((0, 15)):
        senders.append(sx_edge[i].reshape(256, 256))
        for tile in range(2):
            deltas.append(deltas_of(r, tile, slope_edge[i, tile].astype(WIDE)))
    slots = iota((128, 256), 0) % 8
    for r in range(1, 15):
        halo = hx[r - 1].astype(WIDE)
        halo_rise = hslope[r - 1].astype(WIDE)
        for tile, slot in ((0, 0), (1, 7)):
            ours = slots == slot
            senders.append(jnp.where(ours, halo, sx_in[r, tile].astype(WIDE)).astype(LOW))
            deltas.append(deltas_of(r, tile, jnp.where(ours, halo_rise, slope_in[r, tile].astype(WIDE))))
    put_halves(mm_tn(jnp.concatenate(senders, 0), jnp.concatenate(deltas, 0)), keep, send, 0, rep)


def block_place():
    return (lax.axis_index("lat") % 2) * 2 + lax.axis_index("lon") % 2


def quarters_kernel(kept_first, got_first, kept, got, own, *pieces):
    place = block_place()
    for step in range(4):
        rows = pl.ds(pl.multiple_of((place ^ step) * 32, 32), 32)
        for first, mine, other in ((0, kept_first, got_first), (3, kept, got)):
            total = mine[:, rows, :] + other[:, rows, :].astype(WIDE)
            at = slice(first, first + mine.shape[0])
            if step == 0:
                own[at] = total
            else:
                pieces[step - 1][at] = total.astype(LOW)


def add_kernel(*refs):
    total = refs[0][...].astype(WIDE)
    for ref in refs[1:-1]:
        total = total + ref[...].astype(WIDE)
    refs[-1][...] = total.astype(LOW)


def small_kernel(kernel, out_shape, name, *values):
    vmem = pl.BlockSpec(memory_space=pltpu.VMEM)
    return pl.pallas_call(
        kernel,
        out_shape=out_shape,
        in_specs=[vmem] * len(values),
        out_specs=jax.tree.map(lambda _: vmem, out_shape),
        compiler_params=pltpu.CompilerParams(vmem_limit_bytes=8 * 1024 * 1024),
        name=name,
    )(*values)


def spread_kernel(scale, own, *refs):
    pieces, (out, stage, sems) = refs[:4], refs[-3:]
    rep = lax.axis_index("rep")
    place = block_place()
    half = pl.multiple_of((rep if own else 1 - rep) * 128, 128)
    copies = []
    for k in range(9):
        for step in range(4):
            rows = pl.ds(pl.multiple_of((place ^ step) * 32, 32), 32)
            stage[k, rows, :] = pieces[step][k].astype(WIDE) * scale
        copies.append(pltpu.make_async_copy(stage.at[k], out.at[k, pl.ds(half, 128)], sems.at[k]))
        copies[-1].start()
    for copy in copies:
        copy.wait()


def flat_main(dirs, n_lat, *refs):
    n_bands = 3 * len(dirs)
    own, refs = refs[:10], refs[10:]
    sides, refs = refs[:2], refs[2:]
    bands, refs = refs[:n_bands], refs[n_bands:]
    weights, refs = refs[0], refs[1:]
    outs, scratch = refs[:10], refs[10:]
    main_kernel(dirs, n_lat, own, sides, bands, weights, outs, scratch)


class Reduction:
    def __init__(self, mesh):
        self.sizes = (mesh.shape["lon"], mesh.shape["lat"])

    def between(self, values, lon_bit, lat_bit):
        lat_size = self.sizes[1]
        return permute(
            values,
            ("lon", "lat"),
            lambda i: ((i // lat_size) ^ lon_bit) * lat_size + ((i % lat_size) ^ lat_bit),
            self.sizes,
        )

    def siblings(self, values):
        return permute(values, "rep", lambda i: i ^ 1, (2,))

    def quarters(self, *halves):
        _, rows, cols = halves[0].shape
        shape = (9, rows // 4, cols)
        shapes = [jax.ShapeDtypeStruct(shape, WIDE)] + [jax.ShapeDtypeStruct(shape, LOW)] * 3
        return small_kernel(quarters_kernel, shapes, "quarters", *halves)

    def block(self, quarters):
        own, *others = quarters
        got = [self.between(piece, step & 1, step >> 1) for step, piece in zip((1, 2, 3), others)]
        shape = jax.ShapeDtypeStruct(own.shape, LOW)
        return small_kernel(add_kernel, shape, "block_sum", own, *got)

    def total(self, total):
        shape = jax.ShapeDtypeStruct(total.shape, LOW)
        for which, size in enumerate(self.sizes):
            bit = 2
            while bit < size:
                other = self.between(total, *((bit, 0) if which == 0 else (0, bit)))
                total = small_kernel(add_kernel, shape, "pair_sum", total, other)
                bit *= 2
        return total

    def pieces(self, own):
        mine = [own] + [self.between(own, step & 1, step >> 1) for step in (1, 2, 3)]
        return mine + [self.siblings(piece) for piece in mine]


def body(mesh, grid_state, mesh1_state, mesh2_state, grid_edges, up_edges, weights, cotangent):
    n_lat, n_lon = mesh.shape["lat"], mesh.shape["lon"]
    glon = grid_state.shape[1] * 2 * n_lon
    m1lon = mesh1_state.shape[1] * 2 * n_lon
    dirs = (None,) if n_lat == 2 else (True, False)
    vmem = pl.BlockSpec(memory_space=pltpu.VMEM)
    params = pltpu.CompilerParams(vmem_limit_bytes=VMEM_BYTES)
    shapes = [48] + [SIDE_ROWS] * 2 + [BAND_ROWS, CORNER_ROWS, CORNER_ROWS] * len(dirs)
    hbm = pl.BlockSpec(memory_space=pltpu.HBM)
    states = (grid_state, mesh1_state, cotangent, mesh2_state)
    grid_state, mesh1_state, cotangent, mesh2_state, codes, *buffers = pl.pallas_call(
        functools.partial(pack_kernel, dirs, glon, m1lon),
        out_shape=[jax.ShapeDtypeStruct(state.shape, state.dtype) for state in states]
        + [jax.ShapeDtypeStruct((n, 256), LOW) for n in shapes],
        in_specs=[hbm] * 6,
        out_specs=[vmem] * (4 + len(shapes)),
        scratch_shapes=[
            pltpu.VMEM(grid_edges.shape, grid_edges.dtype),
            pltpu.VMEM(up_edges.shape, up_edges.dtype),
            pltpu.SemaphoreType.DMA((6,)),
        ],
        compiler_params=params,
        name="pack_halos",
    )(*(in_hbm(value) for value in (*states, grid_edges, up_edges)))
    frame = 20 if n_lat == 2 else 22
    a_frame = 9 if n_lat == 2 else 10
    c_frame = 2 * a_frame
    g_frame = 2 * frame + 6
    inner = pl.pallas_call(
        inner_kernel,
        out_shape=[
            jax.ShapeDtypeStruct((16, 2, 128, 256), LOW),
            jax.ShapeDtypeStruct((16, 2, 128, 256), LOW),
            jax.ShapeDtypeStruct((16, 16, 256), WIDE),
            jax.ShapeDtypeStruct((16, 16, 256), WIDE),
            jax.ShapeDtypeStruct(weights.shape, LOW),
            jax.ShapeDtypeStruct((3, 128, 256), LOW),
            jax.ShapeDtypeStruct((c_frame * 32, a_frame * 16), LOW),
            jax.ShapeDtypeStruct((a_frame * 16, c_frame * 32), LOW),
        ],
        in_specs=[vmem] * 3 + [hbm],
        out_specs=[vmem] * 8,
        scratch_shapes=[
            pltpu.VMEM((3, 34, 16, 256), LOW),
            pltpu.VMEM((16, 16, 256), LOW),
            pltpu.VMEM((16, 16, 256), WIDE),
            pltpu.SemaphoreType.DMA((2,)),
        ],
        compiler_params=params,
        cost_estimate=pl.CostEstimate(flops=1_000_000_000, bytes_accessed=1_000, transcendentals=0),
        name="inner_rows",
    )(grid_state, mesh1_state, codes, in_hbm(weights))
    sx_in, slope_in, pool_in, ssum_in, weights, *tables = inner
    own = (grid_state, mesh1_state, cotangent, mesh2_state, codes, pool_in, ssum_in, *tables)

    def beyond(lon, core):
        return ((lon + (1 if core else -1)) % n_lon, 1 - core)

    def send_to(values, other_lat, column):
        def partner(i):
            lon, rest = divmod(i, n_lat * 2)
            row, core = divmod(rest, 2)
            row = other_lat(row)
            if row is None:
                return None
            if column == "sibling":
                core = 1 - core
            elif column == "beyond":
                lon, core = beyond(lon, core)
            return (lon * n_lat + row) * 2 + core

        return permute(values, ("lon", "lat", "rep"), partner, (n_lon, n_lat, 2))

    def shift(sends_bottom):
        if sends_bottom is None:
            return lambda row: row ^ 1
        if sends_bottom:
            return lambda row: row + 1 if row + 1 < n_lat else None
        return lambda row: row - 1 if row else None

    got_sides = [send_to(buffers[0], lambda row: row, "sibling"), send_to(buffers[1], lambda row: row, "beyond")]
    got_bands = []
    for i, sends_bottom in enumerate(dirs):
        for k, column in enumerate(("same", "sibling", "beyond")):
            got_bands.append(send_to(buffers[2 + 3 * i + k], shift(sends_bottom), column))

    scratch = [
        pltpu.VMEM((3, g_frame, 16, 256), LOW),
        pltpu.VMEM((frame, 24, 256), WIDE),
        pltpu.VMEM((frame, 24, 256), WIDE),
        pltpu.VMEM((frame, 16, 256), LOW),
        pltpu.VMEM((frame, 16, 256), LOW),
        pltpu.VMEM((a_frame, 8, 128), WIDE),
        pltpu.VMEM((frame, 24, 256), WIDE),
        pltpu.VMEM((frame, 32, 256), LOW),
        pltpu.VMEM((c_frame, 32, 256), LOW),
        pltpu.VMEM((a_frame, 16, 256), WIDE),
        pltpu.VMEM((a_frame, 128, 128), LOW),
        pltpu.VMEM((a_frame, 128, 256), LOW),
        pltpu.VMEM((a_frame, 128, 256), WIDE),
        pltpu.VMEM((2, c_frame, 32, 256), LOW),
    ]
    n_in = 10 + 2 + len(got_bands) + 1
    mesh_out, kept, sent, fine_delta, pool, ssum, sx_edge, slope_edge, hx, hslope = pl.pallas_call(
        functools.partial(flat_main, dirs, n_lat),
        out_shape=[
            jax.ShapeDtypeStruct(mesh1_state.shape, LOW),
            jax.ShapeDtypeStruct((6, 128, 256), WIDE),
            jax.ShapeDtypeStruct((6, 128, 256), LOW),
            jax.ShapeDtypeStruct((256, 256), WIDE),
            jax.ShapeDtypeStruct((256, 256), LOW),
            jax.ShapeDtypeStruct((17, 16, 256), WIDE),
            jax.ShapeDtypeStruct((3, 2, 128, 256), LOW),
            jax.ShapeDtypeStruct((3, 2, 128, 256), LOW),
            jax.ShapeDtypeStruct((14, 128, 256), LOW),
            jax.ShapeDtypeStruct((14, 128, 256), LOW),
        ],
        in_specs=[vmem] * n_in,
        out_specs=[vmem] * 10,
        scratch_shapes=scratch,
        compiler_params=params,
        name="sweep",
    )(*own, *got_sides, *got_bands, weights)
    reduction = Reduction(mesh)
    got = reduction.siblings(sent)
    mesh1_grad, kept_first, sent_first = pl.pallas_call(
        back_kernel,
        out_shape=[
            jax.ShapeDtypeStruct(mesh1_state.shape, LOW),
            jax.ShapeDtypeStruct((3, 128, 256), WIDE),
            jax.ShapeDtypeStruct((3, 128, 256), LOW),
        ],
        in_specs=[vmem] * 11,
        out_specs=[vmem] * 3,
        scratch_shapes=[pltpu.VMEM((16, 16, 256), WIDE)],
        compiler_params=params,
        cost_estimate=pl.CostEstimate(flops=3_000_000_000, bytes_accessed=8_000_000, transcendentals=0),
        name="encoder_back",
    )(mesh1_state, weights, fine_delta, pool, ssum, sx_in, slope_in, sx_edge, slope_edge, hx, hslope)
    node_total = mesh1_state.shape[0] * mesh1_state.shape[1] * n_lat * n_lon * 2
    scale = float(node_total) ** (-0.5)
    quarters = reduction.quarters(kept_first, reduction.siblings(sent_first), kept, got)
    pieces = reduction.pieces(reduction.total(reduction.block(quarters)))
    weight_grads = None
    for own in (True, False):
        before = [] if own else [weight_grads]
        weight_grads = pl.pallas_call(
            functools.partial(spread_kernel, scale, own),
            out_shape=jax.ShapeDtypeStruct((9, 256, 256), WIDE),
            in_specs=[vmem] * 4 + [hbm] * len(before),
            out_specs=hbm,
            scratch_shapes=[pltpu.VMEM((9, 128, 256), WIDE), pltpu.SemaphoreType.DMA((9,))],
            input_output_aliases={} if own else {4: 0},
            compiler_params=pltpu.CompilerParams(vmem_limit_bytes=8 * 1024 * 1024),
            name="spread_own" if own else "spread_other",
        )(*(pieces[:4] if own else pieces[4:]), *before)
    return (mesh_out, mesh1_grad, weight_grads)


def solution(mesh):
    in_specs = (
        P(("groups", "lat"), ("lon", "rep"), None),
        P(("groups", "lat"), ("lon", "rep"), None),
        P(("groups", "lat"), "lon", None),
        P(None, "lat", ("lon", "rep")),
        P(None, "lat", "lon"),
        P(),
        P(("groups", "lat"), ("lon", "rep"), None),
    )
    out_specs = (
        P(("groups", "lat"), ("lon", "rep"), None),
        P(("groups", "lat"), ("lon", "rep"), None),
        P("groups", None, None),
    )
    return jax.shard_map(
        functools.partial(body, mesh), mesh=mesh, in_specs=in_specs, out_specs=out_specs, check_vma=False
    )
```

```python
import functools

import jax
import jax.numpy as jnp
from jax import lax
from jax.experimental import pallas as pl
from jax.experimental.pallas import tpu as pltpu
from jax.sharding import PartitionSpec as P

LOW = jnp.bfloat16
WIDE = jnp.float32
VMEM_BYTES = 24 * 1024 * 1024
HALO_ROWS = 14
INNER_ROWS = 7
CODE = LOW

SIDE_ROWS = 416
BAND_ROWS = 352
CORNER_ROWS = 112


def permute(values, axes, partner, sizes):
    total = 1
    for size in sizes:
        total *= size
    pairs = [(i, partner(i)) for i in range(total)]
    return lax.ppermute(values, axes, [(i, j) for i, j in pairs if j is not None])


def mm(left, right):
    return jnp.dot(left, right, preferred_element_type=WIDE)


def mm_nt(left, right):
    return lax.dot_general(left, right, (((1,), (1,)), ((), ())), preferred_element_type=WIDE)


def mm_tn(left, right):
    return lax.dot_general(left, right, (((0,), (0,)), ((), ())), preferred_element_type=WIDE)


def two_parts(value):
    high = value.astype(LOW)
    return high, (value - high.astype(WIDE)).astype(LOW)


def silu_of(half):
    t = jnp.tanh(half)
    up = 1.0 + t
    act = half * up
    return act, up + act * (1.0 - t)


def halved(weight):
    return (weight.astype(WIDE) * 0.5).astype(LOW)


def iota(shape, dim):
    return lax.broadcasted_iota(jnp.int32, shape, dim)


def in_hbm(value):
    return pltpu.with_memory_space_constraint(value, pltpu.HBM)


def split(value, size):
    if size & (size - 1) == 0:
        return value >> (size.bit_length() - 1), value & (size - 1)
    return value // size, value % size


def wrapped(value, size):
    if size & (size - 1) == 0:
        return value & (size - 1)
    return jnp.mod(value, size)


def edge_codes(edges, glon, lat, col, rows, cols):
    row = iota(edges.shape, 0)
    lane = iota(edges.shape, 1)
    j = lane % 16
    at_row, at_col = split(edges, glon)
    down = at_row - (2 * (lat * rows + row) - 2)
    across = wrapped(at_col - (2 * (col * cols + j) - 2), glon)
    place = 2 * (j % 8) + 6 + across
    own = down * 16 + place + jnp.where(place >= 16, 112, 0)
    base = down * 16 + across + 6
    turned = jnp.where(j < 4, pltpu.roll(base, 256 - 12, 1), pltpu.roll(base, 4, 1))
    sent = turned + 2 * (j - 4) + jnp.where(j < 4, 0, 128)
    return own.astype(WIDE), sent.astype(WIDE)


def up_codes(edges, m1lon, lat, col, rep, rows, cols):
    row = iota(edges.shape, 0)
    l16 = iota(edges.shape, 1) % 16
    low = jnp.where(l16 < 8, edges, pltpu.roll(edges, 8, 1))
    high = jnp.where(l16 < 8, pltpu.roll(edges, 128 - 8, 1), edges)
    edges = jnp.where(rep == 0, low, high)
    b = l16 % 8
    at_row, at_col = split(edges, m1lon)
    down = at_row - (2 * (lat * rows + row) - 1)
    across = wrapped(at_col - (2 * (col * cols + b) - 1), m1lon)
    base = jnp.where(l16 < 8, b, jnp.where(b >= 4, b - 8, b + 8))
    at = 2 * base - 1 + across
    at = jnp.where(at < 0, at + 20, jnp.where(at >= 16, at + 4, at))
    return (down * 32 + at).astype(WIDE)


def pack_kernel(dirs, glon, m1lon, *refs):
    far, (grid, m1, cot, m2, codes), rest = refs[:6], refs[6:11], refs[11:]
    outs, (edges, ups, sems) = rest[:-3], rest[-3:]
    copies = [
        pltpu.make_async_copy(a, b, sems.at[i]) for i, (a, b) in enumerate(zip(far, (grid, m1, cot, m2, edges, ups)))
    ]
    for copy in copies:
        copy.start()
    for copy in copies[::-1]:
        copy.wait()
    rep = lax.axis_index("rep")
    lat = lax.axis_index("lat")
    col = lax.axis_index("lon") * 2 + rep
    sides = outs[:2]
    bands = outs[2:]
    flat = jnp.concatenate([edges[k] for k in range(16)], axis=1)
    own_k, sent_k = edge_codes(flat, glon, lat, col, 16, 16)
    flat = jnp.concatenate([ups[k] for k in range(8)], axis=1)
    up_k = up_codes(flat, m1lon, lat, col, rep, 8, 8)
    up_k = jnp.concatenate([up_k, jnp.zeros_like(up_k)], 1)
    codes[0:16, :] = own_k.astype(LOW)
    codes[16:32, :] = sent_k.astype(LOW)
    codes[32:48, :] = jnp.concatenate([up_k, jnp.zeros_like(up_k)], 0).astype(LOW)
    m2w = m2[...].astype(WIDE)
    m2_half = jnp.where(rep == 0, m2w[:, 0:8], m2w[:, 8:16])
    row8 = iota((8, 256), 0)

    def few(k_rows, last, ghost):
        up = jnp.where(last, up_k[7:8], up_k[0:1])
        rest = jnp.where(row8 == 3, jnp.broadcast_to(up, (8, 256)), 0.0)
        if ghost is not None:
            rest = jnp.where(row8 == 4, jnp.broadcast_to(ghost, (8, 256)), rest)
        return jnp.where(last, jnp.where(row8 >= 5, k_rows[8:16], rest), jnp.where(row8 < 3, k_rows[0:8], rest))

    def last_rows(sends_bottom):
        if sends_bottom is None:
            return lat == 0
        return jnp.bool_(sends_bottom)

    def fill(targets, right):
        side, corners = targets
        g = grid[:, 16:32, :] if right else grid[:, 0:16, :]
        g = g.astype(WIDE)[:, 8:16] if right else g.astype(WIDE)[:, 0:8]
        part = slice(12, 16) if right else slice(0, 4)
        pair = jnp.concatenate([m1[...].astype(WIDE)[:, part], cot[...].astype(WIDE)[:, part]], axis=1)
        edge = 7 if right else 0
        ghosts = jnp.zeros((8, 256), WIDE)
        for a in range(8):
            ghosts = jnp.where(row8 == a, jnp.broadcast_to(m2_half[a, edge : edge + 1], (8, 256)), ghosts)
        side[0:256, :] = g.reshape(256, 256).astype(LOW)
        side[256:384, :] = pair.reshape(128, 256).astype(LOW)
        side[384:400, :] = sent_k.astype(LOW)
        side[400:416, :] = jnp.concatenate([up_k, ghosts], 0).astype(LOW)
        for sends_bottom, corner in corners:
            last = last_rows(sends_bottom)
            corner[0:64, :] = jnp.where(last, g[24:32], g[0:8]).reshape(64, 256).astype(LOW)
            corner[64:96, :] = jnp.where(last, pair[12:16], pair[0:4]).reshape(32, 256).astype(LOW)
            block = few(sent_k, last, jnp.where(last, ghosts[7:8], ghosts[0:1]))
            corner[96:112, :] = jnp.concatenate([block, block], 0).astype(LOW)

    sib = (sides[0], [(d, bands[3 * i + 1]) for i, d in enumerate(dirs)])
    out = (sides[1], [(d, bands[3 * i + 2]) for i, d in enumerate(dirs)])

    @pl.when(rep == 0)
    def _():
        fill(sib, True)
        fill(out, False)

    @pl.when(rep == 1)
    def _():
        fill(sib, False)
        fill(out, True)

    for i, sends_bottom in enumerate(dirs):
        band = bands[3 * i]
        last = last_rows(sends_bottom)
        first = jnp.where(last, 1, 0)
        band[0:256, :] = grid[pl.ds(first * 24, 8)].reshape(256, 256)
        band[256:304, :] = m1[pl.ds(first * 13, 3)].reshape(48, 256)
        band[304:336, :] = cot[pl.ds(first * 14, 2)].reshape(32, 256)
        mt = jnp.where(last, m2_half[7], m2_half[0])
        band[336:352, :] = jnp.concatenate([few(own_k, last, None), mt], 0).astype(LOW)


def set_masks(masks):
    edge = iota((128, 256), 0)
    lanes = iota((128, 256), 1)
    slot = edge % 8
    base = (edge // 8) * 16
    masks[0] = jnp.where(lanes == base + slot, 1.0, 0.0).astype(LOW)
    masks[1] = jnp.where(lanes == base + 8 + slot, 1.0, 0.0).astype(LOW)
    masks[2] = jnp.where(lanes == base + jnp.where(slot < 7, slot, 15), 1.0, 0.0).astype(LOW)


def encode_tiles(tiles, weight):
    ones = jnp.ones((256, 256), LOW)
    places = iota((128, 256), 1).astype(WIDE).astype(CODE)
    one, zero = jnp.ones((128, 256), LOW), jnp.zeros((128, 256), LOW)
    picked = [(mask.reshape(8, 16, 256) * codes[None]).reshape(128, 256) for mask, codes, _, _ in tiles]
    found = mm(jnp.concatenate(picked, 0), ones).astype(CODE)
    senders = []
    for i, (_, _, window, _) in enumerate(tiles):
        chosen = jnp.where(found[i * 128 : i * 128 + 128] == places, one, zero)
        senders.append(mm(chosen, jnp.concatenate(window, 0)).astype(LOW))
    pre_all = mm(jnp.concatenate(senders, 0), weight)
    results = []
    for i, (_, _, _, received) in enumerate(tiles):
        act, rise = silu_of(pre_all[i * 128 : i * 128 + 128].reshape(16, 8, 256) + received[None])
        results.append(
            (senders[i], jnp.sum(act, axis=0) * (1.0 / 16), rise.reshape(128, 256).astype(LOW), jnp.sum(rise, axis=0))
        )
    return results


BLOCKS = ((0, 1), (1, 2), (0, 2))


def inner_kernel(grid, m1, codes, far, sx, slope, pool, ssum, weights, masks, spread, gather, gx, ko, recv, sems):
    first = pltpu.make_async_copy(far.at[0:2], weights.at[0:2], sems.at[0])
    others = pltpu.make_async_copy(far.at[2:9], weights.at[2:9], sems.at[1])
    first.start()
    others.start()
    set_masks(masks)

    def place_grid(step, carry):
        r = step * 8
        wide = grid[pl.ds(r, 8)].astype(WIDE)
        edge = jnp.zeros((8, 8, 256), WIDE)
        gx[0, pl.ds(r, 8)] = jnp.concatenate([edge, wide[:, 0:8]], 1).astype(LOW)
        gx[1, pl.ds(r, 8)] = wide[:, 8:24].astype(LOW)
        gx[2, pl.ds(r, 8)] = jnp.concatenate([wide[:, 24:32], edge], 1).astype(LOW)
        return carry

    lax.fori_loop(0, 4, place_grid, 0)
    gx[:, 32:34] = jnp.zeros((3, 2, 16, 256), LOW)
    own = codes[0:16, :].astype(WIDE)
    for r in range(16):
        ko[r] = jnp.broadcast_to(own[r : r + 1], (16, 256)).astype(LOW)
    first.wait()
    recv[...] = mm(m1[...].reshape(256, 256), weights[1]).reshape(16, 16, 256) * 0.5
    weight = halved(weights[0])

    def rows(step, carry):
        spots = [(1 + INNER_ROWS * step + k, tile) for k in range(INNER_ROWS) for tile in range(2)]
        tiles = []
        for r, tile in spots:
            window = [gx[blk, pl.ds(2 * r - 2, 8)].reshape(128, 256) for blk in BLOCKS[tile]]
            tiles.append((masks[tile], ko[r], window, recv[r, tile * 8 : tile * 8 + 8]))
        for (r, tile), (senders, mean, rise, total) in zip(spots, encode_tiles(tiles, weight)):
            sx[r, tile] = senders
            slope[r, tile] = rise
            pool[r, tile * 8 : tile * 8 + 8] = mean
            ssum[r, tile * 8 : tile * 8 + 8] = total
        return carry

    def family(node, state):
        q = state % 32
        slot = jnp.where(q < 16, q // 2, jnp.where((q == 18) | (q == 19), 15, jnp.where((q == 20) | (q == 21), 8, -1)))
        return jnp.where((state // 64 == node // 16) & (slot == node % 16), 1.0, 0.0).astype(LOW)

    spread[...] = family(iota(spread.shape, 1), iota(spread.shape, 0))
    gather[...] = family(iota(gather.shape, 0), iota(gather.shape, 1))
    lax.fori_loop(0, 14 // INNER_ROWS, rows, 0)
    others.wait()


def put_halves(grad, keep, send, index, rep):
    first, second = grad[0:128], grad[128:256]
    keep[index] = jnp.where(rep == 0, first, second)
    send[index] = jnp.where(rep == 0, second, first).astype(LOW)


def main_kernel(
    dirs, n_lat, own, sides, bands, weights, outs, scratch
):
    grid, m1, cot, m2, codes, pool_in, ssum_in, masks, spread, gather = own
    mesh_out, keep, send, fd_out, pool_out, ssum, sx, slope, hx, hslope = outs
    gx, m1x, recv, ko, k2, uv, pool, fx, cx, m2x, ohu, su, uslope, dd = scratch
    rep = lax.axis_index("rep")
    lat = lax.axis_index("lat")
    frame = m1x.shape[0]
    a_frame = m2x.shape[0]
    if n_lat == 2:
        g_own, f_own, c_own, a_own = 4 + 4 * lat, 1 + 2 * lat, 2 * lat, lat
        odd_rows = 5
        odd_row = lambda i: jnp.where(lat == 0, jnp.where(i == 0, 1, 15 + i), jnp.where(i < 4, i, 18))
    else:
        g_own, f_own, c_own, a_own = 8, 3, 2, 1
        odd_rows = 8
        odd_row = lambda i: jnp.where(i < 4, i, 14 + i)

    def left_right(sib, out):
        return jnp.where(rep == 1, sib, out), jnp.where(rep == 1, out, sib)

    zero_rows = jnp.zeros((4, 16, 256), LOW)
    for blk in range(3):
        gx[blk, 0:4] = zero_rows
        gx[blk, gx.shape[1] - 6 : gx.shape[1] - 2] = zero_rows
        gx[blk, gx.shape[1] - 4 :] = zero_rows

    def put_grid(at, mid, sib, out):
        n = mid.shape[0]
        left, right = left_right(sib.astype(WIDE), out.astype(WIDE))
        left = left.reshape(n, 8, 256)
        right = right.reshape(n, 8, 256)
        wide = mid.astype(WIDE)
        gx[0, pl.ds(at, n)] = jnp.concatenate([left, wide[:, 0:8]], 1).astype(LOW)
        gx[1, pl.ds(at, n)] = wide[:, 8:24].astype(LOW)
        gx[2, pl.ds(at, n)] = jnp.concatenate([wide[:, 24:32], right], 1).astype(LOW)

    def own_grid(step, carry):
        r = step * 8
        r8 = pl.multiple_of(step * 64, 64)
        put_grid(g_own + r, grid[pl.ds(r, 8)], sides[0][pl.ds(r8, 64), :], sides[1][pl.ds(r8, 64), :])
        return carry

    lax.fori_loop(0, 4, own_grid, 0)

    def put_fine(sib, out, n, mid):
        left, right = left_right(sib.astype(WIDE), out.astype(WIDE))
        left = left.reshape(n, 8, 256)
        right = right.reshape(n, 8, 256)
        slot = iota((n, 8, 256), 1)
        states = jnp.concatenate([left[:, 0:4], right[:, 0:4]], 1)
        states = jnp.where(slot == 0, mid[:, 0:8], jnp.where(slot == 7, mid[:, 8:16], states))
        cots = jnp.concatenate([left[:, 4:8], right[:, 4:8]], 1)
        return states, cots

    m1x[...] = jnp.zeros_like(m1x)
    cx[...] = jnp.zeros_like(cx)
    m1_wide = m1[...].astype(WIDE)
    states, cots = put_fine(sides[0][256:384, :], sides[1][256:384, :], 16, m1_wide)
    m1x[pl.ds(f_own, 16), 0:16] = m1_wide
    m1x[pl.ds(f_own, 16), 16:24] = states
    cx[pl.ds(c_own, 16), 0:16] = cot[...]
    cx[pl.ds(c_own, 16), 16:32] = jnp.concatenate([cots, jnp.zeros_like(cots)], 1).astype(LOW)

    def put_m2(at, mid, sib, out, n):
        left, right = left_right(sib, out)
        slot = iota((8, 256), 0)
        for a in range(n):
            l_a = jnp.broadcast_to(left[a : a + 1], (8, 256))
            r_a = jnp.broadcast_to(right[a : a + 1], (8, 256))
            ghost = jnp.where(slot == 7, l_a, jnp.where(slot == 0, r_a, 0.0))
            m2x[at + a] = jnp.concatenate([mid[a], ghost], 0)

    m2w = m2[...].astype(WIDE)
    m2_half = jnp.where(rep == 0, m2w[:, 0:8], m2w[:, 8:16])
    side_few = [side[384:416, :].astype(WIDE) for side in sides]
    put_m2(a_own, m2_half, side_few[0][24:32], side_few[1][24:32], 8)

    def codes_of(mid, sib, out):
        left, right = left_right(sib, out)
        l16 = iota(mid.shape, 1) % 16
        return jnp.where((l16 == 0) | (l16 == 15), mid, jnp.where(l16 < 4, left, right))

    def ups_of(mid, sib, out):
        left, right = left_right(sib, out)
        l16 = iota(mid.shape, 1) % 16
        return jnp.where(l16 < 8, mid, jnp.where(l16 < 12, right, left))[:, 0:128]

    def put_codes(f_at, a_at, own_rows, halo_rows, up_rows):
        for r in range(own_rows.shape[0]):
            ko[f_at + r] = jnp.broadcast_to(own_rows[r : r + 1], (16, 256)).astype(LOW)
            k2[f_at + r] = jnp.broadcast_to(halo_rows[r : r + 1], (16, 256)).astype(LOW)
        for r in range(up_rows.shape[0]):
            uv[a_at + r] = jnp.broadcast_to(up_rows[r : r + 1], (16, 128)).astype(LOW)

    own_codes = codes[...].astype(WIDE)
    put_codes(
        f_own, a_own, own_codes[0:16],
        codes_of(own_codes[0:16], side_few[0][0:16], side_few[1][0:16]),
        ups_of(own_codes[32:40], side_few[0][16:24], side_few[1][16:24]),
    )
    for i, sends_bottom in enumerate(dirs):
        band, corner_sib, corner_out = bands[3 * i : 3 * i + 3]
        if sends_bottom is None:
            top = lat
        else:
            top = 1 if sends_bottom else 0
        below = 1 - top
        put_grid(
            below * (g_own + 32), band[0:256, :].reshape(8, 32, 256), corner_sib[0:64, :], corner_out[0:64, :]
        )
        is_top = top == 1
        mids = band[256:304, :].astype(WIDE).reshape(3, 16, 256)
        mids4 = jnp.where(is_top, jnp.concatenate([mids[0:1], mids], 0), jnp.concatenate([mids, mids[2:3]], 0))
        states, cots = put_fine(corner_sib[64:96, :], corner_out[64:96, :], 4, mids4)
        f_at = below * (f_own + 16)
        c_at = below * (c_own + 16)
        a_at = below * (a_own + 8)
        m1x[pl.ds(f_at, 3), 0:16] = mids
        m1x[pl.ds(f_at, 3), 16:24] = jnp.where(is_top, states[1:4], states[0:3])
        cx[pl.ds(c_at, 2), 0:16] = band[304:336, :].reshape(2, 16, 256)
        cots = jnp.where(is_top, cots[2:4], cots[0:2])
        cx[pl.ds(c_at, 2), 16:32] = jnp.concatenate([cots, jnp.zeros_like(cots)], 1).astype(LOW)
        band_few = band[336:352, :].astype(WIDE)
        sib_few = corner_sib[96:112, :].astype(WIDE)[0:8]
        out_few = corner_out[96:112, :].astype(WIDE)[0:8]
        put_m2(a_at, band_few[8:16].reshape(1, 8, 256), sib_few[4:5], out_few[4:5], 1)
        own_k = band_few[0:8]
        halo_k = codes_of(own_k, sib_few, out_few)
        up_k = ups_of(own_k, sib_few, out_few)
        put_codes(
            f_at, a_at,
            jnp.where(is_top, own_k[5:8], own_k[0:3]),
            jnp.where(is_top, halo_k[5:8], halo_k[0:3]),
            up_k[3:4],
        )

    recv[...] = mm(m1x[...].reshape(frame * 24, 256).astype(LOW), weights[1]).reshape(frame, 24, 256) * 0.5
    weight = halved(weights[0])
    pool[...] = jnp.zeros_like(pool)

    def window_of(f, tile):
        return [gx[blk, pl.ds(2 * f, 8)].reshape(128, 256) for blk in BLOCKS[tile]]

    batch = 5 if odd_rows == 5 else 4

    def encode_rows(step, carry):
        spots = [(odd_row(step * batch + k), tile) for k in range(batch) for tile in range(3)]
        tiles = []
        for f, tile in spots:
            vec = ko[f] if tile < 2 else k2[f]
            tiles.append((masks[tile], vec, window_of(f, tile), recv[f, tile * 8 : tile * 8 + 8]))
        for (f, tile), (senders, mean, rise, total) in zip(spots, encode_tiles(tiles, weight)):
            row = f - f_own
            kept_at = jnp.where(row == 0, 0, jnp.where(row == 15, 1, 2))
            row = jnp.where(kept_at == 2, 16, row)
            pool[f, tile * 8 : tile * 8 + 8] = mean
            if tile < 2:
                sx[kept_at, tile] = senders
                slope[kept_at, tile] = rise
                ssum[row, tile * 8 : tile * 8 + 8] = total
        return carry

    lax.fori_loop(0, odd_rows // batch, encode_rows, 0)
    slots = iota((8, 256), 0)

    def encode_halo(step, carry):
        tiles = []
        for k in range(HALO_ROWS):
            f = f_own + 1 + HALO_ROWS * step + k
            tiles.append((masks[2], k2[f], window_of(f, 2), recv[f, 16:24]))
        done = encode_tiles(tiles, weight)
        for k in range(HALO_ROWS):
            r = 1 + HALO_ROWS * step + k
            f = f_own + r
            senders, mean, rise, total = done[k]
            pool[f, 16:24] = mean
            hx[r - 1] = senders
            hslope[r - 1] = rise
            for tile, slot in ((0, 0), (1, 7)):
                part = slice(tile * 8, tile * 8 + 8)
                pool[f, part] = jnp.where(slots == slot, mean, pool_in[r, part])
                ssum[r, part] = jnp.where(slots == slot, total, ssum_in[r, part])
        return carry

    lax.fori_loop(0, 14 // HALO_ROWS, encode_halo, 0)
    fine = m1x[...].reshape(frame * 24, 256) + mm(pool[...].reshape(frame * 24, 256).astype(LOW), weights[2])
    fine = fine.reshape(frame, 24, 256)
    fx[:, 0:16] = fine[:, 0:16].astype(LOW)
    fx[:, 16:32] = jnp.concatenate([fine[:, 16:24], jnp.zeros((frame, 8, 256), WIDE)], 1).astype(LOW)

    lanes = iota((128, 128), 1)
    up_mask = jnp.where(lanes == iota((128, 128), 0), 1.0, 0.0).astype(LOW).reshape(8, 16, 128)
    up_places = lanes.astype(WIDE).astype(CODE)
    one, zero = jnp.ones((128, 128), LOW), jnp.zeros((128, 128), LOW)
    m2_flat = m2x[...].reshape(a_frame * 16, 256)
    m2_low = m2_flat.astype(LOW)
    up_recv = mm(m2_low, weights[4]).reshape(a_frame, 16, 256) * 0.5
    picked = [(up_mask * uv[aa][None]).reshape(128, 128) for aa in range(a_frame)]
    found = mm(jnp.concatenate(picked, 0), jnp.ones((128, 128), LOW)).astype(CODE)
    senders = []
    for aa in range(a_frame):
        chosen = jnp.where(found[aa * 128 : aa * 128 + 128] == up_places, one, zero)
        ohu[aa] = chosen
        senders.append(mm(chosen, fx[2 * aa : 2 * aa + 4].reshape(128, 256)).astype(LOW))
        su[aa] = senders[aa]
    up_pre = mm(jnp.concatenate(senders, 0), halved(weights[3]))
    pools = []
    for aa in range(a_frame):
        act, rise = silu_of(up_pre[aa * 128 : aa * 128 + 128].reshape(8, 16, 256) + up_recv[aa][None])
        pools.append(jnp.sum(act, axis=0) * (1.0 / 8))
        uslope[aa] = rise.reshape(128, 256)
    cot_w = mm_nt(cx[...].reshape(cx.shape[0] * 32, 256), weights[8])
    up_pool = jnp.concatenate(pools, 0).astype(LOW)
    coarse = (m2_flat + mm(up_pool, weights[5])).astype(LOW)

    c_frame = 2 * a_frame
    nodes = a_frame * 16

    parents = mm(spread[...], coarse).astype(LOW)
    fine_mid = fx[1 : 1 + c_frame].reshape(c_frame * 32, 256)
    act, rise = silu_of((mm(parents, weights[6]) + mm(fine_mid, weights[7])) * 0.5)
    dd[0] = (cot_w * 0.5 * rise).astype(LOW).reshape(c_frame, 32, 256)
    dd[1] = act.astype(LOW).reshape(c_frame, 32, 256)

    def put_grad(index, value):
        put_halves(value, keep, send, index - 3, rep)

    act_own = dd[1, pl.ds(c_own, 16), 0:16].reshape(256, 256)
    delta_own = dd[0, pl.ds(c_own, 16), 0:16].reshape(256, 256)
    fine_own = fx[pl.ds(f_own, 16), 0:16].reshape(256, 256)
    cot_own = cot[...].reshape(256, 256)
    out = fine_own.astype(WIDE) + mm(act_own, weights[8])
    mesh_out[...] = out.astype(LOW).reshape(16, 16, 256)
    put_grad(8, mm_tn(act_own, cot_own))
    put_grad(7, mm_tn(fine_own, delta_own))

    child_sum = mm(gather[...], dd[0].reshape(c_frame * 32, 256))
    n_i = iota((nodes, 256), 0)
    aa_i, bb_i = n_i // 16, n_i % 16
    is_own = (aa_i >= a_own) & (aa_i < a_own + 8) & (bb_i < 8)
    is_real = (bb_i <= 8) | (bb_i == 15)
    if n_lat != 2:
        above = lat * 8 - 1 + aa_i
        is_real = is_real & (above >= 0) & (above < n_lat * 8)
    sum_high, sum_low = two_parts(child_sum)
    coarse_delta = (mm_nt(sum_high, weights[6]) + mm_nt(sum_low, weights[6])).astype(LOW)
    own_high, own_low = two_parts(jnp.where(is_own, child_sum, 0.0))
    put_grad(6, mm_tn(coarse, own_high) + mm_tn(coarse, own_low))
    own_delta = jnp.where(is_own, coarse_delta.astype(WIDE), 0.0).astype(LOW)
    put_grad(5, mm_tn(up_pool, own_delta))
    pool2 = jnp.where(is_real, mm_nt(coarse_delta, weights[5]) * (1.0 / 16), 0.0)
    own_f = jnp.where(is_own, 1.0, 0.0)
    node_sums, own_deltas, backs = [], [], []
    for aa in range(a_frame):
        d = pool2[aa * 16 : aa * 16 + 16][None] * uslope[aa].reshape(8, 16, 256)
        mine = own_f[aa * 16 : aa * 16 + 16][None]
        up_delta = d.astype(LOW)
        owned = up_delta.astype(WIDE) * mine
        node_sums.append(jnp.sum(owned, axis=0))
        own_deltas.append(owned.reshape(128, 256).astype(LOW))
        backs.append(mm_tn(ohu[aa], up_delta.reshape(128, 256)).reshape(4, 32, 256))
    for pair in range(a_frame + 1):
        parts = [backs[pair][0:2]] if pair < a_frame else []
        parts += [backs[pair - 1][2:4]] if pair else []
        recv[2 * pair : 2 * pair + 2] = sum(parts[1:], parts[0])[:, 0:24]
    put_grad(3, mm_tn(su[...].reshape(a_frame * 128, 256), jnp.concatenate(own_deltas, 0)))
    ns_high, ns_low = two_parts(jnp.concatenate(node_sums, 0))
    put_grad(4, mm_tn(m2_low, ns_high) + mm_tn(m2_low, ns_low))
    back_high, back_low = two_parts(recv[pl.ds(f_own, 16), 0:16].reshape(256, 256))
    fine_delta = (
        cot_own.astype(WIDE)
        + mm_nt(delta_own, weights[7])
        + mm_nt(back_high, weights[3])
        + mm_nt(back_low, weights[3])
    )
    fd_out[...] = fine_delta
    pool_out[...] = pool[pl.ds(f_own, 16), 0:16].reshape(256, 256).astype(LOW)


def back_kernel(
    m1, weights, fine_delta, pool, ssum, sx_in, slope_in, sx_edge, slope_edge, hx, hslope, mesh1_grad, keep, send, pd
):
    rep = lax.axis_index("rep")
    delta_b = fine_delta[...].astype(LOW)
    pool_delta = mm_nt(delta_b, weights[2]) * (1.0 / 32)
    pd[...] = pool_delta.reshape(16, 16, 256)
    node_delta = pool_delta * ssum[0:16].reshape(256, 256)
    high, low = two_parts(node_delta)
    m1_own = m1[...].reshape(256, 256)
    grad_in = fine_delta[...] + (mm_nt(high, weights[1]) + mm_nt(low, weights[1]))
    mesh1_grad[...] = grad_in.astype(LOW).reshape(16, 16, 256)
    put_halves(mm_tn(pool[...], delta_b), keep, send, 2, rep)
    put_halves(mm_tn(m1_own, high) + mm_tn(m1_own, low), keep, send, 1, rep)

    def deltas_of(r, tile, rise):
        d = pd[r, tile * 8 : tile * 8 + 8][None] * rise.reshape(16, 8, 256)
        return d.reshape(128, 256).astype(LOW)

    senders, deltas = [], []
    for i, r in enumerate((0, 15)):
        senders.append(sx_edge[i].reshape(256, 256))
        for tile in range(2):
            deltas.append(deltas_of(r, tile, slope_edge[i, tile].astype(WIDE)))
    slots = iota((128, 256), 0) % 8
    for r in range(1, 15):
        halo = hx[r - 1].astype(WIDE)
        halo_rise = hslope[r - 1].astype(WIDE)
        for tile, slot in ((0, 0), (1, 7)):
            ours = slots == slot
            senders.append(jnp.where(ours, halo, sx_in[r, tile].astype(WIDE)).astype(LOW))
            deltas.append(deltas_of(r, tile, jnp.where(ours, halo_rise, slope_in[r, tile].astype(WIDE))))
    put_halves(mm_tn(jnp.concatenate(senders, 0), jnp.concatenate(deltas, 0)), keep, send, 0, rep)


def block_place():
    return (lax.axis_index("lat") % 2) * 2 + lax.axis_index("lon") % 2


def quarters_kernel(kept_first, got_first, kept, got, own, *pieces):
    place = block_place()
    for step in range(4):
        rows = pl.ds(pl.multiple_of((place ^ step) * 32, 32), 32)
        for first, mine, other in ((0, kept_first, got_first), (3, kept, got)):
            total = mine[:, rows, :] + other[:, rows, :].astype(WIDE)
            at = slice(first, first + mine.shape[0])
            if step == 0:
                own[at] = total
            else:
                pieces[step - 1][at] = total.astype(LOW)


def add_kernel(*refs):
    total = refs[0][...].astype(WIDE)
    for ref in refs[1:-1]:
        total = total + ref[...].astype(WIDE)
    refs[-1][...] = total.astype(LOW)


def small_kernel(kernel, out_shape, name, *values):
    vmem = pl.BlockSpec(memory_space=pltpu.VMEM)
    return pl.pallas_call(
        kernel,
        out_shape=out_shape,
        in_specs=[vmem] * len(values),
        out_specs=jax.tree.map(lambda _: vmem, out_shape),
        compiler_params=pltpu.CompilerParams(vmem_limit_bytes=8 * 1024 * 1024),
        name=name,
    )(*values)


def spread_kernel(scale, own, *refs):
    pieces, (out, stage, sems) = refs[:4], refs[-3:]
    rep = lax.axis_index("rep")
    place = block_place()
    half = pl.multiple_of((rep if own else 1 - rep) * 128, 128)
    copies = []
    for k in range(9):
        for step in range(4):
            rows = pl.ds(pl.multiple_of((place ^ step) * 32, 32), 32)
            stage[k, rows, :] = pieces[step][k].astype(WIDE) * scale
        copies.append(pltpu.make_async_copy(stage.at[k], out.at[k, pl.ds(half, 128)], sems.at[k]))
        copies[-1].start()
    for copy in copies:
        copy.wait()


def flat_main(dirs, n_lat, *refs):
    n_bands = 3 * len(dirs)
    own, refs = refs[:10], refs[10:]
    sides, refs = refs[:2], refs[2:]
    bands, refs = refs[:n_bands], refs[n_bands:]
    weights, refs = refs[0], refs[1:]
    outs, scratch = refs[:10], refs[10:]
    main_kernel(dirs, n_lat, own, sides, bands, weights, outs, scratch)


class Reduction:
    def __init__(self, mesh):
        self.sizes = (mesh.shape["lon"], mesh.shape["lat"])

    def between(self, values, lon_bit, lat_bit):
        lat_size = self.sizes[1]
        return permute(
            values,
            ("lon", "lat"),
            lambda i: ((i // lat_size) ^ lon_bit) * lat_size + ((i % lat_size) ^ lat_bit),
            self.sizes,
        )

    def siblings(self, values):
        return permute(values, "rep", lambda i: i ^ 1, (2,))

    def quarters(self, *halves):
        _, rows, cols = halves[0].shape
        shape = (9, rows // 4, cols)
        shapes = [jax.ShapeDtypeStruct(shape, WIDE)] + [jax.ShapeDtypeStruct(shape, LOW)] * 3
        return small_kernel(quarters_kernel, shapes, "quarters", *halves)

    def block(self, quarters):
        own, *others = quarters
        got = [self.between(piece, step & 1, step >> 1) for step, piece in zip((1, 2, 3), others)]
        shape = jax.ShapeDtypeStruct(own.shape, LOW)
        return small_kernel(add_kernel, shape, "block_sum", own, *got)

    def total(self, total):
        shape = jax.ShapeDtypeStruct(total.shape, LOW)
        for which, size in enumerate(self.sizes):
            bit = 2
            while bit < size:
                other = self.between(total, *((bit, 0) if which == 0 else (0, bit)))
                total = small_kernel(add_kernel, shape, "pair_sum", total, other)
                bit *= 2
        return total

    def pieces(self, own):
        mine = [own] + [self.between(own, step & 1, step >> 1) for step in (1, 2, 3)]
        return mine + [self.siblings(piece) for piece in mine]


def body(mesh, grid_state, mesh1_state, mesh2_state, grid_edges, up_edges, weights, cotangent):
    n_lat, n_lon = mesh.shape["lat"], mesh.shape["lon"]
    glon = grid_state.shape[1] * 2 * n_lon
    m1lon = mesh1_state.shape[1] * 2 * n_lon
    dirs = (None,) if n_lat == 2 else (True, False)
    vmem = pl.BlockSpec(memory_space=pltpu.VMEM)
    params = pltpu.CompilerParams(vmem_limit_bytes=VMEM_BYTES)
    shapes = [48] + [SIDE_ROWS] * 2 + [BAND_ROWS, CORNER_ROWS, CORNER_ROWS] * len(dirs)
    hbm = pl.BlockSpec(memory_space=pltpu.HBM)
    states = (grid_state, mesh1_state, cotangent, mesh2_state)
    grid_state, mesh1_state, cotangent, mesh2_state, codes, *buffers = pl.pallas_call(
        functools.partial(pack_kernel, dirs, glon, m1lon),
        out_shape=[jax.ShapeDtypeStruct(state.shape, state.dtype) for state in states]
        + [jax.ShapeDtypeStruct((n, 256), LOW) for n in shapes],
        in_specs=[hbm] * 6,
        out_specs=[vmem] * (4 + len(shapes)),
        scratch_shapes=[
            pltpu.VMEM(grid_edges.shape, grid_edges.dtype),
            pltpu.VMEM(up_edges.shape, up_edges.dtype),
            pltpu.SemaphoreType.DMA((6,)),
        ],
        compiler_params=params,
        name="pack_halos",
    )(*(in_hbm(value) for value in (*states, grid_edges, up_edges)))
    frame = 20 if n_lat == 2 else 22
    a_frame = 9 if n_lat == 2 else 10
    c_frame = 2 * a_frame
    g_frame = 2 * frame + 6
    inner = pl.pallas_call(
        inner_kernel,
        out_shape=[
            jax.ShapeDtypeStruct((16, 2, 128, 256), LOW),
            jax.ShapeDtypeStruct((16, 2, 128, 256), LOW),
            jax.ShapeDtypeStruct((16, 16, 256), WIDE),
            jax.ShapeDtypeStruct((16, 16, 256), WIDE),
            jax.ShapeDtypeStruct(weights.shape, LOW),
            jax.ShapeDtypeStruct((3, 128, 256), LOW),
            jax.ShapeDtypeStruct((c_frame * 32, a_frame * 16), LOW),
            jax.ShapeDtypeStruct((a_frame * 16, c_frame * 32), LOW),
        ],
        in_specs=[vmem] * 3 + [hbm],
        out_specs=[vmem] * 8,
        scratch_shapes=[
            pltpu.VMEM((3, 34, 16, 256), LOW),
            pltpu.VMEM((16, 16, 256), LOW),
            pltpu.VMEM((16, 16, 256), WIDE),
            pltpu.SemaphoreType.DMA((2,)),
        ],
        compiler_params=params,
        cost_estimate=pl.CostEstimate(flops=1_000_000_000, bytes_accessed=1_000, transcendentals=0),
        name="inner_rows",
    )(grid_state, mesh1_state, codes, in_hbm(weights))
    sx_in, slope_in, pool_in, ssum_in, weights, *tables = inner
    own = (grid_state, mesh1_state, cotangent, mesh2_state, codes, pool_in, ssum_in, *tables)

    def beyond(lon, core):
        return ((lon + (1 if core else -1)) % n_lon, 1 - core)

    def send_to(values, other_lat, column):
        def partner(i):
            lon, rest = divmod(i, n_lat * 2)
            row, core = divmod(rest, 2)
            row = other_lat(row)
            if row is None:
                return None
            if column == "sibling":
                core = 1 - core
            elif column == "beyond":
                lon, core = beyond(lon, core)
            return (lon * n_lat + row) * 2 + core

        return permute(values, ("lon", "lat", "rep"), partner, (n_lon, n_lat, 2))

    def shift(sends_bottom):
        if sends_bottom is None:
            return lambda row: row ^ 1
        if sends_bottom:
            return lambda row: row + 1 if row + 1 < n_lat else None
        return lambda row: row - 1 if row else None

    got_sides = [send_to(buffers[0], lambda row: row, "sibling"), send_to(buffers[1], lambda row: row, "beyond")]
    got_bands = []
    for i, sends_bottom in enumerate(dirs):
        for k, column in enumerate(("same", "sibling", "beyond")):
            got_bands.append(send_to(buffers[2 + 3 * i + k], shift(sends_bottom), column))

    scratch = [
        pltpu.VMEM((3, g_frame, 16, 256), LOW),
        pltpu.VMEM((frame, 24, 256), WIDE),
        pltpu.VMEM((frame, 24, 256), WIDE),
        pltpu.VMEM((frame, 16, 256), LOW),
        pltpu.VMEM((frame, 16, 256), LOW),
        pltpu.VMEM((a_frame, 16, 128), LOW),
        pltpu.VMEM((frame, 24, 256), WIDE),
        pltpu.VMEM((frame, 32, 256), LOW),
        pltpu.VMEM((c_frame, 32, 256), LOW),
        pltpu.VMEM((a_frame, 16, 256), WIDE),
        pltpu.VMEM((a_frame, 128, 128), LOW),
        pltpu.VMEM((a_frame, 128, 256), LOW),
        pltpu.VMEM((a_frame, 128, 256), WIDE),
        pltpu.VMEM((2, c_frame, 32, 256), LOW),
    ]
    n_in = 10 + 2 + len(got_bands) + 1
    mesh_out, kept, sent, fine_delta, pool, ssum, sx_edge, slope_edge, hx, hslope = pl.pallas_call(
        functools.partial(flat_main, dirs, n_lat),
        out_shape=[
            jax.ShapeDtypeStruct(mesh1_state.shape, LOW),
            jax.ShapeDtypeStruct((6, 128, 256), WIDE),
            jax.ShapeDtypeStruct((6, 128, 256), LOW),
            jax.ShapeDtypeStruct((256, 256), WIDE),
            jax.ShapeDtypeStruct((256, 256), LOW),
            jax.ShapeDtypeStruct((17, 16, 256), WIDE),
            jax.ShapeDtypeStruct((3, 2, 128, 256), LOW),
            jax.ShapeDtypeStruct((3, 2, 128, 256), LOW),
            jax.ShapeDtypeStruct((14, 128, 256), LOW),
            jax.ShapeDtypeStruct((14, 128, 256), LOW),
        ],
        in_specs=[vmem] * n_in,
        out_specs=[vmem] * 10,
        scratch_shapes=scratch,
        compiler_params=params,
        name="sweep",
    )(*own, *got_sides, *got_bands, weights)
    reduction = Reduction(mesh)
    got = reduction.siblings(sent)
    mesh1_grad, kept_first, sent_first = pl.pallas_call(
        back_kernel,
        out_shape=[
            jax.ShapeDtypeStruct(mesh1_state.shape, LOW),
            jax.ShapeDtypeStruct((3, 128, 256), WIDE),
            jax.ShapeDtypeStruct((3, 128, 256), LOW),
        ],
        in_specs=[vmem] * 11,
        out_specs=[vmem] * 3,
        scratch_shapes=[pltpu.VMEM((16, 16, 256), WIDE)],
        compiler_params=params,
        cost_estimate=pl.CostEstimate(flops=3_000_000_000, bytes_accessed=8_000_000, transcendentals=0),
        name="encoder_back",
    )(mesh1_state, weights, fine_delta, pool, ssum, sx_in, slope_in, sx_edge, slope_edge, hx, hslope)
    node_total = mesh1_state.shape[0] * mesh1_state.shape[1] * n_lat * n_lon * 2
    scale = float(node_total) ** (-0.5)
    quarters = reduction.quarters(kept_first, reduction.siblings(sent_first), kept, got)
    pieces = reduction.pieces(reduction.total(reduction.block(quarters)))
    weight_grads = None
    for own in (True, False):
        before = [] if own else [weight_grads]
        weight_grads = pl.pallas_call(
            functools.partial(spread_kernel, scale, own),
            out_shape=jax.ShapeDtypeStruct((9, 256, 256), WIDE),
            in_specs=[vmem] * 4 + [hbm] * len(before),
            out_specs=hbm,
            scratch_shapes=[pltpu.VMEM((9, 128, 256), WIDE), pltpu.SemaphoreType.DMA((9,))],
            input_output_aliases={} if own else {4: 0},
            compiler_params=pltpu.CompilerParams(vmem_limit_bytes=8 * 1024 * 1024),
            name="spread_own" if own else "spread_other",
        )(*(pieces[:4] if own else pieces[4:]), *before)
    return (mesh_out, mesh1_grad, weight_grads)


def solution(mesh):
    in_specs = (
        P(("groups", "lat"), ("lon", "rep"), None),
        P(("groups", "lat"), ("lon", "rep"), None),
        P(("groups", "lat"), "lon", None),
        P(None, "lat", ("lon", "rep")),
        P(None, "lat", "lon"),
        P(),
        P(("groups", "lat"), ("lon", "rep"), None),
    )
    out_specs = (
        P(("groups", "lat"), ("lon", "rep"), None),
        P(("groups", "lat"), ("lon", "rep"), None),
        P("groups", None, None),
    )
    return jax.shard_map(
        functools.partial(body, mesh), mesh=mesh, in_specs=in_specs, out_specs=out_specs, check_vma=False
    )
```

```python
import functools

import jax
import jax.numpy as jnp
from jax import lax
from jax.experimental import pallas as pl
from jax.experimental.pallas import tpu as pltpu
from jax.sharding import PartitionSpec as P

LOW = jnp.bfloat16
WIDE = jnp.float32
VMEM_BYTES = 24 * 1024 * 1024
HALO_ROWS = 14
INNER_ROWS = 7
CODE = LOW

SIDE_ROWS = 416
BAND_ROWS = 352
CORNER_ROWS = 112


def permute(values, axes, partner, sizes):
    total = 1
    for size in sizes:
        total *= size
    pairs = [(i, partner(i)) for i in range(total)]
    return lax.ppermute(values, axes, [(i, j) for i, j in pairs if j is not None])


def mm(left, right):
    return jnp.dot(left, right, preferred_element_type=WIDE)


def mm_nt(left, right):
    return lax.dot_general(left, right, (((1,), (1,)), ((), ())), preferred_element_type=WIDE)


def mm_tn(left, right):
    return lax.dot_general(left, right, (((0,), (0,)), ((), ())), preferred_element_type=WIDE)


def two_parts(value):
    high = value.astype(LOW)
    return high, (value - high.astype(WIDE)).astype(LOW)


def silu_of(half):
    t = jnp.tanh(half)
    up = 1.0 + t
    act = half * up
    return act, up + act * (1.0 - t)


def halved(weight):
    return (weight.astype(WIDE) * 0.5).astype(LOW)


def iota(shape, dim):
    return lax.broadcasted_iota(jnp.int32, shape, dim)


def in_hbm(value):
    return pltpu.with_memory_space_constraint(value, pltpu.HBM)


def split(value, size):
    if size & (size - 1) == 0:
        return value >> (size.bit_length() - 1), value & (size - 1)
    return value // size, value % size


def wrapped(value, size):
    if size & (size - 1) == 0:
        return value & (size - 1)
    return jnp.mod(value, size)


def edge_codes(edges, glon, lat, col, rows, cols):
    row = iota(edges.shape, 0)
    lane = iota(edges.shape, 1)
    j = lane % 16
    at_row, at_col = split(edges, glon)
    down = at_row - (2 * (lat * rows + row) - 2)
    across = wrapped(at_col - (2 * (col * cols + j) - 2), glon)
    place = 2 * (j % 8) + 6 + across
    own = down * 16 + place + jnp.where(place >= 16, 112, 0)
    base = down * 16 + across + 6
    turned = jnp.where(j < 4, pltpu.roll(base, 256 - 12, 1), pltpu.roll(base, 4, 1))
    sent = turned + 2 * (j - 4) + jnp.where(j < 4, 0, 128)
    return own.astype(WIDE), sent.astype(WIDE)


def up_codes(edges, m1lon, lat, col, rep, rows, cols):
    row = iota(edges.shape, 0)
    l16 = iota(edges.shape, 1) % 16
    low = jnp.where(l16 < 8, edges, pltpu.roll(edges, 8, 1))
    high = jnp.where(l16 < 8, pltpu.roll(edges, 128 - 8, 1), edges)
    edges = jnp.where(rep == 0, low, high)
    b = l16 % 8
    at_row, at_col = split(edges, m1lon)
    down = at_row - (2 * (lat * rows + row) - 1)
    across = wrapped(at_col - (2 * (col * cols + b) - 1), m1lon)
    base = jnp.where(l16 < 8, b, jnp.where(b >= 4, b - 8, b + 8))
    at = 2 * base - 1 + across
    at = jnp.where(at < 0, at + 20, jnp.where(at >= 16, at + 4, at))
    return (down * 32 + at).astype(WIDE)


def pack_kernel(dirs, glon, m1lon, *refs):
    far, (grid, m1, cot, m2, codes), rest = refs[:6], refs[6:11], refs[11:]
    outs, (edges, ups, sems) = rest[:-3], rest[-3:]
    copies = [
        pltpu.make_async_copy(a, b, sems.at[i]) for i, (a, b) in enumerate(zip(far, (grid, m1, cot, m2, edges, ups)))
    ]
    for copy in copies[::-1]:
        copy.start()
    for copy in copies[4:]:
        copy.wait()
    rep = lax.axis_index("rep")
    lat = lax.axis_index("lat")
    col = lax.axis_index("lon") * 2 + rep
    sides = outs[:2]
    bands = outs[2:]
    flat = jnp.concatenate([edges[k] for k in range(16)], axis=1)
    own_k, sent_k = edge_codes(flat, glon, lat, col, 16, 16)
    flat = jnp.concatenate([ups[k] for k in range(8)], axis=1)
    up_k = up_codes(flat, m1lon, lat, col, rep, 8, 8)
    up_k = jnp.concatenate([up_k, jnp.zeros_like(up_k)], 1)
    codes[0:16, :] = own_k.astype(LOW)
    codes[16:32, :] = sent_k.astype(LOW)
    codes[32:48, :] = jnp.concatenate([up_k, jnp.zeros_like(up_k)], 0).astype(LOW)
    for copy in copies[:4]:
        copy.wait()
    m2w = m2[...].astype(WIDE)
    m2_half = jnp.where(rep == 0, m2w[:, 0:8], m2w[:, 8:16])
    row8 = iota((8, 256), 0)

    def few(k_rows, last, ghost):
        up = jnp.where(last, up_k[7:8], up_k[0:1])
        rest = jnp.where(row8 == 3, jnp.broadcast_to(up, (8, 256)), 0.0)
        if ghost is not None:
            rest = jnp.where(row8 == 4, jnp.broadcast_to(ghost, (8, 256)), rest)
        return jnp.where(last, jnp.where(row8 >= 5, k_rows[8:16], rest), jnp.where(row8 < 3, k_rows[0:8], rest))

    def last_rows(sends_bottom):
        if sends_bottom is None:
            return lat == 0
        return jnp.bool_(sends_bottom)

    def fill(targets, right):
        side, corners = targets
        g = grid[:, 16:32, :] if right else grid[:, 0:16, :]
        g = g.astype(WIDE)[:, 8:16] if right else g.astype(WIDE)[:, 0:8]
        part = slice(12, 16) if right else slice(0, 4)
        pair = jnp.concatenate([m1[...].astype(WIDE)[:, part], cot[...].astype(WIDE)[:, part]], axis=1)
        edge = 7 if right else 0
        ghosts = jnp.zeros((8, 256), WIDE)
        for a in range(8):
            ghosts = jnp.where(row8 == a, jnp.broadcast_to(m2_half[a, edge : edge + 1], (8, 256)), ghosts)
        side[0:256, :] = g.reshape(256, 256).astype(LOW)
        side[256:384, :] = pair.reshape(128, 256).astype(LOW)
        side[384:400, :] = sent_k.astype(LOW)
        side[400:416, :] = jnp.concatenate([up_k, ghosts], 0).astype(LOW)
        for sends_bottom, corner in corners:
            last = last_rows(sends_bottom)
            corner[0:64, :] = jnp.where(last, g[24:32], g[0:8]).reshape(64, 256).astype(LOW)
            corner[64:96, :] = jnp.where(last, pair[12:16], pair[0:4]).reshape(32, 256).astype(LOW)
            block = few(sent_k, last, jnp.where(last, ghosts[7:8], ghosts[0:1]))
            corner[96:112, :] = jnp.concatenate([block, block], 0).astype(LOW)

    sib = (sides[0], [(d, bands[3 * i + 1]) for i, d in enumerate(dirs)])
    out = (sides[1], [(d, bands[3 * i + 2]) for i, d in enumerate(dirs)])

    @pl.when(rep == 0)
    def _():
        fill(sib, True)
        fill(out, False)

    @pl.when(rep == 1)
    def _():
        fill(sib, False)
        fill(out, True)

    for i, sends_bottom in enumerate(dirs):
        band = bands[3 * i]
        last = last_rows(sends_bottom)
        first = jnp.where(last, 1, 0)
        band[0:256, :] = grid[pl.ds(first * 24, 8)].reshape(256, 256)
        band[256:304, :] = m1[pl.ds(first * 13, 3)].reshape(48, 256)
        band[304:336, :] = cot[pl.ds(first * 14, 2)].reshape(32, 256)
        mt = jnp.where(last, m2_half[7], m2_half[0])
        band[336:352, :] = jnp.concatenate([few(own_k, last, None), mt], 0).astype(LOW)


def set_masks(masks):
    edge = iota((128, 256), 0)
    lanes = iota((128, 256), 1)
    slot = edge % 8
    base = (edge // 8) * 16
    masks[0] = jnp.where(lanes == base + slot, 1.0, 0.0).astype(LOW)
    masks[1] = jnp.where(lanes == base + 8 + slot, 1.0, 0.0).astype(LOW)
    masks[2] = jnp.where(lanes == base + jnp.where(slot < 7, slot, 15), 1.0, 0.0).astype(LOW)


def encode_tiles(tiles, weight):
    ones = jnp.ones((256, 256), LOW)
    places = iota((128, 256), 1).astype(WIDE).astype(CODE)
    one, zero = jnp.ones((128, 256), LOW), jnp.zeros((128, 256), LOW)
    picked = [(mask.reshape(8, 16, 256) * codes[None]).reshape(128, 256) for mask, codes, _, _ in tiles]
    found = mm(jnp.concatenate(picked, 0), ones).astype(CODE)
    senders = []
    for i, (_, _, window, _) in enumerate(tiles):
        chosen = jnp.where(found[i * 128 : i * 128 + 128] == places, one, zero)
        senders.append(mm(chosen, jnp.concatenate(window, 0)).astype(LOW))
    pre_all = mm(jnp.concatenate(senders, 0), weight)
    results = []
    for i, (_, _, _, received) in enumerate(tiles):
        act, rise = silu_of(pre_all[i * 128 : i * 128 + 128].reshape(16, 8, 256) + received[None])
        results.append(
            (senders[i], jnp.sum(act, axis=0) * (1.0 / 16), rise.reshape(128, 256).astype(LOW), jnp.sum(rise, axis=0))
        )
    return results


BLOCKS = ((0, 1), (1, 2), (0, 2))


def inner_kernel(grid, m1, codes, far, sx, slope, pool, ssum, weights, masks, spread, gather, gx, ko, recv, sems):
    first = pltpu.make_async_copy(far.at[0:2], weights.at[0:2], sems.at[0])
    others = pltpu.make_async_copy(far.at[2:9], weights.at[2:9], sems.at[1])
    first.start()
    others.start()
    set_masks(masks)

    def place_grid(step, carry):
        r = step * 8
        wide = grid[pl.ds(r, 8)].astype(WIDE)
        edge = jnp.zeros((8, 8, 256), WIDE)
        gx[0, pl.ds(r, 8)] = jnp.concatenate([edge, wide[:, 0:8]], 1).astype(LOW)
        gx[1, pl.ds(r, 8)] = wide[:, 8:24].astype(LOW)
        gx[2, pl.ds(r, 8)] = jnp.concatenate([wide[:, 24:32], edge], 1).astype(LOW)
        return carry

    lax.fori_loop(0, 4, place_grid, 0)
    gx[:, 32:34] = jnp.zeros((3, 2, 16, 256), LOW)
    own = codes[0:16, :].astype(WIDE)
    for r in range(16):
        ko[r] = jnp.broadcast_to(own[r : r + 1], (16, 256)).astype(LOW)
    first.wait()
    recv[...] = mm(m1[...].reshape(256, 256), weights[1]).reshape(16, 16, 256) * 0.5
    weight = halved(weights[0])

    def rows(step, carry):
        spots = [(1 + INNER_ROWS * step + k, tile) for k in range(INNER_ROWS) for tile in range(2)]
        tiles = []
        for r, tile in spots:
            window = [gx[blk, pl.ds(2 * r - 2, 8)].reshape(128, 256) for blk in BLOCKS[tile]]
            tiles.append((masks[tile], ko[r], window, recv[r, tile * 8 : tile * 8 + 8]))
        for (r, tile), (senders, mean, rise, total) in zip(spots, encode_tiles(tiles, weight)):
            sx[r, tile] = senders
            slope[r, tile] = rise
            pool[r, tile * 8 : tile * 8 + 8] = mean
            ssum[r, tile * 8 : tile * 8 + 8] = total
        return carry

    def family(node, state):
        q = state % 32
        slot = jnp.where(q < 16, q // 2, jnp.where((q == 18) | (q == 19), 15, jnp.where((q == 20) | (q == 21), 8, -1)))
        return jnp.where((state // 64 == node // 16) & (slot == node % 16), 1.0, 0.0).astype(LOW)

    spread[...] = family(iota(spread.shape, 1), iota(spread.shape, 0))
    gather[...] = family(iota(gather.shape, 0), iota(gather.shape, 1))
    lax.fori_loop(0, 14 // INNER_ROWS, rows, 0)
    others.wait()


def put_halves(grad, keep, send, index, rep):
    first, second = grad[0:128], grad[128:256]
    keep[index] = jnp.where(rep == 0, first, second)
    send[index] = jnp.where(rep == 0, second, first).astype(LOW)


def main_kernel(
    dirs, n_lat, own, sides, bands, weights, outs, scratch
):
    grid, m1, cot, m2, codes, pool_in, ssum_in, masks, spread, gather = own
    mesh_out, keep, send, fd_out, pool_out, ssum, sx, slope, hx, hslope = outs
    gx, m1x, recv, ko, k2, uv, pool, fx, cx, m2x, ohu, su, uslope, dd = scratch
    rep = lax.axis_index("rep")
    lat = lax.axis_index("lat")
    frame = m1x.shape[0]
    a_frame = m2x.shape[0]
    if n_lat == 2:
        g_own, f_own, c_own, a_own = 4 + 4 * lat, 1 + 2 * lat, 2 * lat, lat
        odd_rows = 5
        odd_row = lambda i: jnp.where(lat == 0, jnp.where(i == 0, 1, 15 + i), jnp.where(i < 4, i, 18))
    else:
        g_own, f_own, c_own, a_own = 8, 3, 2, 1
        odd_rows = 8
        odd_row = lambda i: jnp.where(i < 4, i, 14 + i)

    def left_right(sib, out):
        return jnp.where(rep == 1, sib, out), jnp.where(rep == 1, out, sib)

    zero_rows = jnp.zeros((4, 16, 256), LOW)
    for blk in range(3):
        gx[blk, 0:4] = zero_rows
        gx[blk, gx.shape[1] - 6 : gx.shape[1] - 2] = zero_rows
        gx[blk, gx.shape[1] - 4 :] = zero_rows

    def put_grid(at, mid, sib, out):
        n = mid.shape[0]
        left, right = left_right(sib.astype(WIDE), out.astype(WIDE))
        left = left.reshape(n, 8, 256)
        right = right.reshape(n, 8, 256)
        wide = mid.astype(WIDE)
        gx[0, pl.ds(at, n)] = jnp.concatenate([left, wide[:, 0:8]], 1).astype(LOW)
        gx[1, pl.ds(at, n)] = wide[:, 8:24].astype(LOW)
        gx[2, pl.ds(at, n)] = jnp.concatenate([wide[:, 24:32], right], 1).astype(LOW)

    def own_grid(step, carry):
        r = step * 8
        r8 = step * 64
        put_grid(g_own + r, grid[pl.ds(r, 8)], sides[0][pl.ds(r8, 64), :], sides[1][pl.ds(r8, 64), :])
        return carry

    for step in range(4):
        own_grid(step, 0)

    def put_fine(sib, out, n, mid):
        left, right = left_right(sib.astype(WIDE), out.astype(WIDE))
        left = left.reshape(n, 8, 256)
        right = right.reshape(n, 8, 256)
        slot = iota((n, 8, 256), 1)
        states = jnp.concatenate([left[:, 0:4], right[:, 0:4]], 1)
        states = jnp.where(slot == 0, mid[:, 0:8], jnp.where(slot == 7, mid[:, 8:16], states))
        cots = jnp.concatenate([left[:, 4:8], right[:, 4:8]], 1)
        return states, cots

    m1x[...] = jnp.zeros_like(m1x)
    cx[...] = jnp.zeros_like(cx)
    m1_wide = m1[...].astype(WIDE)
    states, cots = put_fine(sides[0][256:384, :], sides[1][256:384, :], 16, m1_wide)
    m1x[pl.ds(f_own, 16), 0:16] = m1_wide
    m1x[pl.ds(f_own, 16), 16:24] = states
    cx[pl.ds(c_own, 16), 0:16] = cot[...]
    cx[pl.ds(c_own, 16), 16:32] = jnp.concatenate([cots, jnp.zeros_like(cots)], 1).astype(LOW)

    def put_m2(at, mid, sib, out, n):
        left, right = left_right(sib, out)
        slot = iota((8, 256), 0)
        for a in range(n):
            l_a = jnp.broadcast_to(left[a : a + 1], (8, 256))
            r_a = jnp.broadcast_to(right[a : a + 1], (8, 256))
            ghost = jnp.where(slot == 7, l_a, jnp.where(slot == 0, r_a, 0.0))
            m2x[at + a] = jnp.concatenate([mid[a], ghost], 0)

    m2w = m2[...].astype(WIDE)
    m2_half = jnp.where(rep == 0, m2w[:, 0:8], m2w[:, 8:16])
    side_few = [side[384:416, :].astype(WIDE) for side in sides]
    put_m2(a_own, m2_half, side_few[0][24:32], side_few[1][24:32], 8)

    def codes_of(mid, sib, out):
        left, right = left_right(sib, out)
        l16 = iota(mid.shape, 1) % 16
        return jnp.where((l16 == 0) | (l16 == 15), mid, jnp.where(l16 < 4, left, right))

    def ups_of(mid, sib, out):
        left, right = left_right(sib, out)
        l16 = iota(mid.shape, 1) % 16
        return jnp.where(l16 < 8, mid, jnp.where(l16 < 12, right, left))[:, 0:128]

    def put_codes(f_at, a_at, own_rows, halo_rows, up_rows):
        for r in range(own_rows.shape[0]):
            ko[f_at + r] = jnp.broadcast_to(own_rows[r : r + 1], (16, 256)).astype(LOW)
            k2[f_at + r] = jnp.broadcast_to(halo_rows[r : r + 1], (16, 256)).astype(LOW)
        for r in range(up_rows.shape[0]):
            uv[a_at + r] = jnp.broadcast_to(up_rows[r : r + 1], (16, 128)).astype(LOW)

    own_codes = codes[...].astype(WIDE)
    put_codes(
        f_own, a_own, own_codes[0:16],
        codes_of(own_codes[0:16], side_few[0][0:16], side_few[1][0:16]),
        ups_of(own_codes[32:40], side_few[0][16:24], side_few[1][16:24]),
    )
    for i, sends_bottom in enumerate(dirs):
        band, corner_sib, corner_out = bands[3 * i : 3 * i + 3]
        if sends_bottom is None:
            top = lat
        else:
            top = 1 if sends_bottom else 0
        below = 1 - top
        put_grid(
            below * (g_own + 32), band[0:256, :].reshape(8, 32, 256), corner_sib[0:64, :], corner_out[0:64, :]
        )
        is_top = top == 1
        mids = band[256:304, :].astype(WIDE).reshape(3, 16, 256)
        mids4 = jnp.where(is_top, jnp.concatenate([mids[0:1], mids], 0), jnp.concatenate([mids, mids[2:3]], 0))
        states, cots = put_fine(corner_sib[64:96, :], corner_out[64:96, :], 4, mids4)
        f_at = below * (f_own + 16)
        c_at = below * (c_own + 16)
        a_at = below * (a_own + 8)
        m1x[pl.ds(f_at, 3), 0:16] = mids
        m1x[pl.ds(f_at, 3), 16:24] = jnp.where(is_top, states[1:4], states[0:3])
        cx[pl.ds(c_at, 2), 0:16] = band[304:336, :].reshape(2, 16, 256)
        cots = jnp.where(is_top, cots[2:4], cots[0:2])
        cx[pl.ds(c_at, 2), 16:32] = jnp.concatenate([cots, jnp.zeros_like(cots)], 1).astype(LOW)
        band_few = band[336:352, :].astype(WIDE)
        sib_few = corner_sib[96:112, :].astype(WIDE)[0:8]
        out_few = corner_out[96:112, :].astype(WIDE)[0:8]
        put_m2(a_at, band_few[8:16].reshape(1, 8, 256), sib_few[4:5], out_few[4:5], 1)
        own_k = band_few[0:8]
        halo_k = codes_of(own_k, sib_few, out_few)
        up_k = ups_of(own_k, sib_few, out_few)
        put_codes(
            f_at, a_at,
            jnp.where(is_top, own_k[5:8], own_k[0:3]),
            jnp.where(is_top, halo_k[5:8], halo_k[0:3]),
            up_k[3:4],
        )

    recv[...] = mm(m1x[...].reshape(frame * 24, 256).astype(LOW), weights[1]).reshape(frame, 24, 256) * 0.5
    weight = halved(weights[0])
    pool[...] = jnp.zeros_like(pool)

    def window_of(f, tile):
        return [gx[blk, pl.ds(2 * f, 8)].reshape(128, 256) for blk in BLOCKS[tile]]

    batch = 5 if odd_rows == 5 else 4

    def encode_rows(step, carry):
        spots = [(odd_row(step * batch + k), tile) for k in range(batch) for tile in range(3)]
        tiles = []
        for f, tile in spots:
            vec = ko[f] if tile < 2 else k2[f]
            tiles.append((masks[tile], vec, window_of(f, tile), recv[f, tile * 8 : tile * 8 + 8]))
        for (f, tile), (senders, mean, rise, total) in zip(spots, encode_tiles(tiles, weight)):
            row = f - f_own
            kept_at = jnp.where(row == 0, 0, jnp.where(row == 15, 1, 2))
            row = jnp.where(kept_at == 2, 16, row)
            pool[f, tile * 8 : tile * 8 + 8] = mean
            if tile < 2:
                sx[kept_at, tile] = senders
                slope[kept_at, tile] = rise
                ssum[row, tile * 8 : tile * 8 + 8] = total
        return carry

    lax.fori_loop(0, odd_rows // batch, encode_rows, 0)
    slots = iota((8, 256), 0)

    def encode_halo(step, carry):
        tiles = []
        for k in range(HALO_ROWS):
            f = f_own + 1 + HALO_ROWS * step + k
            tiles.append((masks[2], k2[f], window_of(f, 2), recv[f, 16:24]))
        done = encode_tiles(tiles, weight)
        for k in range(HALO_ROWS):
            r = 1 + HALO_ROWS * step + k
            f = f_own + r
            senders, mean, rise, total = done[k]
            pool[f, 16:24] = mean
            hx[r - 1] = senders
            hslope[r - 1] = rise
            for tile, slot in ((0, 0), (1, 7)):
                part = slice(tile * 8, tile * 8 + 8)
                pool[f, part] = jnp.where(slots == slot, mean, pool_in[r, part])
                ssum[r, part] = jnp.where(slots == slot, total, ssum_in[r, part])
        return carry

    lax.fori_loop(0, 14 // HALO_ROWS, encode_halo, 0)
    fine = m1x[...].reshape(frame * 24, 256) + mm(pool[...].reshape(frame * 24, 256).astype(LOW), weights[2])
    fine = fine.reshape(frame, 24, 256)
    fx[:, 0:16] = fine[:, 0:16].astype(LOW)
    fx[:, 16:32] = jnp.concatenate([fine[:, 16:24], jnp.zeros((frame, 8, 256), WIDE)], 1).astype(LOW)

    lanes = iota((128, 128), 1)
    up_mask = jnp.where(lanes == iota((128, 128), 0), 1.0, 0.0).astype(LOW).reshape(8, 16, 128)
    up_places = lanes.astype(WIDE).astype(CODE)
    one, zero = jnp.ones((128, 128), LOW), jnp.zeros((128, 128), LOW)
    m2_flat = m2x[...].reshape(a_frame * 16, 256)
    m2_low = m2_flat.astype(LOW)
    up_recv = mm(m2_low, weights[4]).reshape(a_frame, 16, 256) * 0.5
    picked = [(up_mask * uv[aa][None]).reshape(128, 128) for aa in range(a_frame)]
    found = mm(jnp.concatenate(picked, 0), jnp.ones((128, 128), LOW)).astype(CODE)
    senders = []
    for aa in range(a_frame):
        chosen = jnp.where(found[aa * 128 : aa * 128 + 128] == up_places, one, zero)
        ohu[aa] = chosen
        senders.append(mm(chosen, fx[2 * aa : 2 * aa + 4].reshape(128, 256)).astype(LOW))
        su[aa] = senders[aa]
    up_pre = mm(jnp.concatenate(senders, 0), halved(weights[3]))
    pools = []
    for aa in range(a_frame):
        act, rise = silu_of(up_pre[aa * 128 : aa * 128 + 128].reshape(8, 16, 256) + up_recv[aa][None])
        pools.append(jnp.sum(act, axis=0) * (1.0 / 8))
        uslope[aa] = rise.reshape(128, 256)
    cot_w = mm_nt(cx[...].reshape(cx.shape[0] * 32, 256), weights[8])
    up_pool = jnp.concatenate(pools, 0).astype(LOW)
    coarse = (m2_flat + mm(up_pool, weights[5])).astype(LOW)

    c_frame = 2 * a_frame
    nodes = a_frame * 16

    parents = mm(spread[...], coarse).astype(LOW)
    fine_mid = fx[1 : 1 + c_frame].reshape(c_frame * 32, 256)
    act, rise = silu_of((mm(parents, weights[6]) + mm(fine_mid, weights[7])) * 0.5)
    dd[0] = (cot_w * 0.5 * rise).astype(LOW).reshape(c_frame, 32, 256)
    dd[1] = act.astype(LOW).reshape(c_frame, 32, 256)

    def put_grad(index, value):
        put_halves(value, keep, send, index - 3, rep)

    act_own = dd[1, pl.ds(c_own, 16), 0:16].reshape(256, 256)
    delta_own = dd[0, pl.ds(c_own, 16), 0:16].reshape(256, 256)
    fine_own = fx[pl.ds(f_own, 16), 0:16].reshape(256, 256)
    cot_own = cot[...].reshape(256, 256)
    out = fine_own.astype(WIDE) + mm(act_own, weights[8])
    mesh_out[...] = out.astype(LOW).reshape(16, 16, 256)
    put_grad(8, mm_tn(act_own, cot_own))
    put_grad(7, mm_tn(fine_own, delta_own))

    child_sum = mm(gather[...], dd[0].reshape(c_frame * 32, 256))
    n_i = iota((nodes, 256), 0)
    aa_i, bb_i = n_i // 16, n_i % 16
    is_own = (aa_i >= a_own) & (aa_i < a_own + 8) & (bb_i < 8)
    is_real = (bb_i <= 8) | (bb_i == 15)
    if n_lat != 2:
        above = lat * 8 - 1 + aa_i
        is_real = is_real & (above >= 0) & (above < n_lat * 8)
    sum_high, sum_low = two_parts(child_sum)
    coarse_delta = (mm_nt(sum_high, weights[6]) + mm_nt(sum_low, weights[6])).astype(LOW)
    own_high, own_low = two_parts(jnp.where(is_own, child_sum, 0.0))
    put_grad(6, mm_tn(coarse, own_high) + mm_tn(coarse, own_low))
    own_delta = jnp.where(is_own, coarse_delta.astype(WIDE), 0.0).astype(LOW)
    put_grad(5, mm_tn(up_pool, own_delta))
    pool2 = jnp.where(is_real, mm_nt(coarse_delta, weights[5]) * (1.0 / 16), 0.0)
    own_f = jnp.where(is_own, 1.0, 0.0)
    node_sums, own_deltas, backs = [], [], []
    for aa in range(a_frame):
        d = pool2[aa * 16 : aa * 16 + 16][None] * uslope[aa].reshape(8, 16, 256)
        mine = own_f[aa * 16 : aa * 16 + 16][None]
        up_delta = d.astype(LOW)
        owned = up_delta.astype(WIDE) * mine
        node_sums.append(jnp.sum(owned, axis=0))
        own_deltas.append(owned.reshape(128, 256).astype(LOW))
        backs.append(mm_tn(ohu[aa], up_delta.reshape(128, 256)).reshape(4, 32, 256))
    for pair in range(a_frame + 1):
        parts = [backs[pair][0:2]] if pair < a_frame else []
        parts += [backs[pair - 1][2:4]] if pair else []
        recv[2 * pair : 2 * pair + 2] = sum(parts[1:], parts[0])[:, 0:24]
    put_grad(3, mm_tn(su[...].reshape(a_frame * 128, 256), jnp.concatenate(own_deltas, 0)))
    ns_high, ns_low = two_parts(jnp.concatenate(node_sums, 0))
    put_grad(4, mm_tn(m2_low, ns_high) + mm_tn(m2_low, ns_low))
    back_high, back_low = two_parts(recv[pl.ds(f_own, 16), 0:16].reshape(256, 256))
    fine_delta = (
        cot_own.astype(WIDE)
        + mm_nt(delta_own, weights[7])
        + mm_nt(back_high, weights[3])
        + mm_nt(back_low, weights[3])
    )
    fd_out[...] = fine_delta
    pool_out[...] = pool[pl.ds(f_own, 16), 0:16].reshape(256, 256).astype(LOW)


def back_kernel(
    m1, weights, fine_delta, pool, ssum, sx_in, slope_in, sx_edge, slope_edge, hx, hslope, mesh1_grad, keep, send, pd
):
    rep = lax.axis_index("rep")
    delta_b = fine_delta[...].astype(LOW)
    pool_delta = mm_nt(delta_b, weights[2]) * (1.0 / 32)
    pd[...] = pool_delta.reshape(16, 16, 256)
    node_delta = pool_delta * ssum[0:16].reshape(256, 256)
    high, low = two_parts(node_delta)
    m1_own = m1[...].reshape(256, 256)
    grad_in = fine_delta[...] + (mm_nt(high, weights[1]) + mm_nt(low, weights[1]))
    mesh1_grad[...] = grad_in.astype(LOW).reshape(16, 16, 256)
    put_halves(mm_tn(pool[...], delta_b), keep, send, 2, rep)
    put_halves(mm_tn(m1_own, high) + mm_tn(m1_own, low), keep, send, 1, rep)

    def deltas_of(r, tile, rise):
        d = pd[r, tile * 8 : tile * 8 + 8][None] * rise.reshape(16, 8, 256)
        return d.reshape(128, 256).astype(LOW)

    senders, deltas = [], []
    for i, r in enumerate((0, 15)):
        senders.append(sx_edge[i].reshape(256, 256))
        for tile in range(2):
            deltas.append(deltas_of(r, tile, slope_edge[i, tile].astype(WIDE)))
    slots = iota((128, 256), 0) % 8
    for r in range(1, 15):
        halo = hx[r - 1].astype(WIDE)
        halo_rise = hslope[r - 1].astype(WIDE)
        for tile, slot in ((0, 0), (1, 7)):
            ours = slots == slot
            senders.append(jnp.where(ours, halo, sx_in[r, tile].astype(WIDE)).astype(LOW))
            deltas.append(deltas_of(r, tile, jnp.where(ours, halo_rise, slope_in[r, tile].astype(WIDE))))
    put_halves(mm_tn(jnp.concatenate(senders, 0), jnp.concatenate(deltas, 0)), keep, send, 0, rep)


def block_place():
    return (lax.axis_index("lat") % 2) * 2 + lax.axis_index("lon") % 2


def quarters_kernel(kept_first, got_first, kept, got, own, *pieces):
    place = block_place()
    for step in range(4):
        rows = pl.ds(pl.multiple_of((place ^ step) * 32, 32), 32)
        for first, mine, other in ((0, kept_first, got_first), (3, kept, got)):
            total = mine[:, rows, :] + other[:, rows, :].astype(WIDE)
            at = slice(first, first + mine.shape[0])
            if step == 0:
                own[at] = total
            else:
                pieces[step - 1][at] = total.astype(LOW)


def add_kernel(*refs):
    total = refs[0][...].astype(WIDE)
    for ref in refs[1:-1]:
        total = total + ref[...].astype(WIDE)
    refs[-1][...] = total.astype(LOW)


def small_kernel(kernel, out_shape, name, *values):
    vmem = pl.BlockSpec(memory_space=pltpu.VMEM)
    return pl.pallas_call(
        kernel,
        out_shape=out_shape,
        in_specs=[vmem] * len(values),
        out_specs=jax.tree.map(lambda _: vmem, out_shape),
        compiler_params=pltpu.CompilerParams(vmem_limit_bytes=8 * 1024 * 1024),
        name=name,
    )(*values)


def spread_kernel(scale, own, *refs):
    pieces, (out, stage, sems) = refs[:4], refs[-3:]
    rep = lax.axis_index("rep")
    place = block_place()
    half = pl.multiple_of((rep if own else 1 - rep) * 128, 128)
    copies = []
    for k in range(9):
        for step in range(4):
            rows = pl.ds(pl.multiple_of((place ^ step) * 32, 32), 32)
            stage[k, rows, :] = pieces[step][k].astype(WIDE) * scale
        copies.append(pltpu.make_async_copy(stage.at[k], out.at[k, pl.ds(half, 128)], sems.at[k]))
        copies[-1].start()
    for copy in copies:
        copy.wait()


def flat_main(dirs, n_lat, *refs):
    n_bands = 3 * len(dirs)
    own, refs = refs[:10], refs[10:]
    sides, refs = refs[:2], refs[2:]
    bands, refs = refs[:n_bands], refs[n_bands:]
    weights, refs = refs[0], refs[1:]
    outs, scratch = refs[:10], refs[10:]
    main_kernel(dirs, n_lat, own, sides, bands, weights, outs, scratch)


class Reduction:
    def __init__(self, mesh):
        self.sizes = (mesh.shape["lon"], mesh.shape["lat"])

    def between(self, values, lon_bit, lat_bit):
        lat_size = self.sizes[1]
        return permute(
            values,
            ("lon", "lat"),
            lambda i: ((i // lat_size) ^ lon_bit) * lat_size + ((i % lat_size) ^ lat_bit),
            self.sizes,
        )

    def siblings(self, values):
        return permute(values, "rep", lambda i: i ^ 1, (2,))

    def quarters(self, *halves):
        _, rows, cols = halves[0].shape
        shape = (9, rows // 4, cols)
        shapes = [jax.ShapeDtypeStruct(shape, WIDE)] + [jax.ShapeDtypeStruct(shape, LOW)] * 3
        return small_kernel(quarters_kernel, shapes, "quarters", *halves)

    def block(self, quarters):
        own, *others = quarters
        got = [self.between(piece, step & 1, step >> 1) for step, piece in zip((1, 2, 3), others)]
        shape = jax.ShapeDtypeStruct(own.shape, LOW)
        return small_kernel(add_kernel, shape, "block_sum", own, *got)

    def total(self, total):
        shape = jax.ShapeDtypeStruct(total.shape, LOW)
        for which, size in enumerate(self.sizes):
            bit = 2
            while bit < size:
                other = self.between(total, *((bit, 0) if which == 0 else (0, bit)))
                total = small_kernel(add_kernel, shape, "pair_sum", total, other)
                bit *= 2
        return total

    def pieces(self, own):
        mine = [own] + [self.between(own, step & 1, step >> 1) for step in (1, 2, 3)]
        return mine + [self.siblings(piece) for piece in mine]


def body(mesh, grid_state, mesh1_state, mesh2_state, grid_edges, up_edges, weights, cotangent):
    n_lat, n_lon = mesh.shape["lat"], mesh.shape["lon"]
    glon = grid_state.shape[1] * 2 * n_lon
    m1lon = mesh1_state.shape[1] * 2 * n_lon
    dirs = (None,) if n_lat == 2 else (True, False)
    vmem = pl.BlockSpec(memory_space=pltpu.VMEM)
    params = pltpu.CompilerParams(vmem_limit_bytes=VMEM_BYTES)
    shapes = [48] + [SIDE_ROWS] * 2 + [BAND_ROWS, CORNER_ROWS, CORNER_ROWS] * len(dirs)
    hbm = pl.BlockSpec(memory_space=pltpu.HBM)
    states = (grid_state, mesh1_state, cotangent, mesh2_state)
    grid_state, mesh1_state, cotangent, mesh2_state, codes, *buffers = pl.pallas_call(
        functools.partial(pack_kernel, dirs, glon, m1lon),
        out_shape=[jax.ShapeDtypeStruct(state.shape, state.dtype) for state in states]
        + [jax.ShapeDtypeStruct((n, 256), LOW) for n in shapes],
        in_specs=[hbm] * 6,
        out_specs=[vmem] * (4 + len(shapes)),
        scratch_shapes=[
            pltpu.VMEM(grid_edges.shape, grid_edges.dtype),
            pltpu.VMEM(up_edges.shape, up_edges.dtype),
            pltpu.SemaphoreType.DMA((6,)),
        ],
        compiler_params=params,
        name="pack_halos",
    )(*(in_hbm(value) for value in (*states, grid_edges, up_edges)))
    frame = 20 if n_lat == 2 else 22
    a_frame = 9 if n_lat == 2 else 10
    c_frame = 2 * a_frame
    g_frame = 2 * frame + 6
    inner = pl.pallas_call(
        inner_kernel,
        out_shape=[
            jax.ShapeDtypeStruct((16, 2, 128, 256), LOW),
            jax.ShapeDtypeStruct((16, 2, 128, 256), LOW),
            jax.ShapeDtypeStruct((16, 16, 256), WIDE),
            jax.ShapeDtypeStruct((16, 16, 256), WIDE),
            jax.ShapeDtypeStruct(weights.shape, LOW),
            jax.ShapeDtypeStruct((3, 128, 256), LOW),
            jax.ShapeDtypeStruct((c_frame * 32, a_frame * 16), LOW),
            jax.ShapeDtypeStruct((a_frame * 16, c_frame * 32), LOW),
        ],
        in_specs=[vmem] * 3 + [hbm],
        out_specs=[vmem] * 8,
        scratch_shapes=[
            pltpu.VMEM((3, 34, 16, 256), LOW),
            pltpu.VMEM((16, 16, 256), LOW),
            pltpu.VMEM((16, 16, 256), WIDE),
            pltpu.SemaphoreType.DMA((2,)),
        ],
        compiler_params=params,
        cost_estimate=pl.CostEstimate(flops=1_000_000_000, bytes_accessed=1_000, transcendentals=0),
        name="inner_rows",
    )(grid_state, mesh1_state, codes, in_hbm(weights))
    sx_in, slope_in, pool_in, ssum_in, weights, *tables = inner
    own = (grid_state, mesh1_state, cotangent, mesh2_state, codes, pool_in, ssum_in, *tables)

    def beyond(lon, core):
        return ((lon + (1 if core else -1)) % n_lon, 1 - core)

    def send_to(values, other_lat, column):
        def partner(i):
            lon, rest = divmod(i, n_lat * 2)
            row, core = divmod(rest, 2)
            row = other_lat(row)
            if row is None:
                return None
            if column == "sibling":
                core = 1 - core
            elif column == "beyond":
                lon, core = beyond(lon, core)
            return (lon * n_lat + row) * 2 + core

        return permute(values, ("lon", "lat", "rep"), partner, (n_lon, n_lat, 2))

    def shift(sends_bottom):
        if sends_bottom is None:
            return lambda row: row ^ 1
        if sends_bottom:
            return lambda row: row + 1 if row + 1 < n_lat else None
        return lambda row: row - 1 if row else None

    got_sides = [send_to(buffers[0], lambda row: row, "sibling"), send_to(buffers[1], lambda row: row, "beyond")]
    got_bands = []
    for i, sends_bottom in enumerate(dirs):
        for k, column in enumerate(("same", "sibling", "beyond")):
            got_bands.append(send_to(buffers[2 + 3 * i + k], shift(sends_bottom), column))

    scratch = [
        pltpu.VMEM((3, g_frame, 16, 256), LOW),
        pltpu.VMEM((frame, 24, 256), WIDE),
        pltpu.VMEM((frame, 24, 256), WIDE),
        pltpu.VMEM((frame, 16, 256), LOW),
        pltpu.VMEM((frame, 16, 256), LOW),
        pltpu.VMEM((a_frame, 16, 128), LOW),
        pltpu.VMEM((frame, 24, 256), WIDE),
        pltpu.VMEM((frame, 32, 256), LOW),
        pltpu.VMEM((c_frame, 32, 256), LOW),
        pltpu.VMEM((a_frame, 16, 256), WIDE),
        pltpu.VMEM((a_frame, 128, 128), LOW),
        pltpu.VMEM((a_frame, 128, 256), LOW),
        pltpu.VMEM((a_frame, 128, 256), WIDE),
        pltpu.VMEM((2, c_frame, 32, 256), LOW),
    ]
    n_in = 10 + 2 + len(got_bands) + 1
    mesh_out, kept, sent, fine_delta, pool, ssum, sx_edge, slope_edge, hx, hslope = pl.pallas_call(
        functools.partial(flat_main, dirs, n_lat),
        out_shape=[
            jax.ShapeDtypeStruct(mesh1_state.shape, LOW),
            jax.ShapeDtypeStruct((6, 128, 256), WIDE),
            jax.ShapeDtypeStruct((6, 128, 256), LOW),
            jax.ShapeDtypeStruct((256, 256), WIDE),
            jax.ShapeDtypeStruct((256, 256), LOW),
            jax.ShapeDtypeStruct((17, 16, 256), WIDE),
            jax.ShapeDtypeStruct((3, 2, 128, 256), LOW),
            jax.ShapeDtypeStruct((3, 2, 128, 256), LOW),
            jax.ShapeDtypeStruct((14, 128, 256), LOW),
            jax.ShapeDtypeStruct((14, 128, 256), LOW),
        ],
        in_specs=[vmem] * n_in,
        out_specs=[vmem] * 10,
        scratch_shapes=scratch,
        compiler_params=params,
        name="sweep",
    )(*own, *got_sides, *got_bands, weights)
    reduction = Reduction(mesh)
    got = reduction.siblings(sent)
    mesh1_grad, kept_first, sent_first = pl.pallas_call(
        back_kernel,
        out_shape=[
            jax.ShapeDtypeStruct(mesh1_state.shape, LOW),
            jax.ShapeDtypeStruct((3, 128, 256), WIDE),
            jax.ShapeDtypeStruct((3, 128, 256), LOW),
        ],
        in_specs=[vmem] * 11,
        out_specs=[vmem] * 3,
        scratch_shapes=[pltpu.VMEM((16, 16, 256), WIDE)],
        compiler_params=params,
        cost_estimate=pl.CostEstimate(flops=3_000_000_000, bytes_accessed=8_000_000, transcendentals=0),
        name="encoder_back",
    )(mesh1_state, weights, fine_delta, pool, ssum, sx_in, slope_in, sx_edge, slope_edge, hx, hslope)
    node_total = mesh1_state.shape[0] * mesh1_state.shape[1] * n_lat * n_lon * 2
    scale = float(node_total) ** (-0.5)
    quarters = reduction.quarters(kept_first, reduction.siblings(sent_first), kept, got)
    pieces = reduction.pieces(reduction.total(reduction.block(quarters)))
    weight_grads = None
    for own in (True, False):
        before = [] if own else [weight_grads]
        weight_grads = pl.pallas_call(
            functools.partial(spread_kernel, scale, own),
            out_shape=jax.ShapeDtypeStruct((9, 256, 256), WIDE),
            in_specs=[vmem] * 4 + [hbm] * len(before),
            out_specs=hbm,
            scratch_shapes=[pltpu.VMEM((9, 128, 256), WIDE), pltpu.SemaphoreType.DMA((9,))],
            input_output_aliases={} if own else {4: 0},
            compiler_params=pltpu.CompilerParams(vmem_limit_bytes=8 * 1024 * 1024),
            name="spread_own" if own else "spread_other",
        )(*(pieces[:4] if own else pieces[4:]), *before)
    return (mesh_out, mesh1_grad, weight_grads)


def solution(mesh):
    in_specs = (
        P(("groups", "lat"), ("lon", "rep"), None),
        P(("groups", "lat"), ("lon", "rep"), None),
        P(("groups", "lat"), "lon", None),
        P(None, "lat", ("lon", "rep")),
        P(None, "lat", "lon"),
        P(),
        P(("groups", "lat"), ("lon", "rep"), None),
    )
    out_specs = (
        P(("groups", "lat"), ("lon", "rep"), None),
        P(("groups", "lat"), ("lon", "rep"), None),
        P("groups", None, None),
    )
    return jax.shard_map(
        functools.partial(body, mesh), mesh=mesh, in_specs=in_specs, out_specs=out_specs, check_vma=False
    )
```
